256 devices in a mesh: tiles: 256 (over z, x, y, core).
Axes of the slice: x: 4, y: 4, z: 8, core: 2. Of those that a mesh axis runs over, the one named last changes fastest.
Arguments:
- features: bfloat16 [256, 64, 4096], P('tiles'), may hold values from -6 to 6
- weights_first: bfloat16 [9, 64, 64], replicated, may hold values from -0.25 to 0.25
- weights_second: bfloat16 [9, 64, 64], replicated, may hold values from -0.25 to 0.25
- cotangent: bfloat16 [256, 32, 2048], P('tiles'), may hold values from -6 to 6
- neighbours: int32 [256, 8], P('tiles'), may hold values from 0 to 255, as said below
- turns: int32 [256, 8], P('tiles'), may hold values from 0 to 3
- corners: int32 [256, 4], P('tiles'), may hold values 0 or 1
Outputs:
- pooled: bfloat16 [256, 32, 2048], P('tiles')
- grad_features: bfloat16 [256, 64, 4096], P('tiles')
- grad_first: float32 [9, 64, 64], replicated
- grad_second: float32 [9, 64, 64], replicated
The draws below stay inside these ranges and needn't reach their ends.
Inputs may be any that keep to these rules, and one draw needn't show every extreme that they name: With 1 tiles a device in order, the owner of neighbours[t, j] lies within 3 devices of the owner of t around the cycle of devices, and both 3 devices ahead and behind occur.
All inputs are finite; a program needn't handle non-finite values. No bound on the sum of `corners` on one device may be relied on, other than what follows from the above.
Results may differ from the reference program's by a relative error of at most 0.006.
Values may be sent and summed in bfloat16 or wider, within the bound.
A program may use at most 128 MiB of HBM per device.

```python
import jax
import jax.numpy as jnp
from jax import lax

P_SIZE = 64
C = 64
TILE_DEV = 1
REACH = 3
TILES = 256


def draw_neighbours(key, part):
    key = jax.random.fold_in(key, 11)
    first, second = jax.random.split(key)
    devices = TILES // TILE_DEV
    offsets = jax.random.randint(first, (TILES, 8), -REACH, REACH + 1)
    local = jax.random.randint(second, (TILES, 8), 0, TILE_DEV)
    owner = jnp.arange(TILES, dtype=jnp.int32) // TILE_DEV
    target = (owner[:, None] + offsets) % devices * TILE_DEV + local
    target = target.at[0, 6].set(TILES - 1)
    target = target.at[TILES - 1, 2].set(0)
    target = target.at[0, 0].set(REACH * TILE_DEV)
    target = target.at[0, 4].set((devices - REACH) * TILE_DEV)
    return target.astype(jnp.int32)


def with_ends(array, own_key, least, top_value):
    dims = array.shape
    spot = [jax.random.randint(jax.random.fold_in(own_key, axis), (), 0, dims[axis]) for axis in range(len(dims))]
    array = array.at[tuple(spot)].set(least)
    longest = dims.index(max(dims))
    spot[longest] = (spot[longest] + 1) % dims[longest]
    return array.at[tuple(spot)].set(top_value)


def steps_of(rng, shape, cuts, least, largest):
    level, own = 1.0, jax.random.fold_in(rng, 6)
    for dim, blocks in cuts:
        draws = jnp.exp(jax.random.uniform(jax.random.fold_in(own, dim), (blocks,), jnp.float32, least / len(cuts), largest / len(cuts)))
        level = level * jnp.repeat(draws, shape[dim] // blocks).reshape([-1 if axis == dim else 1 for axis in range(len(shape))])
    return level


def bell_draw(rng, shape, scale, reach, shards=(), held_as=jnp.bfloat16):
    drawn = scale * jax.random.normal(rng, shape, jnp.float32)
    if shards:
        drawn = drawn * steps_of(rng, shape, shards, -0.22, 0.18)
    return jnp.clip(drawn, -reach, reach).astype(held_as)


def setup_inputs(seed: int = 0) -> dict:
    splits = jax.random.split(jax.random.key(seed), 8)
    features = bell_draw(splits[0], (TILES, P_SIZE, P_SIZE * C), 1.0, 6.0, ((0, 256),))
    weights_first = bell_draw(splits[1], (9, C, C), (9 * C) ** -0.5, 0.25)
    weights_second = bell_draw(splits[2], (9, C, C), (9 * C) ** -0.5, 0.25)
    cotangent = bell_draw(splits[3], (TILES, P_SIZE // 2, P_SIZE // 2 * C), 1.0, 6.0, ((0, 256),))
    neighbours = draw_neighbours(jax.random.fold_in(splits[7], 71), 0)
    turns = with_ends(jax.random.randint(splits[5], (TILES, 8), 0, 4), jax.random.fold_in(splits[5], 1), 0, 3).astype(jnp.int32)
    corners = with_ends((jax.random.randint(splits[6], (TILES, 4), 0, 4) < 3).astype(jnp.int32), jax.random.fold_in(splits[6], 1), 0, 1)
    return {"features": features, "weights_first": weights_first, "weights_second": weights_second, "cotangent": cotangent, "neighbours": neighbours, "turns": turns, "corners": corners}


DIRS = ((-1, 0), (-1, 1), (0, 1), (1, 1), (1, 0), (1, -1), (0, -1), (-1, -1))


def turn(tile, count):
    result = tile
    for step in (1, 2, 3):
        result = jnp.where(count == step, jnp.rot90(tile, step, axes=(0, 1)), result)
    return result


def spans(step, width, tile_side):
    if step < 0:
        return slice(0, width), slice(tile_side - width, tile_side)
    if step == 0:
        return slice(width, width + tile_side), slice(0, tile_side)
    return slice(width + tile_side, tile_side + 2 * width), slice(0, width)


def extend(owned_tile, nbrs, turn_row, corner_row, width):
    tile_side = owned_tile.shape[0]
    extended_tile = jnp.pad(owned_tile, ((width, width), (width, width), (0, 0)))
    for j, (dy, dx) in enumerate(DIRS):
        ext_rows, src_rows = spans(dy, width, tile_side)
        ext_cols, src_cols = spans(dx, width, tile_side)
        block = turn(nbrs[j], turn_row[j])[src_rows, src_cols]
        if dy != 0 and dx != 0:
            block = block * corner_row[j // 2].astype(block.dtype)
        extended_tile = extended_tile.at[ext_rows, ext_cols].set(block)
    return extended_tile


def spill(grad_ext, turn_row, corner_row, width):
    tile_side = grad_ext.shape[0] - 2 * width
    outputs = []
    for j, (dy, dx) in enumerate(DIRS):
        ext_rows, src_rows = spans(dy, width, tile_side)
        ext_cols, src_cols = spans(dx, width, tile_side)
        block = grad_ext[ext_rows, ext_cols]
        if dy != 0 and dx != 0:
            block = block * corner_row[j // 2].astype(block.dtype)
        framed = jnp.zeros((tile_side, tile_side, grad_ext.shape[2]), grad_ext.dtype).at[src_rows, src_cols].set(block)
        outputs.append(turn(framed, (4 - turn_row[j]) % 4))
    return jnp.stack(outputs)


def tile_convolve(extended_tile, kernel_weights, dilation_factor):
    tile_side = extended_tile.shape[0] - 2 * dilation_factor
    running_total = jnp.zeros((tile_side, tile_side, kernel_weights.shape[2]), jnp.float32)
    for left_operand in range(3):
        for right_operand in range(3):
            window_patch = extended_tile[left_operand * dilation_factor:left_operand * dilation_factor + tile_side, right_operand * dilation_factor:right_operand * dilation_factor + tile_side].astype(jnp.float32)
            running_total = running_total + jnp.einsum("ijc,cd->ijd", window_patch, kernel_weights[3 * left_operand + right_operand].astype(jnp.float32))
    return running_total


def transposed_convolve(gradient_tile, kernel_weights, dilation_factor):
    running_total = jnp.zeros((gradient_tile.shape[0] + 2 * dilation_factor, gradient_tile.shape[1] + 2 * dilation_factor, kernel_weights.shape[1]), jnp.float32)
    for left_operand in range(3):
        for right_operand in range(3):
            product_term = jnp.einsum("ijd,cd->ijc", gradient_tile.astype(jnp.float32), kernel_weights[3 * left_operand + right_operand].astype(jnp.float32))
            running_total = running_total + jnp.pad(product_term, ((left_operand * dilation_factor, (2 - left_operand) * dilation_factor), (right_operand * dilation_factor, (2 - right_operand) * dilation_factor), (0, 0)))
    return running_total


def cross_correlate(extended_tile, gradient_tile, dilation_factor):
    tile_side = gradient_tile.shape[0]
    taps = []
    for left_operand in range(3):
        for right_operand in range(3):
            window_patch = extended_tile[left_operand * dilation_factor:left_operand * dilation_factor + tile_side, right_operand * dilation_factor:right_operand * dilation_factor + tile_side].astype(jnp.float32)
            taps.append(jnp.einsum("ijc,ijd->cd", window_patch, gradient_tile.astype(jnp.float32)))
    return jnp.stack(taps)


def reference(features, weights_first, weights_second, cotangent, neighbours, turns, corners):
    tiles = features.reshape(TILES, P_SIZE, P_SIZE, C)
    grads = cotangent.reshape(TILES, P_SIZE // 2, P_SIZE // 2, C)
    order = jnp.arange(TILES, dtype=jnp.int32)

    def first_pre(t):
        extended_tile = extend(tiles[t], tiles[neighbours[t]], turns[t], corners[t], 1)
        return extended_tile, tile_convolve(extended_tile, weights_first, 1)

    def first_out(t):
        z = first_pre(t)[1]
        return (z * jax.nn.sigmoid(z)).astype(jnp.bfloat16)

    y1 = lax.map(first_out, order)

    def second(carry, t):
        acc, gw = carry
        extended_tile = extend(y1[t], y1[neighbours[t]], turns[t], corners[t], 2)
        z = tile_convolve(extended_tile, weights_second, 2)
        s = jax.nn.sigmoid(z)
        pooled = (z * s).reshape(P_SIZE // 2, 2, P_SIZE // 2, 2, C).mean(axis=(1, 3)).astype(jnp.bfloat16)
        g_act = jnp.repeat(jnp.repeat(grads[t].astype(jnp.float32), 2, 0), 2, 1) * 0.25
        g_z = (g_act * s * (1.0 + z * (1.0 - s))).astype(jnp.bfloat16)
        gext = transposed_convolve(g_z, weights_second, 2)
        gw = gw + cross_correlate(extended_tile, g_z, 2)
        acc = acc.at[t].add(gext[2:-2, 2:-2])
        acc = acc.at[neighbours[t]].add(spill(gext, turns[t], corners[t], 2))
        return (acc, gw), pooled

    start = (jnp.zeros((TILES, P_SIZE, P_SIZE, C), jnp.float32), jnp.zeros((9, C, C), jnp.float32))
    (g_y1, grad_second), pooled = lax.scan(second, start, order)

    def first_back(carry, t):
        acc, gw = carry
        extended_tile, z = first_pre(t)
        s = jax.nn.sigmoid(z)
        g_z = (g_y1[t] * s * (1.0 + z * (1.0 - s))).astype(jnp.bfloat16)
        gext = transposed_convolve(g_z, weights_first, 1)
        gw = gw + cross_correlate(extended_tile, g_z, 1)
        acc = acc.at[t].add(gext[1:-1, 1:-1])
        acc = acc.at[neighbours[t]].add(spill(gext, turns[t], corners[t], 1))
        return (acc, gw), None

    (g_x, grad_first), unused = lax.scan(first_back, start, order)
    return (pooled.reshape(TILES, P_SIZE // 2, P_SIZE // 2 * C),
            g_x.astype(jnp.bfloat16).reshape(TILES, P_SIZE, P_SIZE * C),
            grad_first, grad_second)
```

```python
import jax
import jax.numpy as jnp
from jax import lax
from jax.experimental import pallas as pl
from jax.experimental.pallas import tpu as pltpu
from jax.sharding import PartitionSpec as P

REACH = 3


DIRS = ((-1, 0), (-1, 1), (0, 1), (1, 1), (1, 0), (1, -1), (0, -1), (-1, -1))


MESH = pl.DeviceIdType.MESH
GROUP = 16


def plane_peer(here, member):
    return here // 32 * 32 + member * 2 + here % 2


def column_peer(here, member):
    return member // 2 * 32 + here // 2 % 16 * 2 + member % 2


def reduce_kernel(
    src, out, plane_parts, column_parts, send_plane, recv_plane, send_column, recv_column, send_out, recv_out
):
    here = lax.axis_index("tiles")
    plane_me = here // 2 % 16
    column_me = here // 32 * 2 + here % 2
    barrier = pltpu.get_barrier_semaphore()

    def greet(k, unused):
        pl.semaphore_signal(
            barrier, inc=1, device_id=(plane_peer(here, (plane_me + k) % GROUP),), device_id_type=MESH
        )
        pl.semaphore_signal(
            barrier, inc=1, device_id=(column_peer(here, (column_me + k) % GROUP),), device_id_type=MESH
        )
        return unused

    lax.fori_loop(1, GROUP, greet, 0)
    pl.semaphore_wait(barrier, 2 * (GROUP - 1))

    def scatter_copy(k):
        peer = (plane_me + k) % GROUP
        return pltpu.make_async_remote_copy(
            src_ref=src.at[peer],
            dst_ref=plane_parts.at[plane_me],
            send_sem=send_plane.at[peer],
            recv_sem=recv_plane.at[plane_me],
            device_id=(plane_peer(here, peer),),
            device_id_type=MESH,
        )

    def column_copy(k):
        peer = (column_me + k) % GROUP
        return pltpu.make_async_remote_copy(
            src_ref=column_parts.at[column_me],
            dst_ref=column_parts.at[column_me],
            send_sem=send_column.at[peer],
            recv_sem=recv_column.at[column_me],
            device_id=(column_peer(here, peer),),
            device_id_type=MESH,
        )

    def gather_copy(k):
        peer = (plane_me + k) % GROUP
        return pltpu.make_async_remote_copy(
            src_ref=out.at[plane_me],
            dst_ref=out.at[plane_me],
            send_sem=send_out.at[peer],
            recv_sem=recv_out.at[plane_me],
            device_id=(plane_peer(here, peer),),
            device_id_type=MESH,
        )

    def arrived(buffer, sem, member):
        pltpu.make_async_copy(buffer.at[member], buffer.at[member], sem.at[member]).wait()

    def start_all(copy_of):
        def body(k, unused):
            copy_of(k).start()
            return unused

        lax.fori_loop(1, GROUP, body, 0)

    def wait_sends(copy_of):
        def body(k, unused):
            copy_of(k).wait_send()
            return unused

        lax.fori_loop(1, GROUP, body, 0)

    def wait_arrivals(buffer, sem, mine):
        def body(k, unused):
            arrived(buffer, sem, (mine + k) % GROUP)
            return unused

        lax.fori_loop(1, GROUP, body, 0)

    start_all(scatter_copy)
    plane_parts[plane_me] = src[plane_me]
    wait_arrivals(plane_parts, recv_plane, plane_me)
    column_parts[column_me] = jnp.sum(plane_parts[...], axis=0)
    start_all(column_copy)
    wait_arrivals(column_parts, recv_column, column_me)
    out[plane_me] = jnp.sum(column_parts[...], axis=0)
    start_all(gather_copy)
    wait_arrivals(out, recv_out, plane_me)
    wait_sends(scatter_copy)
    wait_sends(column_copy)
    wait_sends(gather_copy)


def sum_over_devices(first, second):
    flat = jnp.concatenate([first.reshape(-1, 128), second.reshape(-1, 128)], 0)
    rows = flat.shape[0]
    share = -(-rows // (8 * GROUP)) * 8
    flat = jnp.pad(flat, ((0, share * GROUP - rows), (0, 0))).reshape(GROUP, share, 128)
    total = pl.pallas_call(
        reduce_kernel,
        out_shape=jax.ShapeDtypeStruct(flat.shape, jnp.float32),
        in_specs=[pl.BlockSpec(memory_space=pltpu.VMEM)],
        out_specs=pl.BlockSpec(memory_space=pltpu.VMEM),
        scratch_shapes=[pltpu.VMEM(flat.shape, jnp.float32)] * 2
        + [pltpu.SemaphoreType.DMA((GROUP,))] * 6,
        compiler_params=pltpu.CompilerParams(collective_id=0, has_side_effects=True),
        name="reduce",
    )(flat)
    total = total.reshape(-1, 128)[:rows]
    half = rows // 2
    return total[:half].reshape(first.shape), total[half:].reshape(second.shape)


def from_behind(x, axis, by):
    count = lax.axis_size(axis)
    return lax.ppermute(x, axis, [(i, (i + by) % count) for i in range(count)])


def spans(step, width, tile_side):
    if step < 0:
        return slice(0, width)
    if step == 0:
        return slice(width, width + tile_side)
    return slice(width + tile_side, tile_side + 2 * width)


def needed_edge(dy, dx):
    if dy < 0:
        return 2
    if dy > 0:
        return 0
    if dx < 0:
        return 3
    return 1


def corner_cols(dx, width, tile_side):
    if dx < 0:
        return slice(tile_side - width, tile_side)
    return slice(0, width)


def natural(index, strip):
    if index % 2 == 1:
        return jnp.swapaxes(strip, 0, 1)
    return strip


def edges_of(field, width):
    tile_side = field.shape[1]
    top = field[:, :width]
    left = jnp.swapaxes(field[:, :, :width], 1, 2)
    bottom = field[:, tile_side - width :]
    right = jnp.swapaxes(field[:, :, tile_side - width :], 1, 2)
    return jnp.stack([top, left, bottom, right], 1)


def rim_of(strips, quarter, edge):
    result = None
    for steps in range(4):
        source_tile = (edge - steps) % 4
        candidate = jnp.rot90(natural(source_tile, strips[source_tile]), steps, axes=(0, 1))
        result = candidate if result is None else jnp.where(quarter == steps, candidate, result)
    return result


def extend_tile(owned_tile, nbr_strips, turn_row, corner_row, width):
    tile_side = owned_tile.shape[0]
    blocks = []
    for j, (dy, dx) in enumerate(DIRS):
        rim = rim_of(nbr_strips[j], turn_row[j], needed_edge(dy, dx))
        if dy != 0 and dx != 0:
            rim = rim[:, corner_cols(dx, width, tile_side)] * corner_row[j // 2].astype(rim.dtype)
        blocks.append(rim)
    upper = jnp.concatenate([blocks[7], blocks[0], blocks[1]], 1)
    middle = jnp.concatenate([blocks[6], owned_tile, blocks[2]], 1)
    lower = jnp.concatenate([blocks[5], blocks[4], blocks[3]], 1)
    return jnp.concatenate([upper, middle, lower], 0)


def return_tile(grad_ext, turn_row, corner_row, width):
    tile_side = grad_ext.shape[0] - 2 * width
    chans = grad_ext.shape[2]
    outputs = []
    for j, (dy, dx) in enumerate(DIRS):
        edge = needed_edge(dy, dx)
        block = grad_ext[spans(dy, width, tile_side), spans(dx, width, tile_side)]
        if dy != 0 and dx != 0:
            block = block * corner_row[j // 2].astype(block.dtype)
            placed = (
                jnp.zeros((width, tile_side, chans), block.dtype)
                .at[:, corner_cols(dx, width, tile_side)]
                .set(block)
            )
        else:
            placed = block
        slots = []
        for source_tile in range(4):
            steps = (edge - source_tile) % 4
            back = natural(source_tile, jnp.rot90(placed, -steps, axes=(0, 1)))
            slots.append(jnp.where(turn_row[j] == steps, back, jnp.zeros_like(back)))
        outputs.append(jnp.stack(slots))
    return jnp.stack(outputs)


def convolve_piece(
    source_tile, kernel_weights, dilation_factor, corner_anchor_point, row_total, column_total
):
    running_total = None
    for left_operand in range(3):
        for right_operand in range(3):
            row_start = row_total[0] - corner_anchor_point + left_operand * dilation_factor
            column_start = column_total[0] - corner_anchor_point + right_operand * dilation_factor
            window_patch = source_tile[
                :,
                row_start : row_start + row_total[1] - row_total[0],
                column_start : column_start + column_total[1] - column_total[0],
                :,
            ]
            product_term = jnp.einsum(
                "tijc,cd->tijd",
                window_patch,
                kernel_weights[3 * left_operand + right_operand],
                preferred_element_type=jnp.float32,
            )
            running_total = product_term if running_total is None else running_total + product_term
    return running_total


def transposed_convolve(gradient_tile, kernel_weights, dilation_factor):
    running_total = None
    for left_operand in range(3):
        for right_operand in range(3):
            product_term = jnp.einsum(
                "tijd,cd->tijc",
                gradient_tile,
                kernel_weights[3 * left_operand + right_operand],
                preferred_element_type=jnp.float32,
            )
            product_term = jnp.pad(
                product_term,
                (
                    (0, 0),
                    (left_operand * dilation_factor, (2 - left_operand) * dilation_factor),
                    (right_operand * dilation_factor, (2 - right_operand) * dilation_factor),
                    (0, 0),
                ),
            )
            running_total = product_term if running_total is None else running_total + product_term
    return running_total


def cross_correlate(extended_tile, gradient_tile, dilation_factor):
    tile_side = gradient_tile.shape[1]
    taps = []
    for left_operand in range(3):
        for right_operand in range(3):
            window_patch = extended_tile[
                :,
                left_operand * dilation_factor : left_operand * dilation_factor + tile_side,
                right_operand * dilation_factor : right_operand * dilation_factor + tile_side,
            ]
            taps.append(
                jnp.einsum(
                    "tijc,tijd->cd", window_patch, gradient_tile, preferred_element_type=jnp.float32
                )
            )
    return jnp.stack(taps)


def local(features, weights_first, weights_second, cotangent, neighbours, turns, corners):
    count = features.shape[0]
    tile_side = features.shape[1]
    chans = features.shape[2] // tile_side
    tiles = features.reshape(count, tile_side, tile_side, chans)
    devices = lax.axis_size("tiles")
    here = lax.axis_index("tiles")
    reach = REACH
    delta = (neighbours // count - here + reach) % devices - reach
    slot = (delta + reach) * count + neighbours % count

    def collect(package):
        pieces = {0: package}
        for offset in range(-reach, reach + 1):
            if offset != 0:
                pieces[offset] = from_behind(package, "tiles", -offset)
        return jnp.concatenate([pieces[offset] for offset in range(-reach, reach + 1)], 0)

    def neighbour_extend(owned_tile, width):
        package = edges_of(owned_tile, width).reshape(count, 4 * width, tile_side * chans)
        pool = collect(package).reshape(-1, 4, width, tile_side, chans)
        nbr_strips = pool[slot]
        return jax.vmap(lambda o, n, r, c: extend_tile(o, n, r, c, width))(
            owned_tile, nbr_strips, turns, corners
        )

    def forward_convolve(owned_tile, kernel_weights, dilation_factor):
        extended_tile = neighbour_extend(owned_tile, dilation_factor)
        return (
            extended_tile,
            convolve_piece(
                extended_tile, kernel_weights, dilation_factor, 0, (0, tile_side), (0, tile_side)
            ),
        )

    def give_back(grad_ext, width):
        returned = jax.vmap(lambda g, r, c: return_tile(g, r, c, width))(grad_ext, turns, corners)
        messages = returned.reshape(count * 8, 4 * width * tile_side * chans)
        target = slot.reshape(count * 8)
        places = jnp.arange((2 * reach + 1) * count, dtype=jnp.int32)
        onehot = (target[None, :] == places[:, None]).astype(jnp.float32)
        buffers = jnp.dot(onehot, messages, precision=lax.Precision.HIGHEST)
        buffers = buffers.reshape(2 * reach + 1, count, 4 * width, tile_side * chans)
        running_total = buffers[reach]
        for offset in range(-reach, reach + 1):
            if offset != 0:
                running_total = running_total + from_behind(
                    buffers[offset + reach], "tiles", offset
                )
        strips = running_total.reshape(count, 4, width, tile_side, chans)
        field = grad_ext[:, width : width + tile_side, width : width + tile_side]
        field = field.at[:, :width].add(strips[:, 0])
        field = field.at[:, :, :width].add(jnp.swapaxes(strips[:, 1], 1, 2))
        field = field.at[:, tile_side - width :].add(strips[:, 2])
        field = field.at[:, :, tile_side - width :].add(jnp.swapaxes(strips[:, 3], 1, 2))
        return field

    ext_first, z_first = forward_convolve(tiles, weights_first, 1)
    s_first = jax.nn.sigmoid(z_first)
    y_first = (z_first * s_first).astype(jnp.bfloat16)
    ext_second, z_second = forward_convolve(y_first, weights_second, 2)
    s_second = jax.nn.sigmoid(z_second)
    pooled = (
        (z_second * s_second)
        .reshape(count, tile_side // 2, 2, tile_side // 2, 2, chans)
        .mean(axis=(2, 4))
    )
    pooled = pooled.astype(jnp.bfloat16)
    upstream = cotangent.reshape(count, tile_side // 2, tile_side // 2, chans).astype(jnp.float32)
    g_act = jnp.repeat(jnp.repeat(upstream, 2, 1), 2, 2) * 0.25
    g_second = (g_act * s_second * (1.0 + z_second * (1.0 - s_second))).astype(jnp.bfloat16)
    gext_second = transposed_convolve(g_second, weights_second, 2)
    wgrad_second = cross_correlate(ext_second, g_second, 2)
    g_y_first = give_back(gext_second, 2)
    g_first = (g_y_first * s_first * (1.0 + z_first * (1.0 - s_first))).astype(jnp.bfloat16)
    gext_first = transposed_convolve(g_first, weights_first, 1)
    wgrad_first = cross_correlate(ext_first, g_first, 1)
    g_input = give_back(gext_first, 1)
    grad_first, grad_second = sum_over_devices(wgrad_first, wgrad_second)
    return (
        pooled.reshape(count, tile_side // 2, tile_side // 2 * chans),
        g_input.astype(jnp.bfloat16).reshape(count, tile_side, tile_side * chans),
        grad_first,
        grad_second,
    )


def solution(mesh):
    return jax.shard_map(
        local,
        mesh=mesh,
        in_specs=(
            P("tiles", None, None),
            P(),
            P(),
            P("tiles", None, None),
            P("tiles", None),
            P("tiles", None),
            P("tiles", None),
        ),
        out_specs=(P("tiles", None, None), P("tiles", None, None), P(), P()),
        check_vma=False,
    )
```

```python
import functools

import jax
import jax.numpy as jnp
from jax import lax
from jax.experimental import pallas as pl
from jax.experimental.pallas import tpu as pltpu
from jax.sharding import PartitionSpec as P

REACH = 3
SLOTS = 2 * REACH + 1
SIDE = 64
CHANS = 64
PAIRS = SIDE // 2
ROWS = PAIRS * SIDE
STRIP = 4 * SIDE
GROUP = 16
SHARE = 24
CHUNK = 8
RIMS = 4 * SIDE + 32
MESH = pl.DeviceIdType.MESH
BF16 = jnp.bfloat16
F32 = jnp.float32
EDGE_DIRS = ((0, 2), (2, 1), (4, 0), (6, 3))
CORNER_DIRS = ((1, 2, False), (3, 0, False), (5, 0, True), (7, 2, True))
OFFSETS = (1, -1, 2, -2, 3, -3)


def dot(a, b):
    return jnp.dot(a, b, preferred_element_type=F32)


def dot_rows(a, b):
    return lax.dot_general(a, b, (((0,), (0,)), ((), ())), preferred_element_type=F32)


def half_turn(x):
    return pltpu.roll(x, 64, axis=1)


def low_half(x):
    return lax.broadcasted_iota(jnp.int32, x.shape, 1) < 64


def swap(x, y):
    low = low_half(x)
    return jnp.where(low, x, half_turn(y)), jnp.where(low, half_turn(x), y)


def sigmoid(z):
    return 1.0 / (1.0 + jnp.exp(-z))


def plane_peer(here, member):
    return here // 32 * 32 + member * 2 + here % 2


def column_peer(here, member):
    return member // 2 * 32 + here // 2 % 16 * 2 + member % 2


def blocks_of(w_ref, dilation, turned):
    taps = [w_ref[t].astype(F32) for t in range(9)]
    if turned:
        taps = [jnp.transpose(tap) for tap in taps]
    zero = jnp.zeros((CHANS, CHANS), F32)
    result = {}
    for a in range(3):
        left, mid, right = taps[3 * a : 3 * a + 3]
        if dilation == 2:
            quads = {d: (w, zero, zero, w) for d, w in ((-1, left), (0, mid), (1, right))}
        else:
            quads = {-1: (zero, zero, left, zero), 0: (mid, left, right, mid), 1: (zero, right, zero, zero)}
        for d, (q00, q01, q10, q11) in quads.items():
            if turned:
                q01, q10 = q10, q01
                d = -d
            block = jnp.concatenate(
                [jnp.concatenate([q00, q01], 1), jnp.concatenate([q10, q11], 1)], 0
            )
            result[a, d] = block.astype(BF16)
    return result


def fill_weights(w_ref, dilation, turned, big):
    for (a, d), block in blocks_of(w_ref, dilation, turned).items():
        big[(d + 1) * 128 : (d + 2) * 128, a * 128 : (a + 1) * 128] = block


def combine(product, dilation, turned):
    rows = product.shape[0]
    up, mid, down = product[:, :128], product[:, 128:256], product[:, 256:]
    if turned:
        up, down = down, up
    i = lax.broadcasted_iota(jnp.int32, (rows, 128), 0) % SIDE
    up = jnp.where(i >= dilation, pltpu.roll(up, dilation, axis=0), 0.0)
    down = jnp.where(i < SIDE - dilation, pltpu.roll(down, rows - dilation, axis=0), 0.0)
    return mid + up + down


def neighbouring(x_ref, start, count):
    parts = [x_ref[pl.ds(start + k, count)].reshape(count * SIDE, 128) for k in range(3)]
    return jnp.concatenate(parts, 1)


def chunks(body):
    def step(c, unused):
        body(c)
        return unused

    lax.fori_loop(0, PAIRS // CHUNK, step, 0)


def chunk_rows(c):
    return pl.ds(pl.multiple_of(c * (CHUNK * SIDE), CHUNK * SIDE), CHUNK * SIDE)


def convolve(x_ref, big, z_ref, dilation):
    def body(c):
        product = dot(neighbouring(x_ref, c * CHUNK, CHUNK), big[...])
        z_ref[chunk_rows(c), :] = combine(product, dilation, False)

    chunks(body)


def keep_edges(edge_ref, c, value):
    value = value.reshape(CHUNK, SIDE, 128)
    place = pl.ds(pl.multiple_of(c * (CHUNK * 8), CHUNK * 8), CHUNK * 8)
    edge_ref[0, place, :] = value[:, :8].reshape(CHUNK * 8, 128)
    edge_ref[1, place, :] = value[:, SIDE - 8 :].reshape(CHUNK * 8, 128)


def edge_row(edge_ref, side, depth):
    return edge_ref[side, pl.ds(depth if side == 0 else 7 - depth, PAIRS, stride=8), :]


def write_strips(x_ref, edge_ref, strip_ref):
    top = swap(edge_row(edge_ref, 0, 0), edge_row(edge_ref, 0, 1))
    bottom = swap(edge_row(edge_ref, 1, 0), edge_row(edge_ref, 1, 1))
    strip_ref[0:64] = jnp.concatenate(top, 0).astype(BF16)
    strip_ref[64:128] = x_ref[1]
    strip_ref[128:192] = jnp.concatenate(bottom, 0).astype(BF16)
    strip_ref[192:256] = half_turn(x_ref[PAIRS].astype(F32)).astype(BF16)


def fill_select(here, devices, nbr_ref, turn_ref, corner_ref, select):
    def slot_of(j):
        return lax.rem(nbr_ref[0, j] - here + REACH + devices, devices)

    def columns_of(p, edge, quarter, flips):
        source = lax.rem(edge + 4 - quarter, 4)
        flip = jnp.where(quarter == flips[0], 1, jnp.where(quarter == flips[1], 1, 0))
        p = p + flip * (63 - 2 * p)
        split = (p % 2) * 32 + p // 2
        place = split + lax.rem(source, 2) * (p - split)
        return source * 64 + place

    lane = lax.broadcasted_iota(jnp.int32, (SIDE, STRIP), 1)
    row = lax.broadcasted_iota(jnp.int32, (SIDE, STRIP), 0)
    for n, (j, edge) in enumerate(EDGE_DIRS):
        if edge % 2 == 0:
            cols = columns_of(row % 32 * 2 + row // 32, edge, turn_ref[0, j], (2, 3))
        else:
            cols = columns_of(row, edge, turn_ref[0, j], (1, 2))
        hit = jnp.where(lane == cols, 1.0, 0.0)
        slot = slot_of(j)
        for k in range(SLOTS):
            select[k, n * 64 : (n + 1) * 64] = (hit * jnp.where(slot == k, 1.0, 0.0)).astype(BF16)
    lane = lane[:8]
    row = row[:8]
    hits = []
    for j, edge, last in CORNER_DIRS:
        cols = columns_of(63 - row if last else row, edge, turn_ref[0, j], (2, 3))
        hit = jnp.where(lane == cols, 1.0, 0.0) * jnp.where(row < 2, 1.0, 0.0)
        hits.append((hit * corner_ref[0, j // 2].astype(F32), slot_of(j)))
    for k in range(SLOTS):
        parts = [hit * jnp.where(slot == k, 1.0, 0.0) for hit, slot in hits]
        select[k, 256:288] = jnp.concatenate(parts, 0).astype(BF16)


def place_rims(rims, x_ref, rows_ref):
    north, east, south, west = (rims[64 * n : 64 * n + 64] for n in range(4))
    x_ref[PAIRS + 1] = east.astype(BF16)
    x_ref[0] = half_turn(west).astype(BF16)
    ne, se, sw, nw = (rims[256 + 8 * n : 264 + 8 * n] for n in range(4))
    for base, strip, right, left in ((0, north, ne, nw), (2, south, se, sw)):
        inner = swap(strip[:32], strip[32:])
        ends = swap(right[0:1], right[1:2])
        starts = swap(left[1:2], left[0:1])
        for d in range(2):
            rows_ref[base + d, 8:40, :] = inner[d]
            rows_ref[base + d, 40:41, :] = ends[d]
            rows_ref[base + d, 7:8, :] = starts[d]


def strips_beside(rows_ref):
    parts = []
    for k in range(4):
        parts.append(jnp.concatenate([rows_ref[k, 7 + d : 39 + d, :] for d in range(3)], 1))
    return jnp.concatenate(parts, 0).astype(BF16)


def add_rims(x_ref, beside, big, z_ref, dilation):
    west = combine(dot(x_ref[0], big[0:128, :]), dilation, False)
    z_ref[0:64, :] += west
    east = combine(dot(x_ref[PAIRS + 1], big[256:384, :]), dilation, False)
    z_ref[ROWS - 64 : ROWS, :] += east
    north = dot(beside[:64], big[:, 0:128])
    south = dot(beside[64:], big[:, 256:384])
    for d in range(dilation):
        z_ref[pl.ds(dilation - 1 - d, PAIRS, stride=SIDE), :] += north[32 * d : 32 * d + 32]
        z_ref[pl.ds(SIDE - dilation + d, PAIRS, stride=SIDE), :] += south[32 * d : 32 * d + 32]


def transposed(g_ref, big, z_ref, edge_ref, dilation):
    def keep(place, product):
        count = product.shape[0] // SIDE
        value = product.reshape(count, SIDE, 384)
        edge_ref[0, place, :] = value[:, :8, 0:128].reshape(count * 8, 128)
        edge_ref[1, place, :] = value[:, SIDE - 8 :, 256:384].reshape(count * 8, 128)

    def body(c):
        product = dot(neighbouring(g_ref, c * CHUNK, CHUNK), big[...])
        z_ref[chunk_rows(c), :] = combine(product, dilation, True)
        keep(pl.ds(pl.multiple_of(c * (CHUNK * 8) + 8, 8), CHUNK * 8), product)

    chunks(body)
    before = dot(g_ref[1], big[256:384, :])
    after = dot(g_ref[PAIRS], big[0:128, :])
    keep(pl.ds(0, 8), before)
    keep(pl.ds(8 * PAIRS + 8, 8), after)
    return combine(before, dilation, True), combine(after, dilation, True)


def leaving_rims(edge_ref, before, after, dilation):
    def row_strip(side, depth, start, count):
        if depth >= dilation:
            return jnp.zeros((count, 128), F32)
        row = dilation - 1 - depth if side == 0 else 8 - dilation + depth
        if count == 1:
            return edge_ref[side, 8 * start + row : 8 * start + row + 1, :]
        return edge_ref[side, pl.ds(8 * start + row, count, stride=8), :]

    strips, corners = [], []
    gap = jnp.zeros((6, 128), F32)
    for side in range(2):
        inner = [row_strip(side, d, 1, PAIRS) for d in range(2)]
        strips.append(jnp.concatenate(swap(*inner), 0))
        first, second = swap(*[row_strip(side, d, PAIRS + 1, 1) for d in range(2)])
        right = jnp.concatenate([first, second, gap], 0)
        second, first = swap(*[row_strip(side, d, 0, 1) for d in range(2)])
        left = jnp.concatenate([first, second, gap], 0)
        corners.append((right, left))
    order = [strips[0], after, strips[1], half_turn(before)]
    order += [corners[0][0], corners[1][0], corners[1][1], corners[0][1]]
    return jnp.concatenate(order, 0).astype(BF16)


def add_returned(strips, z_ref, dilation):
    z_ref[0:64, :] += strips[64:128]
    z_ref[ROWS - 64 : ROWS, :] += half_turn(strips[192:256])
    top = swap(strips[0:32], strips[32:64])
    bottom = swap(strips[128:160], strips[160:192])
    for d in range(dilation):
        z_ref[pl.ds(d, PAIRS, stride=SIDE), :] += top[d]
        z_ref[pl.ds(SIDE - 1 - d, PAIRS, stride=SIDE), :] += bottom[d]


def write_gradient(c, g, dilation, g_ref, shifted, edge_ref):
    rows = CHUNK * SIDE
    g_ref[pl.ds(c * CHUNK + 1, CHUNK)] = g.astype(BF16).reshape(CHUNK, SIDE, 128)
    i = lax.broadcasted_iota(jnp.int32, (rows, 128), 0) % SIDE
    up = jnp.where(i < SIDE - dilation, pltpu.roll(g, rows - dilation, axis=0), 0.0)
    down = jnp.where(i >= dilation, pltpu.roll(g, dilation, axis=0), 0.0)
    shifted[chunk_rows(c), 0:128] = up.astype(BF16)
    shifted[chunk_rows(c), 128:256] = g.astype(BF16)
    shifted[chunk_rows(c), 256:384] = down.astype(BF16)
    keep_edges(edge_ref, c, g)


def weight_gradient(x_ref, shifted, beside, edge_ref, raw, dilation):
    strip_grads = []
    zero = jnp.zeros((PAIRS, 128), F32)
    for side in range(2):
        for d in range(2):
            if d >= dilation:
                part = jnp.zeros((PAIRS, 384), F32)
            else:
                row = edge_row(edge_ref, side, dilation - 1 - d)
                part = jnp.concatenate([row, zero, zero] if side == 0 else [zero, zero, row], 1)
            strip_grads.append(part)
    strip_grads = jnp.concatenate(strip_grads, 0).astype(BF16)
    for k in range(3):
        total = dot_rows(x_ref[k : k + PAIRS].reshape(ROWS, 128), shifted[...])
        raw[k] = total + dot_rows(beside[:, 128 * k : 128 * k + 128], strip_grads)
    taps = []
    for a in range(3):
        lanes = slice(128 * a, 128 * a + 128)
        upper = [raw[k, 0:64, lanes] for k in range(3)]
        lower = [raw[k, 64:128, lanes] for k in range(3)]
        if dilation == 2:
            taps += [upper[k] + half_turn(lower[k]) for k in range(3)]
        else:
            taps.append(half_turn(upper[1]) + lower[0])
            taps.append(upper[1] + half_turn(lower[1]))
            taps.append(lower[1] + half_turn(upper[2]))
    zero = jnp.zeros((CHANS, 128), F32)
    taps.append(zero)
    low = low_half(zero)
    packed = [jnp.where(low, taps[t], half_turn(taps[t + 1])) for t in range(0, 10, 2)] + [zero]
    return jnp.concatenate(packed, 0).reshape(GROUP, SHARE, 128)


def write_taps(total_ref, out_ref):
    flat = total_ref[...].reshape(GROUP * SHARE, 128)
    for t in range(9):
        block = flat[t // 2 * 64 : t // 2 * 64 + 64]
        if t % 2 == 1:
            block = half_turn(block)
        out_ref[t] = block[:, :CHANS]


class Ring:
    def __init__(self, here, devices, source, target, send, recv):
        self.here, self.devices = here, devices
        self.source, self.target, self.send, self.recv = source, target, send, recv

    def copy(self, offset):
        return pltpu.make_async_remote_copy(
            src_ref=self.source(offset),
            dst_ref=self.target.at[REACH - offset],
            send_sem=self.send.at[REACH + offset],
            recv_sem=self.recv.at[REACH - offset],
            device_id=(lax.rem(self.here + offset + self.devices, self.devices),),
            device_id_type=MESH,
        )

    def start(self, offset):
        self.copy(offset).start()

    def arrived(self, slot):
        there = self.target.at[slot]
        pltpu.make_async_copy(there, there, self.recv.at[slot]).wait()

    def finish(self):
        for offset in OFFSETS:
            self.copy(offset).wait_send()


class Reduction:
    def __init__(self, here, src, plane, column, out, sems):
        self.here, self.src, self.plane, self.column, self.out = here, src, plane, column, out
        self.sems = sems
        self.me = here // 2 % 16
        self.level = here // 32 * 2 + here % 2

    def scatter_copy(self, k):
        peer = (self.me + k) % GROUP
        return pltpu.make_async_remote_copy(
            src_ref=self.src.at[peer], dst_ref=self.plane.at[self.me],
            send_sem=self.sems.at[0, peer], recv_sem=self.sems.at[1, self.me],
            device_id=(plane_peer(self.here, peer),), device_id_type=MESH,
        )

    def column_copy(self, k):
        peer = (self.level + k) % GROUP
        return pltpu.make_async_remote_copy(
            src_ref=self.column.at[self.level], dst_ref=self.column.at[self.level],
            send_sem=self.sems.at[2, peer], recv_sem=self.sems.at[3, self.level],
            device_id=(column_peer(self.here, peer),), device_id_type=MESH,
        )

    def gather_copy(self, k):
        peer = (self.me + k) % GROUP
        return pltpu.make_async_remote_copy(
            src_ref=self.out.at[self.me], dst_ref=self.out.at[self.me],
            send_sem=self.sems.at[4, peer], recv_sem=self.sems.at[5, self.me],
            device_id=(plane_peer(self.here, peer),), device_id_type=MESH,
        )

    def each(self, act):
        def body(k, unused):
            act(k)
            return unused

        lax.fori_loop(1, GROUP, body, 0)

    def arrivals(self, buffer, row, mine):
        def one(k):
            there = buffer.at[(mine + k) % GROUP]
            pltpu.make_async_copy(there, there, self.sems.at[row, (mine + k) % GROUP]).wait()

        self.each(one)

    def scatter(self, value):
        self.src[...] = value
        self.each(lambda k: self.scatter_copy(k).start())
        self.plane[self.me] = self.src[self.me]

    def across(self):
        self.arrivals(self.plane, 1, self.me)
        self.column[self.level] = jnp.sum(self.plane[...], axis=0)
        self.each(lambda k: self.column_copy(k).start())

    def gather(self):
        self.arrivals(self.column, 3, self.level)
        self.out[self.me] = jnp.sum(self.column[...], axis=0)
        self.each(lambda k: self.gather_copy(k).start())

    def finish(self):
        self.arrivals(self.out, 5, self.me)
        self.each(lambda k: self.scatter_copy(k).wait_send())
        self.each(lambda k: self.column_copy(k).wait_send())
        self.each(lambda k: self.gather_copy(k).wait_send())


def level_kernel(
    devices,
    f_ref, w1_ref, w2_ref, cot_ref, nbr_ref, turn_ref, corner_ref,
    pooled_ref, gin_ref, dw1_ref, dw2_ref,
    x1, x2, g_ref, shifted, z_ref, d_ref, act_ref, edge_ref, wide_edge, rows1, rows2, raw,
    big1, big1t, big2, big2t, select,
    pool1, pool2, out2, back2, out1, back1,
    src2, plane2, column2, total2, src1, plane1, column1, total1,
    ring_sems, sems2, sems1,
):
    here = lax.axis_index("tiles")
    barrier = pltpu.get_barrier_semaphore()

    def greet(device):
        pl.semaphore_signal(barrier, inc=1, device_id=(device,), device_id_type=MESH)

    for offset in OFFSETS:
        greet(lax.rem(here + offset + devices, devices))

    def greet_group(k, unused):
        greet(plane_peer(here, (here // 2 + k) % GROUP))
        greet(column_peer(here, (here // 32 * 2 + here % 2 + k) % GROUP))
        return unused

    lax.fori_loop(1, GROUP, greet_group, 0)

    for jp in range(PAIRS):
        x1[jp + 1] = f_ref[:, 128 * jp : 128 * jp + 128]
    empty = jnp.zeros((SIDE, 128), BF16)
    for x in (x1, x2, g_ref):
        x[0] = empty
        x[PAIRS + 1] = empty
    for jp in range(PAIRS):
        edge_ref[0, 8 * jp : 8 * jp + 8, :] = f_ref[0:16, 128 * jp : 128 * jp + 128].astype(F32)[:8]
        edge_ref[1, 8 * jp : 8 * jp + 8, :] = f_ref[48:64, 128 * jp : 128 * jp + 128].astype(F32)[8:]
    write_strips(x1, edge_ref, pool1.at[REACH])

    ring1 = Ring(here, devices, lambda o: pool1.at[REACH], pool1, ring_sems.at[0], ring_sems.at[1])
    ring2 = Ring(here, devices, lambda o: pool2.at[REACH], pool2, ring_sems.at[2], ring_sems.at[3])
    ring3 = Ring(here, devices, lambda o: out2.at[REACH + o], back2, ring_sems.at[4], ring_sems.at[5])
    ring4 = Ring(here, devices, lambda o: out1.at[REACH + o], back1, ring_sems.at[6], ring_sems.at[7])
    sum2 = Reduction(here, src2, plane2, column2, total2, sems2)
    sum1 = Reduction(here, src1, plane1, column1, total1, sems1)

    def collect(ring, pool):
        rims = dot(select[REACH], pool[REACH])
        for offset in OFFSETS:
            slot = REACH - offset
            ring.arrived(slot)
            rims = rims + dot(select[slot], pool[slot])
        return rims

    def send_back(ring, out_ref, rims):
        for offset in OFFSETS:
            out_ref[REACH + offset] = dot_rows(select[REACH + offset], rims).astype(BF16)
            ring.start(offset)
        return dot_rows(select[REACH], rims)

    def take_back(ring, back_ref, own):
        for offset in OFFSETS:
            ring.arrived(REACH - offset)
            own = own + back_ref[REACH - offset].astype(F32)
        return own

    pl.semaphore_wait(barrier, 2 * REACH + 2 * (GROUP - 1))
    for offset in OFFSETS:
        ring1.start(offset)

    fill_weights(w1_ref, 1, False, big1)
    convolve(x1, big1, z_ref, 1)
    fill_select(here, devices, nbr_ref, turn_ref, corner_ref, select)
    fill_weights(w2_ref, 2, False, big2)
    fill_weights(w2_ref, 2, True, big2t)
    fill_weights(w1_ref, 1, True, big1t)
    low = lax.broadcasted_iota(jnp.int32, (PAIRS, 128), 1) < 64
    for t in range(PAIRS // 2):
        both = cot_ref[:, 128 * t : 128 * t + 128].astype(F32) * 0.25
        turned = half_turn(both)
        for jp, value in ((2 * t, jnp.where(low, both, turned)), (2 * t + 1, jnp.where(low, turned, both))):
            act_ref[pl.ds(SIDE * jp, PAIRS, stride=2), :] = value
            act_ref[pl.ds(SIDE * jp + 1, PAIRS, stride=2), :] = value
    place_rims(collect(ring1, pool1), x1, rows1)
    beside1 = strips_beside(rows1)
    add_rims(x1, beside1, big1, z_ref, 1)

    def activate(c):
        z = z_ref[chunk_rows(c), :]
        s = sigmoid(z)
        y = z * s
        d_ref[chunk_rows(c), :] = s * (1.0 + z * (1.0 - s))
        x2[pl.ds(c * CHUNK + 1, CHUNK)] = y.astype(BF16).reshape(CHUNK, SIDE, 128)
        keep_edges(edge_ref, c, y)

    chunks(activate)
    write_strips(x2, edge_ref, pool2.at[REACH])
    for offset in OFFSETS:
        ring2.start(offset)

    convolve(x2, big2, z_ref, 2)
    place_rims(collect(ring2, pool2), x2, rows2)
    beside2 = strips_beside(rows2)
    add_rims(x2, beside2, big2, z_ref, 2)

    def second(c):
        z = z_ref[chunk_rows(c), :]
        s = sigmoid(z)
        z_ref[chunk_rows(c), :] = z * s * 0.25
        g = act_ref[chunk_rows(c), :] * s * (1.0 + z * (1.0 - s))
        write_gradient(c, g.astype(BF16).astype(F32), 2, g_ref, shifted, edge_ref)

    chunks(second)
    for t in range(PAIRS // 2):
        sums = []
        for jp in (2 * t, 2 * t + 1):
            v = z_ref[pl.ds(SIDE * jp, PAIRS, stride=2), :] + z_ref[pl.ds(SIDE * jp + 1, PAIRS, stride=2), :]
            sums.append(v + half_turn(v))
        pooled_ref[:, 128 * t : 128 * t + 128] = jnp.where(low, sums[0], sums[1]).astype(BF16)

    before, after = transposed(g_ref, big2t, z_ref, wide_edge, 2)
    own = send_back(ring3, out2, leaving_rims(wide_edge, before, after, 2))
    sum2.scatter(weight_gradient(x2, shifted, beside2, edge_ref, raw, 2))
    add_returned(take_back(ring3, back2, own), z_ref, 2)

    def first(c):
        g = z_ref[chunk_rows(c), :] * d_ref[chunk_rows(c), :]
        write_gradient(c, g.astype(BF16).astype(F32), 1, g_ref, shifted, edge_ref)

    chunks(first)
    sum2.across()

    sum1.scatter(weight_gradient(x1, shifted, beside1, edge_ref, raw, 1))
    before, after = transposed(g_ref, big1t, z_ref, wide_edge, 1)
    own = send_back(ring4, out1, leaving_rims(wide_edge, before, after, 1))
    sum2.gather()
    sum1.across()
    add_returned(take_back(ring4, back1, own), z_ref, 1)
    for jp in range(PAIRS):
        gin_ref[:, 128 * jp : 128 * jp + 128] = z_ref[SIDE * jp : SIDE * jp + SIDE, :].astype(BF16)
    sum1.gather()
    sum2.finish()
    write_taps(total2, dw2_ref)
    for ring in (ring1, ring2, ring3, ring4):
        ring.finish()
    sum1.finish()
    write_taps(total1, dw1_ref)


def local(features, weights_first, weights_second, cotangent, neighbours, turns, corners):
    devices = lax.axis_size("tiles")
    vmem = pl.BlockSpec(memory_space=pltpu.VMEM)
    smem = pl.BlockSpec(memory_space=pltpu.SMEM)
    slabs = pltpu.VMEM((PAIRS + 2, SIDE, 128), BF16)
    field = pltpu.VMEM((ROWS, 128), F32)
    big = pltpu.VMEM((384, 384), BF16)
    pool = pltpu.VMEM((SLOTS, STRIP, 128), BF16)
    share = pltpu.VMEM((GROUP, SHARE, 128), F32)
    pooled, grad, first, second = pl.pallas_call(
        functools.partial(level_kernel, devices),
        out_shape=(
            jax.ShapeDtypeStruct((PAIRS, PAIRS * CHANS), BF16),
            jax.ShapeDtypeStruct((SIDE, SIDE * CHANS), BF16),
            jax.ShapeDtypeStruct((9, CHANS, CHANS), F32),
            jax.ShapeDtypeStruct((9, CHANS, CHANS), F32),
        ),
        in_specs=[vmem] * 4 + [smem] * 3,
        out_specs=[vmem] * 4,
        scratch_shapes=[
            slabs, slabs, slabs,
            pltpu.VMEM((ROWS, 384), BF16),
            field, field, field,
            pltpu.VMEM((2, 8 * PAIRS, 128), F32),
            pltpu.VMEM((2, 8 * PAIRS + 16, 128), F32),
            pltpu.VMEM((4, 48, 128), F32),
            pltpu.VMEM((4, 48, 128), F32),
            pltpu.VMEM((3, 128, 384), F32),
            big, big, big, big,
            pltpu.VMEM((SLOTS, RIMS, STRIP), BF16),
            pool, pool, pool, pool, pool, pool,
            share, share, share, share, share, share, share, share,
            pltpu.SemaphoreType.DMA((8, SLOTS)),
            pltpu.SemaphoreType.DMA((6, GROUP)),
            pltpu.SemaphoreType.DMA((6, GROUP)),
        ],
        compiler_params=pltpu.CompilerParams(
            collective_id=0, has_side_effects=True, vmem_limit_bytes=48 * 2**20
        ),
        name="level",
    )(features[0], weights_first, weights_second, cotangent[0], neighbours, turns, corners)
    return pooled[None], grad[None], first, second


def solution(mesh):
    return jax.shard_map(
        local,
        mesh=mesh,
        in_specs=(
            P("tiles", None, None),
            P(),
            P(),
            P("tiles", None, None),
            P("tiles", None),
            P("tiles", None),
            P("tiles", None),
        ),
        out_specs=(P("tiles", None, None), P("tiles", None, None), P(), P()),
        check_vma=False,
    )
```

```python
import functools

import jax
import jax.numpy as jnp
from jax import lax
from jax.experimental import pallas as pl
from jax.experimental.pallas import tpu as pltpu
from jax.sharding import PartitionSpec as P

REACH = 3
SLOTS = 2 * REACH + 1
SIDE = 64
CHANS = 64
PAIRS = SIDE // 2
ROWS = PAIRS * SIDE
STRIP = 4 * SIDE
PLANE = 16
LEVELS = 8
SHARE = 9
CHUNK = 8
RIMS = 4 * SIDE + 32
MESH = pl.DeviceIdType.MESH
BF16 = jnp.bfloat16
F32 = jnp.float32
EDGE_DIRS = ((0, 2), (2, 1), (4, 0), (6, 3))
CORNER_DIRS = ((1, 2, False), (3, 0, False), (5, 0, True), (7, 2, True))
FAR_FIRST = (3, -3, 2, -2, 1, -1)
NEAR_FIRST = (1, -1, 2, -2, 3, -3)


def dot(a, b):
    return jnp.dot(a, b, preferred_element_type=F32)


def dot_rows(a, b):
    return lax.dot_general(a, b, (((0,), (0,)), ((), ())), preferred_element_type=F32)


def half_turn(x):
    return pltpu.roll(x, 64, axis=1)


def low_half(x):
    return lax.broadcasted_iota(jnp.int32, x.shape, 1) < 64


def swap(x, y):
    low = low_half(x)
    return jnp.where(low, x, half_turn(y)), jnp.where(low, half_turn(x), y)


def sigmoid(z):
    return 1.0 / (1.0 + jnp.exp(-z))


def plane_peer(here, member):
    return here // 32 * 32 + member * 2 + here % 2


def level_peer(here, member):
    return member * 32 + here % 32


def blocks_of(w_ref, dilation, turned):
    taps = [w_ref[t].astype(F32) for t in range(9)]
    if turned:
        taps = [jnp.transpose(tap) for tap in taps]
    zero = jnp.zeros((CHANS, CHANS), F32)
    result = {}
    for a in range(3):
        left, mid, right = taps[3 * a : 3 * a + 3]
        if dilation == 2:
            quads = {d: (w, zero, zero, w) for d, w in ((-1, left), (0, mid), (1, right))}
        else:
            quads = {-1: (zero, zero, left, zero), 0: (mid, left, right, mid), 1: (zero, right, zero, zero)}
        for d, (q00, q01, q10, q11) in quads.items():
            if turned:
                q01, q10 = q10, q01
                d = -d
            block = jnp.concatenate(
                [jnp.concatenate([q00, q01], 1), jnp.concatenate([q10, q11], 1)], 0
            )
            result[a, d] = block.astype(BF16)
    return result


def fill_weights(w_ref, dilation, turned, big):
    for (a, d), block in blocks_of(w_ref, dilation, turned).items():
        big[(d + 1) * 128 : (d + 2) * 128, a * 128 : (a + 1) * 128] = block


def combine(product, dilation, turned):
    rows = product.shape[0]
    up, mid, down = product[:, :128], product[:, 128:256], product[:, 256:]
    if turned:
        up, down = down, up
    i = lax.broadcasted_iota(jnp.int32, (rows, 128), 0) % SIDE
    up = jnp.where(i >= dilation, pltpu.roll(up, dilation, axis=0), 0.0)
    down = jnp.where(i < SIDE - dilation, pltpu.roll(down, rows - dilation, axis=0), 0.0)
    return mid + up + down


def neighbouring(x_ref, start, count):
    parts = [x_ref[pl.ds(start + k, count)].reshape(count * SIDE, 128) for k in range(3)]
    return jnp.concatenate(parts, 1)


def chunks(body):
    def step(c, unused):
        body(c)
        return unused

    lax.fori_loop(0, PAIRS // CHUNK, step, 0)


def chunk_rows(c):
    return pl.ds(pl.multiple_of(c * (CHUNK * SIDE), CHUNK * SIDE), CHUNK * SIDE)


def convolve(x_ref, big, z_ref, dilation):
    def body(c):
        product = dot(neighbouring(x_ref, c * CHUNK, CHUNK), big[...])
        z_ref[chunk_rows(c), :] = combine(product, dilation, False)

    chunks(body)


def keep_edges(edge_ref, c, value):
    value = value.reshape(CHUNK, SIDE, 128)
    place = pl.ds(pl.multiple_of(c * (CHUNK * 8), CHUNK * 8), CHUNK * 8)
    edge_ref[0, place, :] = value[:, :8].reshape(CHUNK * 8, 128)
    edge_ref[1, place, :] = value[:, SIDE - 8 :].reshape(CHUNK * 8, 128)


def edge_row(edge_ref, side, depth):
    return edge_ref[side, pl.ds(depth if side == 0 else 7 - depth, PAIRS, stride=8), :]


def write_strips(x_ref, edge_ref, strip_ref):
    top = swap(edge_row(edge_ref, 0, 0), edge_row(edge_ref, 0, 1))
    bottom = swap(edge_row(edge_ref, 1, 0), edge_row(edge_ref, 1, 1))
    strip_ref[0:64] = jnp.concatenate(top, 0).astype(BF16)
    strip_ref[64:128] = x_ref[1]
    strip_ref[128:192] = jnp.concatenate(bottom, 0).astype(BF16)
    strip_ref[192:256] = half_turn(x_ref[PAIRS].astype(F32)).astype(BF16)


def write_thin_strips(x_ref, edge_ref, strip_ref):
    strip_ref[0:64] = jnp.concatenate(swap(edge_row(edge_ref, 0, 0), edge_row(edge_ref, 1, 0)), 0).astype(BF16)
    first, last = x_ref[1].astype(F32), x_ref[PAIRS].astype(F32)
    strip_ref[64:128] = jnp.where(low_half(first), first, last).astype(BF16)


def fill_select(here, devices, nbr_ref, turn_ref, corner_ref, select, thin):
    def slot_of(j):
        return lax.rem(nbr_ref[0, j] - here + REACH + devices, devices)

    def columns_of(p, edge, quarter, flips):
        source = lax.rem(edge + 4 - quarter, 4)
        flip = jnp.where(quarter == flips[0], 1, jnp.where(quarter == flips[1], 1, 0))
        p = p + flip * (63 - 2 * p)
        split = (p % 2) * 32 + p // 2
        place = split + lax.rem(source, 2) * (p - split)
        return source * 64 + place, lax.rem(source, 2) * 64 + place

    lane = lax.broadcasted_iota(jnp.int32, (SIDE, STRIP), 1)
    row = lax.broadcasted_iota(jnp.int32, (SIDE, STRIP), 0)
    for n, (j, edge) in enumerate(EDGE_DIRS):
        if edge % 2 == 0:
            cols, thin_cols = columns_of(row % 32 * 2 + row // 32, edge, turn_ref[0, j], (2, 3))
        else:
            cols, thin_cols = columns_of(row, edge, turn_ref[0, j], (1, 2))
        hit = jnp.where(lane == cols, 1.0, 0.0)
        thin_hit = jnp.where(lane == thin_cols, 1.0, 0.0)[:, :128]
        slot = slot_of(j)
        for k in range(SLOTS):
            here_it_is = jnp.where(slot == k, 1.0, 0.0)
            select[k, n * 64 : (n + 1) * 64] = (hit * here_it_is).astype(BF16)
            thin[k, n * 64 : (n + 1) * 64] = (thin_hit * here_it_is).astype(BF16)
    lane = lane[:8]
    row = row[:8]
    hits = []
    for j, edge, last in CORNER_DIRS:
        cols, thin_cols = columns_of(63 - row if last else row, edge, turn_ref[0, j], (2, 3))
        keep = jnp.where(row < 2, 1.0, 0.0) * corner_ref[0, j // 2].astype(F32)
        hit = jnp.where(lane == cols, 1.0, 0.0) * keep
        thin_hit = (jnp.where(lane == thin_cols, 1.0, 0.0) * keep)[:, :128]
        hits.append((hit, thin_hit, slot_of(j)))
    for k in range(SLOTS):
        parts = [hit * jnp.where(slot == k, 1.0, 0.0) for hit, unused, slot in hits]
        select[k, 256:288] = jnp.concatenate(parts, 0).astype(BF16)
        parts = [hit * jnp.where(slot == k, 1.0, 0.0) for unused, hit, slot in hits]
        thin[k, 256:288] = jnp.concatenate(parts, 0).astype(BF16)


def exchange_halves(rims, turn_ref):
    parts = []
    places = [(j, edge, 64) for j, edge in EDGE_DIRS] + [(j, edge, 8) for j, edge, unused in CORNER_DIRS]
    start = 0
    for j, edge, count in places:
        block = rims[start : start + count]
        high = (lax.rem(edge + 4 - turn_ref[0, j], 4) // 2).astype(F32)
        parts.append(block * (1.0 - high) + half_turn(block) * high)
        start += count
    return jnp.concatenate(parts, 0)


def place_rims(rims, x_ref, rows_ref):
    north, east, south, west = (rims[64 * n : 64 * n + 64] for n in range(4))
    x_ref[PAIRS + 1] = east.astype(BF16)
    x_ref[0] = half_turn(west).astype(BF16)
    ne, se, sw, nw = (rims[256 + 8 * n : 264 + 8 * n] for n in range(4))
    for base, strip, right, left in ((0, north, ne, nw), (2, south, se, sw)):
        inner = swap(strip[:32], strip[32:])
        ends = swap(right[0:1], right[1:2])
        starts = swap(left[1:2], left[0:1])
        for d in range(2):
            rows_ref[base + d, 8:40, :] = inner[d]
            rows_ref[base + d, 40:41, :] = ends[d]
            rows_ref[base + d, 7:8, :] = starts[d]


def strips_beside(rows_ref):
    parts = []
    for k in range(4):
        parts.append(jnp.concatenate([rows_ref[k, 7 + d : 39 + d, :] for d in range(3)], 1))
    return jnp.concatenate(parts, 0).astype(BF16)


def add_rims(x_ref, beside, big, z_ref, dilation):
    west = combine(dot(x_ref[0], big[0:128, :]), dilation, False)
    z_ref[0:64, :] += west
    east = combine(dot(x_ref[PAIRS + 1], big[256:384, :]), dilation, False)
    z_ref[ROWS - 64 : ROWS, :] += east
    north = dot(beside[:64], big[:, 0:128])
    south = dot(beside[64:], big[:, 256:384])
    for d in range(dilation):
        z_ref[pl.ds(dilation - 1 - d, PAIRS, stride=SIDE), :] += north[32 * d : 32 * d + 32]
        z_ref[pl.ds(SIDE - dilation + d, PAIRS, stride=SIDE), :] += south[32 * d : 32 * d + 32]


def transposed(g_ref, big, z_ref, dilation):
    def body(c):
        product = dot(neighbouring(g_ref, c * CHUNK, CHUNK), big[...])
        z_ref[chunk_rows(c), :] = combine(product, dilation, True)

    chunks(body)


def leaving_rims(g_ref, edge_ref, rows_ref, big, dilation):
    before = combine(dot(g_ref[1], big[256:384, :]), dilation, True)
    after = combine(dot(g_ref[PAIRS], big[0:128, :]), dilation, True)
    strips, corners = [], []
    gap = jnp.zeros((6, 128), F32)
    for side in range(2):
        lines = []
        for d in range(2):
            if d < dilation:
                rows_ref[2 * side + d, 8:40, :] = edge_row(edge_ref, side, dilation - 1 - d)
                near = [rows_ref[2 * side + d, 6 + k : 46 + k, :] for k in range(3)]
                near = jnp.concatenate(near, 1).astype(BF16)
                lines.append(dot(near, big[:, 256 * side : 256 * side + 128]))
            else:
                lines.append(jnp.zeros((40, 128), F32))
        strips.append(jnp.concatenate(swap(lines[0][1:33], lines[1][1:33]), 0))
        first, second = swap(lines[0][33:34], lines[1][33:34])
        right = jnp.concatenate([first, second, gap], 0)
        second, first = swap(lines[0][0:1], lines[1][0:1])
        left = jnp.concatenate([first, second, gap], 0)
        corners.append((right, left))
    order = [strips[0], after, strips[1], half_turn(before)]
    order += [corners[0][0], corners[1][0], corners[1][1], corners[0][1]]
    return jnp.concatenate(order, 0)


def add_returned(strips, z_ref, dilation):
    z_ref[0:64, :] += strips[64:128]
    z_ref[ROWS - 64 : ROWS, :] += half_turn(strips[192:256])
    top = swap(strips[0:32], strips[32:64])
    bottom = swap(strips[128:160], strips[160:192])
    for d in range(dilation):
        z_ref[pl.ds(d, PAIRS, stride=SIDE), :] += top[d]
        z_ref[pl.ds(SIDE - 1 - d, PAIRS, stride=SIDE), :] += bottom[d]


def add_thin_returned(strips, z_ref):
    top, bottom = swap(strips[0:32], strips[32:64])
    z_ref[pl.ds(0, PAIRS, stride=SIDE), :] += top
    z_ref[pl.ds(SIDE - 1, PAIRS, stride=SIDE), :] += bottom
    sides = strips[64:128]
    low = low_half(sides)
    z_ref[0:64, :] += jnp.where(low, sides, 0.0)
    z_ref[ROWS - 64 : ROWS, :] += jnp.where(low, 0.0, sides)


def write_gradient(c, g, dilation, g_ref, shifted, edge_ref):
    rows = CHUNK * SIDE
    g_ref[pl.ds(c * CHUNK + 1, CHUNK)] = g.astype(BF16).reshape(CHUNK, SIDE, 128)
    i = lax.broadcasted_iota(jnp.int32, (rows, 128), 0) % SIDE
    up = jnp.where(i < SIDE - dilation, pltpu.roll(g, rows - dilation, axis=0), 0.0)
    down = jnp.where(i >= dilation, pltpu.roll(g, dilation, axis=0), 0.0)
    shifted[chunk_rows(c), 0:128] = up.astype(BF16)
    shifted[chunk_rows(c), 128:256] = g.astype(BF16)
    shifted[chunk_rows(c), 256:384] = down.astype(BF16)
    keep_edges(edge_ref, c, g)


def weight_gradient(x_ref, shifted, beside, edge_ref, raw, flat, dilation):
    strip_grads = []
    zero = jnp.zeros((PAIRS, 128), F32)
    for side in range(2):
        for d in range(2):
            if d >= dilation:
                part = jnp.zeros((PAIRS, 384), F32)
            else:
                row = edge_row(edge_ref, side, dilation - 1 - d)
                part = jnp.concatenate([row, zero, zero] if side == 0 else [zero, zero, row], 1)
            strip_grads.append(part)
    strip_grads = jnp.concatenate(strip_grads, 0).astype(BF16)
    for k in range(3):
        total = dot_rows(x_ref[k : k + PAIRS].reshape(ROWS, 128), shifted[...])
        raw[k] = total + dot_rows(beside[:, 128 * k : 128 * k + 128], strip_grads)
    taps = []
    for a in range(3):
        lanes = slice(128 * a, 128 * a + 128)
        upper = [raw[k, 0:64, lanes] for k in range(3)]
        lower = [raw[k, 64:128, lanes] for k in range(3)]
        if dilation == 2:
            taps += [upper[k] + half_turn(lower[k]) for k in range(3)]
        else:
            taps.append(half_turn(upper[1]) + lower[0])
            taps.append(upper[1] + half_turn(lower[1]))
            taps.append(lower[1] + half_turn(upper[2]))
    low = low_half(taps[0])
    for t in range(0, 8, 2):
        flat[32 * t : 32 * t + 64, :] = jnp.where(low, taps[t], half_turn(taps[t + 1]))
    flat[256:288, :] = jnp.where(low[:32], taps[8][:32], half_turn(taps[8][32:]))


def write_taps(total_ref, flat, out_ref):
    for n in range(2 * PLANE):
        flat[SHARE * n : SHARE * n + SHARE, :] = total_ref[n]
    for t in range(8):
        block = flat[t // 2 * 64 : t // 2 * 64 + 64, :]
        if t % 2 == 1:
            block = half_turn(block)
        out_ref[t] = block[:, :CHANS]
    last = flat[256:288, :]
    out_ref[8] = jnp.concatenate([last, half_turn(last)], 0)[:, :CHANS]


class Ring:
    def __init__(self, here, devices, source, target, send, recv):
        self.here, self.devices = here, devices
        self.source, self.target, self.send, self.recv = source, target, send, recv

    def copy(self, offset):
        return pltpu.make_async_remote_copy(
            src_ref=self.source(offset),
            dst_ref=self.target.at[REACH - offset],
            send_sem=self.send.at[REACH + offset],
            recv_sem=self.recv.at[REACH - offset],
            device_id=(lax.rem(self.here + offset + self.devices, self.devices),),
            device_id_type=MESH,
        )

    def start(self, offset):
        self.copy(offset).start()

    def arrived(self, slot):
        there = self.target.at[slot]
        pltpu.make_async_copy(there, there, self.recv.at[slot]).wait()

    def finish(self):
        for offset in FAR_FIRST:
            self.copy(offset).wait_send()


class Reduction:
    def __init__(self, here, src, other, half, plane, level, out, sems, core_sems):
        self.here, self.src, self.other, self.half = here, src, other, half
        self.plane, self.level, self.out = plane, level, out
        self.sems, self.core_sems = sems, core_sems
        self.core = here % 2
        self.me = here // 2 % PLANE
        self.floor = here // 32

    def core_copy(self, src, dst, step):
        return pltpu.make_async_remote_copy(
            src_ref=src, dst_ref=dst,
            send_sem=self.core_sems.at[step, 0], recv_sem=self.core_sems.at[step, 1],
            device_id=(self.here + 1 - 2 * self.core,), device_id_type=MESH,
        )

    def halving(self):
        return self.core_copy(self.src.at[pl.ds((1 - self.core) * PLANE, PLANE)], self.other, 0)

    def joining(self):
        mine = self.out.at[pl.ds(self.core * PLANE, PLANE)]
        return self.core_copy(mine, mine, 1)

    def scatter_copy(self, k):
        peer = (self.me + k) % PLANE
        return pltpu.make_async_remote_copy(
            src_ref=self.half.at[peer], dst_ref=self.plane.at[self.me],
            send_sem=self.sems.at[0, peer], recv_sem=self.sems.at[1, self.me],
            device_id=(plane_peer(self.here, peer),), device_id_type=MESH,
        )

    def level_copy(self, k):
        peer = (self.floor + k) % LEVELS
        return pltpu.make_async_remote_copy(
            src_ref=self.level.at[self.floor], dst_ref=self.level.at[self.floor],
            send_sem=self.sems.at[2, peer], recv_sem=self.sems.at[3, self.floor],
            device_id=(level_peer(self.here, peer),), device_id_type=MESH,
        )

    def gather_copy(self, k):
        peer = (self.me + k) % PLANE
        mine = self.out.at[self.core * PLANE + self.me]
        return pltpu.make_async_remote_copy(
            src_ref=mine, dst_ref=mine,
            send_sem=self.sems.at[4, peer], recv_sem=self.sems.at[5, self.me],
            device_id=(plane_peer(self.here, peer),), device_id_type=MESH,
        )

    def each(self, count, act):
        def body(k, unused):
            act(k)
            return unused

        lax.fori_loop(1, count, body, 0)

    def arrivals(self, count, buffer, row, mine, base):
        def one(k):
            peer = (mine + k) % count
            there = buffer.at[base + peer]
            pltpu.make_async_copy(there, there, self.sems.at[row, peer]).wait()

        self.each(count, one)

    def start(self, flat):
        for n in range(2 * PLANE):
            self.src[n] = flat[SHARE * n : SHARE * n + SHARE, :]
        self.halving().start()

    def scatter(self):
        self.halving().wait_recv()
        self.half[...] = self.src[pl.ds(self.core * PLANE, PLANE)] + self.other[...]
        self.each(PLANE, lambda k: self.scatter_copy(k).start())
        self.plane[self.me] = self.half[self.me]

    def across(self):
        self.arrivals(PLANE, self.plane, 1, self.me, 0)
        self.level[self.floor] = jnp.sum(self.plane[...], axis=0)
        self.each(LEVELS, lambda k: self.level_copy(k).start())

    def gather(self):
        self.arrivals(LEVELS, self.level, 3, self.floor, 0)
        self.out[self.core * PLANE + self.me] = jnp.sum(self.level[...], axis=0)
        self.each(PLANE, lambda k: self.gather_copy(k).start())

    def join(self):
        self.arrivals(PLANE, self.out, 5, self.me, self.core * PLANE)
        self.joining().start()

    def joined(self):
        theirs = self.out.at[pl.ds((1 - self.core) * PLANE, PLANE)]
        pltpu.make_async_copy(theirs, theirs, self.core_sems.at[1, 1]).wait()

    def sent(self):
        self.halving().wait_send()
        self.joining().wait_send()
        self.each(PLANE, lambda k: self.scatter_copy(k).wait_send())
        self.each(LEVELS, lambda k: self.level_copy(k).wait_send())
        self.each(PLANE, lambda k: self.gather_copy(k).wait_send())


def level_kernel(
    devices,
    f_hbm, w1_hbm, w2_hbm, cot_hbm, nbr_hbm, turn_hbm, corner_hbm,
    pooled_hbm, gin_hbm, dw1_hbm, dw2_hbm,
    f_ref, w1_ref, w2_ref, cot_ref, nbr_ref, turn_ref, corner_ref,
    pooled_ref, gin_ref, dw1_ref, dw2_ref,
    x1, x2, g_ref, shifted, z_ref, d_ref, act_ref, edge_ref, rows1, rows2, leave, raw, flat,
    big1, big1t, big2, big2t, select, thin,
    pool1, pool2, out2, back2, out1, back1,
    src2, other2, half2, plane2, level2, total2,
    src1, other1, half1, plane1, level1, total1,
    load_sems, store_sems, ring_sems, sems2, sems1, core_sems2, core_sems1,
):
    here = lax.axis_index("tiles")
    loads = (
        (f_hbm, f_ref), (nbr_hbm, nbr_ref), (turn_hbm, turn_ref), (corner_hbm, corner_ref),
        (w1_hbm, w1_ref), (w2_hbm, w2_ref), (cot_hbm, cot_ref),
    )
    loads = [pltpu.make_async_copy(a, b, load_sems.at[n]) for n, (a, b) in enumerate(loads)]
    for load in loads:
        load.start()
    stores = ((pooled_ref, pooled_hbm), (gin_ref, gin_hbm), (dw1_ref, dw1_hbm), (dw2_ref, dw2_hbm))
    stores = [pltpu.make_async_copy(a, b, store_sems.at[n]) for n, (a, b) in enumerate(stores)]
    barrier = pltpu.get_barrier_semaphore()

    def greet(device):
        pl.semaphore_signal(barrier, inc=1, device_id=(device,), device_id_type=MESH)

    for offset in FAR_FIRST:
        greet(lax.rem(here + offset + devices, devices))

    def greet_plane(k, unused):
        greet(plane_peer(here, (here // 2 + k) % PLANE))
        return unused

    def greet_level(k, unused):
        greet(level_peer(here, (here // 32 + k) % LEVELS))
        return unused

    lax.fori_loop(1, PLANE, greet_plane, 0)
    lax.fori_loop(1, LEVELS, greet_level, 0)

    ring1 = Ring(here, devices, lambda o: pool1.at[REACH], pool1, ring_sems.at[0], ring_sems.at[1])
    ring2 = Ring(here, devices, lambda o: pool2.at[REACH], pool2, ring_sems.at[2], ring_sems.at[3])
    ring3 = Ring(here, devices, lambda o: out2.at[REACH + o], back2, ring_sems.at[4], ring_sems.at[5])
    ring4 = Ring(here, devices, lambda o: out1.at[REACH + o], back1, ring_sems.at[6], ring_sems.at[7])
    sum2 = Reduction(here, src2, other2, half2, plane2, level2, total2, sems2, core_sems2)
    sum1 = Reduction(here, src1, other1, half1, plane1, level1, total1, sems1, core_sems1)

    def collect(ring, pool, chosen):
        rims = dot(chosen[REACH], pool[REACH])
        for offset in NEAR_FIRST:
            slot = REACH - offset
            ring.arrived(slot)
            rims = rims + dot(chosen[slot], pool[slot])
        return rims

    def send_back(ring, out_ref, rims, chosen):
        rims = rims.astype(BF16)
        for offset in FAR_FIRST:
            out_ref[REACH + offset] = dot_rows(chosen[REACH + offset], rims).astype(BF16)
            ring.start(offset)
        return dot_rows(chosen[REACH], rims)

    def take_back(ring, back_ref, own):
        for offset in NEAR_FIRST:
            ring.arrived(REACH - offset)
            own = own + back_ref[REACH - offset].astype(F32)
        return own

    empty = jnp.zeros((SIDE, 128), BF16)
    for x in (x1, x2, g_ref):
        x[0] = empty
        x[PAIRS + 1] = empty
    leave[...] = jnp.zeros_like(leave)
    loads[0].wait()
    for jp in range(PAIRS):
        x1[jp + 1] = f_ref[:, 128 * jp : 128 * jp + 128]
    for jp in range(PAIRS):
        edge_ref[0, 8 * jp : 8 * jp + 8, :] = f_ref[0:16, 128 * jp : 128 * jp + 128].astype(F32)[:8]
        edge_ref[1, 8 * jp : 8 * jp + 8, :] = f_ref[48:64, 128 * jp : 128 * jp + 128].astype(F32)[8:]
    write_thin_strips(x1, edge_ref, pool1.at[REACH])
    pl.semaphore_wait(barrier, 2 * REACH + PLANE - 1 + LEVELS - 1)
    for offset in FAR_FIRST:
        ring1.start(offset)

    for load in loads[1:]:
        load.wait()
    fill_weights(w1_ref, 1, False, big1)
    convolve(x1, big1, z_ref, 1)
    fill_select(here, devices, nbr_ref, turn_ref, corner_ref, select, thin)
    fill_weights(w2_ref, 2, False, big2)
    fill_weights(w2_ref, 2, True, big2t)
    fill_weights(w1_ref, 1, True, big1t)
    low = lax.broadcasted_iota(jnp.int32, (PAIRS, 128), 1) < 64
    for t in range(PAIRS // 2):
        both = cot_ref[:, 128 * t : 128 * t + 128].astype(F32) * 0.25
        turned = half_turn(both)
        for jp, value in ((2 * t, jnp.where(low, both, turned)), (2 * t + 1, jnp.where(low, turned, both))):
            act_ref[pl.ds(SIDE * jp, PAIRS, stride=2), :] = value
            act_ref[pl.ds(SIDE * jp + 1, PAIRS, stride=2), :] = value
    place_rims(exchange_halves(collect(ring1, pool1, thin), turn_ref), x1, rows1)
    beside1 = strips_beside(rows1)
    add_rims(x1, beside1, big1, z_ref, 1)

    def activate(c):
        z = z_ref[chunk_rows(c), :]
        s = sigmoid(z)
        y = z * s
        d_ref[chunk_rows(c), :] = s * (1.0 + z * (1.0 - s))
        x2[pl.ds(c * CHUNK + 1, CHUNK)] = y.astype(BF16).reshape(CHUNK, SIDE, 128)
        keep_edges(edge_ref, c, y)

    chunks(activate)
    write_strips(x2, edge_ref, pool2.at[REACH])
    for offset in FAR_FIRST:
        ring2.start(offset)

    convolve(x2, big2, z_ref, 2)
    place_rims(collect(ring2, pool2, select), x2, rows2)
    beside2 = strips_beside(rows2)
    add_rims(x2, beside2, big2, z_ref, 2)

    def second(c):
        z = z_ref[chunk_rows(c), :]
        s = sigmoid(z)
        z_ref[chunk_rows(c), :] = z * s * 0.25
        g = act_ref[chunk_rows(c), :] * s * (1.0 + z * (1.0 - s))
        write_gradient(c, g.astype(BF16).astype(F32), 2, g_ref, shifted, edge_ref)

    chunks(second)

    own = send_back(ring3, out2, leaving_rims(g_ref, edge_ref, leave, big2t, 2), select)
    weight_gradient(x2, shifted, beside2, edge_ref, raw, flat, 2)
    sum2.start(flat)
    for t in range(PAIRS // 2):
        sums = []
        for jp in (2 * t, 2 * t + 1):
            v = z_ref[pl.ds(SIDE * jp, PAIRS, stride=2), :] + z_ref[pl.ds(SIDE * jp + 1, PAIRS, stride=2), :]
            sums.append(v + half_turn(v))
        pooled_ref[:, 128 * t : 128 * t + 128] = jnp.where(low, sums[0], sums[1]).astype(BF16)
    stores[0].start()
    transposed(g_ref, big2t, z_ref, 2)
    sum2.scatter()
    add_returned(take_back(ring3, back2, own), z_ref, 2)

    def first(c):
        g = z_ref[chunk_rows(c), :] * d_ref[chunk_rows(c), :]
        write_gradient(c, g.astype(BF16).astype(F32), 1, g_ref, shifted, edge_ref)

    chunks(first)

    weight_gradient(x1, shifted, beside1, edge_ref, raw, flat, 1)
    sum1.start(flat)
    rims = exchange_halves(leaving_rims(g_ref, edge_ref, leave, big1t, 1), turn_ref)
    sum1.scatter()
    own = send_back(ring4, out1, rims, thin)
    sum2.across()
    transposed(g_ref, big1t, z_ref, 1)
    sum1.across()
    sum2.gather()
    add_thin_returned(take_back(ring4, back1, own), z_ref)
    for jp in range(PAIRS):
        gin_ref[:, 128 * jp : 128 * jp + 128] = z_ref[SIDE * jp : SIDE * jp + SIDE, :].astype(BF16)
    stores[1].start()
    sum1.gather()
    sum2.join()
    for ring in (ring1, ring2, ring3, ring4):
        ring.finish()
    sum2.joined()
    write_taps(total2, flat, dw2_ref)
    stores[3].start()
    sum2.sent()
    sum1.join()
    sum1.joined()
    write_taps(total1, flat, dw1_ref)
    stores[2].start()
    sum1.sent()
    for store in stores:
        store.wait()


def finish_kernel(*refs):
    ins, outs, held, (load_sems, store_sems) = refs[:4], refs[4:8], refs[8:12], refs[12:]
    loads = [pltpu.make_async_copy(ins[n], held[n], load_sems.at[n]) for n in range(4)]
    stores = [pltpu.make_async_copy(held[n], outs[n], store_sems.at[n]) for n in range(4)]
    for load in loads:
        load.start()
    for load, store in zip(loads, stores):
        load.wait()
        store.start()
    for store in stores:
        store.wait()


def local(features, weights_first, weights_second, cotangent, neighbours, turns, corners):
    devices = lax.axis_size("tiles")
    anywhere = pl.BlockSpec(memory_space=pl.ANY)
    inputs = (features[0], weights_first, weights_second, cotangent[0], neighbours, turns, corners)
    outputs = (
        jax.ShapeDtypeStruct((PAIRS, PAIRS * CHANS), BF16),
        jax.ShapeDtypeStruct((SIDE, SIDE * CHANS), BF16),
        jax.ShapeDtypeStruct((9, CHANS, CHANS), F32),
        jax.ShapeDtypeStruct((9, CHANS, CHANS), F32),
    )
    slabs = pltpu.VMEM((PAIRS + 2, SIDE, 128), BF16)
    field = pltpu.VMEM((ROWS, 128), F32)
    big = pltpu.VMEM((384, 384), BF16)
    pool = pltpu.VMEM((SLOTS, STRIP, 128), BF16)
    thin_pool = pltpu.VMEM((SLOTS, 128, 128), BF16)
    rows = pltpu.VMEM((4, 48, 128), F32)

    def shares(count):
        return pltpu.VMEM((count, SHARE, 128), F32)

    reduction = [shares(n) for n in (2 * PLANE, PLANE, PLANE, PLANE, LEVELS, 2 * PLANE)]
    results = pl.pallas_call(
        functools.partial(level_kernel, devices),
        out_shape=outputs,
        in_specs=[pl.BlockSpec(memory_space=pltpu.HBM)] * 7,
        out_specs=[anywhere] * 4,
        scratch_shapes=[pltpu.VMEM(x.shape, x.dtype) for x in inputs[:4]]
        + [pltpu.SMEM(x.shape, x.dtype) for x in inputs[4:]]
        + [pltpu.VMEM(x.shape, x.dtype) for x in outputs]
        + [
            slabs, slabs, slabs,
            pltpu.VMEM((ROWS, 384), BF16),
            field, field, field,
            pltpu.VMEM((2, 8 * PAIRS, 128), F32),
            rows, rows, rows,
            pltpu.VMEM((3, 128, 384), F32),
            pltpu.VMEM((2 * PLANE * SHARE, 128), F32),
            big, big, big, big,
            pltpu.VMEM((SLOTS, RIMS, STRIP), BF16),
            pltpu.VMEM((SLOTS, RIMS, 128), BF16),
            thin_pool, pool, pool, pool, thin_pool, thin_pool,
        ]
        + reduction
        + reduction
        + [
            pltpu.SemaphoreType.DMA((7,)),
            pltpu.SemaphoreType.DMA((4,)),
            pltpu.SemaphoreType.DMA((8, SLOTS)),
            pltpu.SemaphoreType.DMA((6, PLANE)),
            pltpu.SemaphoreType.DMA((6, PLANE)),
            pltpu.SemaphoreType.DMA((2, 2)),
            pltpu.SemaphoreType.DMA((2, 2)),
        ],
        compiler_params=pltpu.CompilerParams(
            collective_id=0, has_side_effects=True, vmem_limit_bytes=60 * 2**20
        ),
        name="level",
    )(*inputs)
    pooled, grad, first, second = pl.pallas_call(
        finish_kernel,
        out_shape=outputs,
        in_specs=[anywhere] * 4,
        out_specs=[anywhere] * 4,
        scratch_shapes=[pltpu.VMEM(x.shape, x.dtype) for x in outputs]
        + [pltpu.SemaphoreType.DMA((4,))] * 2,
        compiler_params=pltpu.CompilerParams(vmem_limit_bytes=60 * 2**20),
        name="finish",
    )(*results)
    return pooled[None], grad[None], first, second


def solution(mesh):
    return jax.shard_map(
        local,
        mesh=mesh,
        in_specs=(
            P("tiles", None, None),
            P(),
            P(),
            P("tiles", None, None),
            P("tiles", None),
            P("tiles", None),
            P("tiles", None),
        ),
        out_specs=(P("tiles", None, None), P("tiles", None, None), P(), P()),
        check_vma=False,
    )
```

```python
import functools

import jax
import jax.numpy as jnp
from jax import lax
from jax.experimental import pallas as pl
from jax.experimental.pallas import tpu as pltpu
from jax.sharding import PartitionSpec as P

REACH = 3
SLOTS = 2 * REACH + 1
SIDE = 64
CHANS = 64
PAIRS = SIDE // 2
ROWS = PAIRS * SIDE
STRIP = 4 * SIDE
PLANE = 32
LEVELS = 8
SHARE = 9
CHUNK = 8
RIMS = 4 * SIDE + 32
MESH = pl.DeviceIdType.MESH
BF16 = jnp.bfloat16
F32 = jnp.float32
EDGE_DIRS = ((0, 2), (2, 1), (4, 0), (6, 3))
CORNER_DIRS = ((1, 2, False), (3, 0, False), (5, 0, True), (7, 2, True))
OFFSETS = (1, -1, 2, -2, 3, -3)


def dot(a, b):
    return jnp.dot(a, b, preferred_element_type=F32)


def dot_rows(a, b):
    return lax.dot_general(a, b, (((0,), (0,)), ((), ())), preferred_element_type=F32)


def half_turn(x):
    return pltpu.roll(x, 64, axis=1)


def low_half(x):
    return lax.broadcasted_iota(jnp.int32, x.shape, 1) < 64


def swap(x, y):
    low = low_half(x)
    return jnp.where(low, x, half_turn(y)), jnp.where(low, half_turn(x), y)


def sigmoid(z):
    return 1.0 / (1.0 + jnp.exp(-z))


def hops(steps, size):
    return min(steps, size - steps)


PLANE_STEPS = sorted(
    ((x, y, core) for x in range(4) for y in range(4) for core in range(2) if x or y or core),
    key=lambda step: -(hops(step[0], 4) + hops(step[1], 4)),
)
LEVEL_STEPS = sorted(range(1, LEVELS), key=lambda step: -hops(step, LEVELS))


def plane_members(here):
    x, y, core = here // 8 % 4, here // 2 % 4, here % 2
    xs = [8 * ((x + step) % 4) for step in range(4)]
    ys = [2 * ((y + step) % 4) for step in range(4)]
    cores = [core, 1 - core]
    return [xs[a] + ys[b] + cores[c] for a, b, c in PLANE_STEPS]


def level_members(here):
    return [(here // PLANE + step) % LEVELS for step in LEVEL_STEPS]


def blocks_of(w_ref, dilation, turned):
    taps = [w_ref[t].astype(F32) for t in range(9)]
    if turned:
        taps = [jnp.transpose(tap) for tap in taps]
    zero = jnp.zeros((CHANS, CHANS), F32)
    result = {}
    for a in range(3):
        left, mid, right = taps[3 * a : 3 * a + 3]
        if dilation == 2:
            quads = {d: (w, zero, zero, w) for d, w in ((-1, left), (0, mid), (1, right))}
        else:
            quads = {-1: (zero, zero, left, zero), 0: (mid, left, right, mid), 1: (zero, right, zero, zero)}
        for d, (q00, q01, q10, q11) in quads.items():
            if turned:
                q01, q10 = q10, q01
                d = -d
            block = jnp.concatenate(
                [jnp.concatenate([q00, q01], 1), jnp.concatenate([q10, q11], 1)], 0
            )
            result[a, d] = block.astype(BF16)
    return result


def fill_weights(w_ref, dilation, turned, big):
    for (a, d), block in blocks_of(w_ref, dilation, turned).items():
        big[(d + 1) * 128 : (d + 2) * 128, a * 128 : (a + 1) * 128] = block


def combine(product, dilation, turned):
    rows = product.shape[0]
    up, mid, down = product[:, :128], product[:, 128:256], product[:, 256:]
    if turned:
        up, down = down, up
    i = lax.broadcasted_iota(jnp.int32, (rows, 128), 0) % SIDE
    up = jnp.where(i >= dilation, pltpu.roll(up, dilation, axis=0), 0.0)
    down = jnp.where(i < SIDE - dilation, pltpu.roll(down, rows - dilation, axis=0), 0.0)
    return mid + up + down


def neighbouring(x_ref, start, count):
    parts = [x_ref[pl.ds(start + k, count)].reshape(count * SIDE, 128) for k in range(3)]
    return jnp.concatenate(parts, 1)


def chunks(body):
    def step(c, unused):
        body(c)
        return unused

    lax.fori_loop(0, PAIRS // CHUNK, step, 0)


def chunk_rows(c):
    return pl.ds(pl.multiple_of(c * (CHUNK * SIDE), CHUNK * SIDE), CHUNK * SIDE)


def convolve(x_ref, big, z_ref, dilation):
    def body(c):
        product = dot(neighbouring(x_ref, c * CHUNK, CHUNK), big[...])
        z_ref[chunk_rows(c), :] = combine(product, dilation, False)

    chunks(body)


def edge_row(edge_ref, side, depth):
    return edge_ref[side, pl.ds(depth if side == 0 else 7 - depth, PAIRS, stride=8), :]


def border_of(make):
    rows = {}
    for depth in range(2):
        rows[0, depth] = make(pl.ds(depth, PAIRS, stride=SIDE))
        rows[1, depth] = make(pl.ds(SIDE - 1 - depth, PAIRS, stride=SIDE))
    return rows, make(slice(0, SIDE)), make(slice(ROWS - SIDE, ROWS))


def write_strips(border, strip_ref):
    rows, first, last = border
    strip_ref[0:64] = jnp.concatenate(swap(rows[0, 0], rows[0, 1]), 0).astype(BF16)
    strip_ref[64:128] = first.astype(BF16)
    strip_ref[128:192] = jnp.concatenate(swap(rows[1, 0], rows[1, 1]), 0).astype(BF16)
    strip_ref[192:256] = half_turn(last).astype(BF16)


def write_thin_strips(x_ref, edge_ref, strip_ref):
    strip_ref[0:64] = jnp.concatenate(swap(edge_row(edge_ref, 0, 0), edge_row(edge_ref, 1, 0)), 0).astype(BF16)
    first, last = x_ref[1].astype(F32), x_ref[PAIRS].astype(F32)
    strip_ref[64:128] = jnp.where(low_half(first), first, last).astype(BF16)


def fill_select(here, devices, nbr_ref, turn_ref, corner_ref, select, thin):
    def slot_of(j):
        return lax.rem(nbr_ref[0, j] - here + REACH + devices, devices)

    def columns_of(p, edge, quarter, flips):
        source = lax.rem(edge + 4 - quarter, 4)
        flip = jnp.where(quarter == flips[0], 1, jnp.where(quarter == flips[1], 1, 0))
        p = p + flip * (63 - 2 * p)
        split = (p % 2) * 32 + p // 2
        place = split + lax.rem(source, 2) * (p - split)
        return source * 64 + place, lax.rem(source, 2) * 64 + place

    lane = lax.broadcasted_iota(jnp.int32, (SIDE, STRIP), 1)
    row = lax.broadcasted_iota(jnp.int32, (SIDE, STRIP), 0)
    for n, (j, edge) in enumerate(EDGE_DIRS):
        if edge % 2 == 0:
            cols, thin_cols = columns_of(row % 32 * 2 + row // 32, edge, turn_ref[0, j], (2, 3))
        else:
            cols, thin_cols = columns_of(row, edge, turn_ref[0, j], (1, 2))
        hit = jnp.where(lane == cols, 1.0, 0.0)
        thin_hit = jnp.where(lane == thin_cols, 1.0, 0.0)[:, :128]
        slot = slot_of(j)
        for k in range(SLOTS):
            here_it_is = jnp.where(slot == k, 1.0, 0.0)
            select[k, n * 64 : (n + 1) * 64] = (hit * here_it_is).astype(BF16)
            thin[k, n * 64 : (n + 1) * 64] = (thin_hit * here_it_is).astype(BF16)
    lane = lane[:8]
    row = row[:8]
    hits = []
    for j, edge, last in CORNER_DIRS:
        cols, thin_cols = columns_of(63 - row if last else row, edge, turn_ref[0, j], (2, 3))
        keep = jnp.where(row < 2, 1.0, 0.0) * corner_ref[0, j // 2].astype(F32)
        hit = jnp.where(lane == cols, 1.0, 0.0) * keep
        thin_hit = (jnp.where(lane == thin_cols, 1.0, 0.0) * keep)[:, :128]
        hits.append((hit, thin_hit, slot_of(j)))
    for k in range(SLOTS):
        parts = [hit * jnp.where(slot == k, 1.0, 0.0) for hit, unused, slot in hits]
        select[k, 256:288] = jnp.concatenate(parts, 0).astype(BF16)
        parts = [hit * jnp.where(slot == k, 1.0, 0.0) for unused, hit, slot in hits]
        thin[k, 256:288] = jnp.concatenate(parts, 0).astype(BF16)


def exchange_halves(rims, turn_ref):
    parts = []
    places = [(j, edge, 64) for j, edge in EDGE_DIRS] + [(j, edge, 8) for j, edge, unused in CORNER_DIRS]
    start = 0
    for j, edge, count in places:
        block = rims[start : start + count]
        high = (lax.rem(edge + 4 - turn_ref[0, j], 4) // 2).astype(F32)
        parts.append(block * (1.0 - high) + half_turn(block) * high)
        start += count
    return jnp.concatenate(parts, 0)


def place_rims(rims, x_ref, rows_ref):
    north, east, south, west = (rims[64 * n : 64 * n + 64] for n in range(4))
    x_ref[PAIRS + 1] = east.astype(BF16)
    x_ref[0] = half_turn(west).astype(BF16)
    ne, se, sw, nw = (rims[256 + 8 * n : 264 + 8 * n] for n in range(4))
    for base, strip, right, left in ((0, north, ne, nw), (2, south, se, sw)):
        inner = swap(strip[:32], strip[32:])
        ends = swap(right[0:1], right[1:2])
        starts = swap(left[1:2], left[0:1])
        for d in range(2):
            rows_ref[base + d, 8:40, :] = inner[d]
            rows_ref[base + d, 40:41, :] = ends[d]
            rows_ref[base + d, 7:8, :] = starts[d]


def keep_outer_rows(edge_ref, outer):
    for depth in range(3):
        outer[1 + depth, 8:40, :] = edge_row(edge_ref, 0, depth)
        outer[6 - depth, 8:40, :] = edge_row(edge_ref, 1, depth)


def finish_outer_rows(x_ref, rows_ref, outer, beside):
    outer[0] = rows_ref[0]
    outer[7] = rows_ref[2]
    for place, x in ((7, x_ref[0].astype(F32)), (40, x_ref[PAIRS + 1].astype(F32))):
        for n in range(3):
            outer[1 + n, place : place + 1, :] = x[n : n + 1]
            outer[4 + n, place : place + 1, :] = x[SIDE - 3 + n : SIDE - 2 + n]
    for n in range(8):
        beside[n] = jnp.concatenate([outer[n, 7 + d : 39 + d, :] for d in range(3)], 1).astype(BF16)


def strips_beside(rows_ref):
    parts = []
    for k in range(4):
        parts.append(jnp.concatenate([rows_ref[k, 7 + d : 39 + d, :] for d in range(3)], 1))
    return jnp.concatenate(parts, 0).astype(BF16)


def add_rims(x_ref, beside, big, z_ref, dilation):
    west = combine(dot(x_ref[0], big[0:128, :]), dilation, False)
    z_ref[0:64, :] += west
    east = combine(dot(x_ref[PAIRS + 1], big[256:384, :]), dilation, False)
    z_ref[ROWS - 64 : ROWS, :] += east
    north = dot(beside[:64], big[:, 0:128])
    south = dot(beside[64:], big[:, 256:384])
    for d in range(dilation):
        z_ref[pl.ds(dilation - 1 - d, PAIRS, stride=SIDE), :] += north[32 * d : 32 * d + 32]
        z_ref[pl.ds(SIDE - dilation + d, PAIRS, stride=SIDE), :] += south[32 * d : 32 * d + 32]


def transposed(g_ref, big, z_ref, dilation):
    def body(c):
        product = dot(neighbouring(g_ref, c * CHUNK, CHUNK), big[...])
        z_ref[chunk_rows(c), :] = combine(product, dilation, True)

    chunks(body)


def leaving_rims(border, rows_ref, big, dilation):
    rows, first, last = border
    before = combine(dot(first.astype(BF16), big[256:384, :]), dilation, True)
    after = combine(dot(last.astype(BF16), big[0:128, :]), dilation, True)
    strips, corners = [], []
    gap = jnp.zeros((6, 128), F32)
    for side in range(2):
        lines = []
        for d in range(2):
            if d < dilation:
                rows_ref[2 * side + d, 8:40, :] = rows[side, dilation - 1 - d]
                near = [rows_ref[2 * side + d, 6 + k : 46 + k, :] for k in range(3)]
                near = jnp.concatenate(near, 1).astype(BF16)
                lines.append(dot(near, big[:, 256 * side : 256 * side + 128]))
            else:
                lines.append(jnp.zeros((40, 128), F32))
        strips.append(jnp.concatenate(swap(lines[0][1:33], lines[1][1:33]), 0))
        upper, lower = swap(lines[0][33:34], lines[1][33:34])
        right = jnp.concatenate([upper, lower, gap], 0)
        lower, upper = swap(lines[0][0:1], lines[1][0:1])
        left = jnp.concatenate([upper, lower, gap], 0)
        corners.append((right, left))
    order = [strips[0], after, strips[1], half_turn(before)]
    order += [corners[0][0], corners[1][0], corners[1][1], corners[0][1]]
    return jnp.concatenate(order, 0)


def add_returned(strips, z_ref, dilation):
    z_ref[0:64, :] += strips[64:128]
    z_ref[ROWS - 64 : ROWS, :] += half_turn(strips[192:256])
    top = swap(strips[0:32], strips[32:64])
    bottom = swap(strips[128:160], strips[160:192])
    for d in range(dilation):
        z_ref[pl.ds(d, PAIRS, stride=SIDE), :] += top[d]
        z_ref[pl.ds(SIDE - 1 - d, PAIRS, stride=SIDE), :] += bottom[d]


def add_thin_returned(strips, z_ref):
    top, bottom = swap(strips[0:32], strips[32:64])
    z_ref[pl.ds(0, PAIRS, stride=SIDE), :] += top
    z_ref[pl.ds(SIDE - 1, PAIRS, stride=SIDE), :] += bottom
    sides = strips[64:128]
    low = low_half(sides)
    z_ref[0:64, :] += jnp.where(low, sides, 0.0)
    z_ref[ROWS - 64 : ROWS, :] += jnp.where(low, 0.0, sides)


def row_shifts(g, dilation):
    rows = g.shape[0]
    i = lax.broadcasted_iota(jnp.int32, g.shape, 0) % SIDE
    up = jnp.where(i < SIDE - dilation, pltpu.roll(g, rows - dilation, axis=0), 0.0)
    down = jnp.where(i >= dilation, pltpu.roll(g, dilation, axis=0), 0.0)
    return up.astype(BF16), g.astype(BF16), down.astype(BF16)


def store_shifts(c, g, dilation, shifted):
    for n, moved in enumerate(row_shifts(g, dilation)):
        shifted[chunk_rows(c), 128 * n : 128 * n + 128] = moved


def store_slabs(c, g, g_ref):
    g_ref[pl.ds(c * CHUNK + 1, CHUNK)] = g.astype(BF16).reshape(CHUNK, SIDE, 128)


def inner_products(x_ref, shifted, raw):
    for k in range(3):
        raw[k] = dot_rows(x_ref[k : k + PAIRS].reshape(ROWS, 128), shifted[...])


def strip_products(beside, border, raw):
    rows = border[0]
    zero = jnp.zeros((PAIRS, 128), F32)
    grads = [jnp.concatenate([rows[0, 1 - d], zero, zero], 1) for d in range(2)]
    grads += [jnp.concatenate([zero, zero, rows[1, 1 - d]], 1) for d in range(2)]
    grads = jnp.concatenate(grads, 0).astype(BF16)
    for k in range(3):
        raw[k] += dot_rows(beside[:, 128 * k : 128 * k + 128], grads)


def without_outer_rows(g):
    i = lax.broadcasted_iota(jnp.int32, g.shape, 0) % SIDE
    return jnp.where(i < 2, 0.0, jnp.where(i >= SIDE - 2, 0.0, g))


def border_products(x_ref, outer, border, raw):
    rows, first, last = border
    grads = jnp.concatenate([rows[0, 0], rows[0, 1], rows[1, 1], rows[1, 0]], 0).astype(BF16)
    by_row = []
    for a in range(3):
        near = jnp.concatenate([outer[n] for n in (a, a + 1, a + 4, a + 5)], 0)
        by_row.append(dot_rows(near, grads))
    by_row = jnp.concatenate(by_row, 1)
    left = jnp.concatenate(row_shifts(without_outer_rows(first), 1), 1)
    right = jnp.concatenate(row_shifts(without_outer_rows(last), 1), 1)
    sides = jnp.concatenate([left, right], 0)
    for k in range(3):
        near = jnp.concatenate([x_ref[k], x_ref[PAIRS - 1 + k]], 0)
        raw[k] += by_row[128 * k : 128 * k + 128] + dot_rows(near, sides)


def pack_taps(raw, flat, dilation):
    taps = []
    for a in range(3):
        lanes = slice(128 * a, 128 * a + 128)
        upper = [raw[k, 0:64, lanes] for k in range(3)]
        lower = [raw[k, 64:128, lanes] for k in range(3)]
        if dilation == 2:
            taps += [upper[k] + half_turn(lower[k]) for k in range(3)]
        else:
            taps.append(half_turn(upper[1]) + lower[0])
            taps.append(upper[1] + half_turn(lower[1]))
            taps.append(lower[1] + half_turn(upper[2]))
    low = low_half(taps[0])
    for t in range(0, 8, 2):
        flat[32 * t : 32 * t + 64, :] = jnp.where(low, taps[t], half_turn(taps[t + 1]))
    flat[256:288, :] = jnp.where(low[:32], taps[8][:32], half_turn(taps[8][32:]))


def write_taps(total_ref, flat, out_ref):
    for n in range(PLANE):
        flat[SHARE * n : SHARE * n + SHARE, :] = total_ref[n]
    for t in range(8):
        block = flat[t // 2 * 64 : t // 2 * 64 + 64, :]
        if t % 2 == 1:
            block = half_turn(block)
        out_ref[t] = block[:, :CHANS]
    last = flat[256:288, :]
    out_ref[8] = jnp.concatenate([last, half_turn(last)], 0)[:, :CHANS]


class Ring:
    def __init__(self, peers, source, target, send, recv):
        self.peers, self.source, self.target, self.send, self.recv = peers, source, target, send, recv

    def copy(self, offset):
        return pltpu.make_async_remote_copy(
            src_ref=self.source(offset),
            dst_ref=self.target.at[REACH - offset],
            send_sem=self.send.at[REACH + offset],
            recv_sem=self.recv.at[REACH - offset],
            device_id=(self.peers[offset],),
            device_id_type=MESH,
        )

    def start(self, offset):
        self.copy(offset).start()

    def arrived(self, slot):
        there = self.target.at[slot]
        pltpu.make_async_copy(there, there, self.recv.at[slot]).wait()

    def finish(self):
        for offset in OFFSETS:
            self.copy(offset).wait_send()


class Reduction:
    def __init__(self, here, members, levels, src, plane, level, out, sems):
        self.src, self.plane, self.level, self.out, self.sems = src, plane, level, out, sems
        self.me = here % PLANE
        self.floor = here // PLANE
        self.members = members
        self.in_plane = [here - self.me + member for member in members]
        self.levels = levels
        self.in_column = [PLANE * floor + self.me for floor in levels]

    def copies(self, step):
        result = []
        for n, device in enumerate(self.in_column if step == 1 else self.in_plane):
            if step == 0:
                src, dst = self.src.at[self.members[n]], self.plane.at[n]
            elif step == 1:
                src = dst = self.level.at[self.floor]
            else:
                src = dst = self.out.at[self.me]
            result.append(
                pltpu.make_async_remote_copy(
                    src_ref=src, dst_ref=dst,
                    send_sem=self.sems.at[2 * step, n], recv_sem=self.sems.at[2 * step + 1, n],
                    device_id=(device,), device_id_type=MESH,
                )
            )
        return result

    def start(self, step):
        for copy in self.copies(step):
            copy.start()

    def arrived(self, step):
        for n in range(len(self.levels if step == 1 else self.members)):
            there = (self.plane.at[n], self.level.at[self.levels[n % 7]], self.out.at[self.members[n]])[step]
            pltpu.make_async_copy(there, there, self.sems.at[2 * step + 1, n]).wait()

    def sent(self, step):
        for copy in self.copies(step):
            copy.wait_send()

    def scatter(self, flat):
        for n in range(PLANE):
            self.src[n] = flat[SHARE * n : SHARE * n + SHARE, :]
        self.start(0)
        self.plane[PLANE - 1] = self.src[self.me]

    def across(self):
        self.arrived(0)
        self.level[self.floor] = jnp.sum(self.plane[...], axis=0)
        self.start(1)

    def gather(self):
        self.arrived(1)
        self.out[self.me] = jnp.sum(self.level[...], axis=0)
        self.start(2)

    def gathered(self):
        for step in range(3):
            self.sent(step)
        self.arrived(2)


def level_kernel(
    devices,
    f_hbm, w1_hbm, w2_hbm, cot_hbm, nbr_hbm, turn_hbm, corner_hbm,
    pooled_hbm, gin_hbm, dw1_hbm, dw2_hbm,
    f_ref, w1_ref, w2_ref, cot_ref, nbr_ref, turn_ref, corner_ref,
    pooled_ref, gin_ref, dw1_ref, dw2_ref,
    x1, x2, g_ref, shifted, z_ref, d_ref, act_ref, edge_ref, rows1, rows2, leave, outer, near_outer, raw, flat,
    big1, big1t, big2, big2t, select, select_turned, thin,
    pool1, pool2, out2, back2, out1, back1,
    src2, plane2, level2, total2,
    src1, plane1, level1, total1,
    load_sems, store_sems, ring_sems, sems2, sems1,
):
    here = lax.axis_index("tiles")
    loads = (
        (f_hbm, f_ref), (nbr_hbm, nbr_ref), (turn_hbm, turn_ref), (corner_hbm, corner_ref),
        (w1_hbm, w1_ref), (w2_hbm, w2_ref), (cot_hbm, cot_ref),
    )
    loads = [pltpu.make_async_copy(a, b, load_sems.at[n]) for n, (a, b) in enumerate(loads)]
    for load in loads:
        load.start()
    stores = ((pooled_ref, pooled_hbm), (gin_ref, gin_hbm), (dw1_ref, dw1_hbm), (dw2_ref, dw2_hbm))
    stores = [pltpu.make_async_copy(a, b, store_sems.at[n]) for n, (a, b) in enumerate(stores)]
    barrier = pltpu.get_barrier_semaphore()

    peers = {offset: lax.rem(here + offset + devices, devices) for offset in OFFSETS}
    members, levels = plane_members(here), level_members(here)
    floor = here // PLANE * PLANE
    greeted = [PLANE * level + here % PLANE for level in levels]
    greeted += [floor + member for member in members]
    greeted += [peers[offset] for offset in OFFSETS]
    for device in greeted:
        pl.semaphore_signal(barrier, inc=1, device_id=(device,), device_id_type=MESH)

    ring1 = Ring(peers, lambda o: pool1.at[REACH], pool1, ring_sems.at[0], ring_sems.at[1])
    ring2 = Ring(peers, lambda o: pool2.at[REACH], pool2, ring_sems.at[2], ring_sems.at[3])
    ring3 = Ring(peers, lambda o: out2.at[REACH + o], back2, ring_sems.at[4], ring_sems.at[5])
    ring4 = Ring(peers, lambda o: out1.at[REACH + o], back1, ring_sems.at[6], ring_sems.at[7])
    sum2 = Reduction(here, members, levels, src2, plane2, level2, total2, sems2)
    sum1 = Reduction(here, members, levels, src1, plane1, level1, total1, sems1)

    def collect(ring, pool, chosen):
        rims = dot(chosen[REACH], pool[REACH])
        for offset in OFFSETS:
            slot = REACH - offset
            ring.arrived(slot)
            rims = rims + dot(chosen[slot], pool[slot])
        return rims

    def send_back(ring, out_ref, rims, product):
        rims = rims.astype(BF16)
        for offset in OFFSETS:
            out_ref[REACH + offset] = product(REACH + offset, rims).astype(BF16)
            ring.start(offset)
        return product(REACH, rims)

    def take_back(ring, back_ref, own):
        for offset in OFFSETS:
            ring.arrived(REACH - offset)
            own = own + back_ref[REACH - offset].astype(F32)
        return own

    empty = jnp.zeros((SIDE, 128), BF16)
    for x in (x1, x2, g_ref):
        x[0] = empty
        x[PAIRS + 1] = empty
    leave[...] = jnp.zeros_like(leave)
    loads[0].wait()
    for jp in range(PAIRS):
        x1[jp + 1] = f_ref[:, 128 * jp : 128 * jp + 128]
    for jp in range(PAIRS):
        edge_ref[0, 8 * jp : 8 * jp + 8, :] = f_ref[0:16, 128 * jp : 128 * jp + 128].astype(F32)[:8]
        edge_ref[1, 8 * jp : 8 * jp + 8, :] = f_ref[48:64, 128 * jp : 128 * jp + 128].astype(F32)[8:]
    write_thin_strips(x1, edge_ref, pool1.at[REACH])
    pl.semaphore_wait(barrier, len(greeted))
    for offset in OFFSETS:
        ring1.start(offset)

    for load in loads[1:]:
        load.wait()
    fill_weights(w1_ref, 1, False, big1)
    convolve(x1, big1, z_ref, 1)
    fill_select(here, devices, nbr_ref, turn_ref, corner_ref, select, thin)
    fill_weights(w2_ref, 2, False, big2)
    fill_weights(w2_ref, 2, True, big2t)
    fill_weights(w1_ref, 1, True, big1t)
    low = lax.broadcasted_iota(jnp.int32, (PAIRS, 128), 1) < 64
    for t in range(PAIRS // 2):
        both = cot_ref[:, 128 * t : 128 * t + 128].astype(F32) * 0.25
        turned = half_turn(both)
        for jp, value in ((2 * t, jnp.where(low, both, turned)), (2 * t + 1, jnp.where(low, turned, both))):
            act_ref[pl.ds(SIDE * jp, PAIRS, stride=2), :] = value
            act_ref[pl.ds(SIDE * jp + 1, PAIRS, stride=2), :] = value
    keep_outer_rows(edge_ref, outer)
    for k in range(SLOTS):
        select_turned[k] = jnp.transpose(select[k].astype(F32)).astype(BF16)
    place_rims(exchange_halves(collect(ring1, pool1, thin), turn_ref), x1, rows1)
    add_rims(x1, strips_beside(rows1), big1, z_ref, 1)

    def outer_y(place):
        z = z_ref[place, :]
        return z * sigmoid(z)

    write_strips(border_of(outer_y), pool2.at[REACH])
    for offset in OFFSETS:
        ring2.start(offset)

    def activate(c):
        z = z_ref[chunk_rows(c), :]
        s = sigmoid(z)
        y = z * s
        d_ref[chunk_rows(c), :] = s * (1.0 + z * (1.0 - s))
        store_slabs(c, y, x2)

    chunks(activate)
    finish_outer_rows(x1, rows1, outer, near_outer)

    convolve(x2, big2, z_ref, 2)
    place_rims(collect(ring2, pool2, select), x2, rows2)
    beside2 = strips_beside(rows2)
    add_rims(x2, beside2, big2, z_ref, 2)

    def second_gradient(place):
        z = z_ref[place, :]
        s = sigmoid(z)
        g = act_ref[place, :] * s * (1.0 + z * (1.0 - s))
        return g.astype(BF16).astype(F32)

    border2 = border_of(second_gradient)
    rims = leaving_rims(border2, leave, big2t, 2)
    own = send_back(ring3, out2, rims, lambda k, x: dot(select_turned[k], x))

    def second(c):
        z = z_ref[chunk_rows(c), :]
        s = sigmoid(z)
        z_ref[chunk_rows(c), :] = z * s * 0.25
        g = (act_ref[chunk_rows(c), :] * s * (1.0 + z * (1.0 - s))).astype(BF16).astype(F32)
        store_slabs(c, g, g_ref)
        store_shifts(c, g, 2, shifted)

    chunks(second)
    inner_products(x2, shifted, raw)
    strip_products(beside2, border2, raw)
    pack_taps(raw, flat, 2)
    sum2.scatter(flat)
    for t in range(PAIRS // 2):
        sums = []
        for jp in (2 * t, 2 * t + 1):
            v = z_ref[pl.ds(SIDE * jp, PAIRS, stride=2), :] + z_ref[pl.ds(SIDE * jp + 1, PAIRS, stride=2), :]
            sums.append(v + half_turn(v))
        pooled_ref[:, 128 * t : 128 * t + 128] = jnp.where(low, sums[0], sums[1]).astype(BF16)
    stores[0].start()
    transposed(g_ref, big2t, z_ref, 2)

    def inside(c):
        g = without_outer_rows(z_ref[chunk_rows(c), :] * d_ref[chunk_rows(c), :])
        store_shifts(c, g, 1, shifted)

    chunks(inside)
    shifted[0:SIDE] = jnp.zeros((SIDE, 384), BF16)
    shifted[ROWS - SIDE : ROWS] = jnp.zeros((SIDE, 384), BF16)
    inner_products(x1, shifted, raw)
    sum2.across()
    add_returned(take_back(ring3, back2, own), z_ref, 2)

    def first_gradient(place):
        return (z_ref[place, :] * d_ref[place, :]).astype(BF16).astype(F32)

    border1 = border_of(first_gradient)
    border_products(x1, near_outer, border1, raw)
    pack_taps(raw, flat, 1)
    sum1.scatter(flat)
    rims = exchange_halves(leaving_rims(border1, leave, big1t, 1), turn_ref)
    own = send_back(ring4, out1, rims, lambda k, x: dot_rows(thin[k], x))

    def first(c):
        store_slabs(c, z_ref[chunk_rows(c), :] * d_ref[chunk_rows(c), :], g_ref)

    chunks(first)
    sum2.gather()
    transposed(g_ref, big1t, z_ref, 1)
    sum1.across()
    add_thin_returned(take_back(ring4, back1, own), z_ref)
    for jp in range(PAIRS):
        gin_ref[:, 128 * jp : 128 * jp + 128] = z_ref[SIDE * jp : SIDE * jp + SIDE, :].astype(BF16)
    stores[1].start()
    sum1.gather()
    sum2.gathered()
    for ring in (ring1, ring2, ring3, ring4):
        ring.finish()
    write_taps(total2, flat, dw2_ref)
    stores[3].start()
    sum1.gathered()
    write_taps(total1, flat, dw1_ref)
    stores[2].start()
    for store in stores:
        store.wait()


def finish_kernel(*refs):
    copies = [pltpu.make_async_copy(refs[n], refs[4 + n], refs[8].at[n]) for n in range(4)]
    for copy in copies:
        copy.start()
    for copy in copies:
        copy.wait()


def local(features, weights_first, weights_second, cotangent, neighbours, turns, corners):
    devices = lax.axis_size("tiles")
    anywhere = pl.BlockSpec(memory_space=pl.ANY)
    inputs = (features[0], weights_first, weights_second, cotangent[0], neighbours, turns, corners)
    inputs = tuple(pltpu.with_memory_space_constraint(x, pltpu.HBM) for x in inputs)
    outputs = (
        jax.ShapeDtypeStruct((PAIRS, PAIRS * CHANS), BF16),
        jax.ShapeDtypeStruct((SIDE, SIDE * CHANS), BF16),
        jax.ShapeDtypeStruct((9, CHANS, CHANS), F32),
        jax.ShapeDtypeStruct((9, CHANS, CHANS), F32),
    )
    slabs = pltpu.VMEM((PAIRS + 2, SIDE, 128), BF16)
    field = pltpu.VMEM((ROWS, 128), F32)
    big = pltpu.VMEM((384, 384), BF16)
    pool = pltpu.VMEM((SLOTS, STRIP, 128), BF16)
    thin_pool = pltpu.VMEM((SLOTS, 128, 128), BF16)
    rows = pltpu.VMEM((4, 48, 128), F32)

    def shares(count):
        return pltpu.VMEM((count, SHARE, 128), F32)

    reduction = [shares(n) for n in (PLANE, PLANE, LEVELS, PLANE)]
    results = pl.pallas_call(
        functools.partial(level_kernel, devices),
        out_shape=tuple(pltpu.VMEM(x.shape, x.dtype) for x in outputs),
        in_specs=[pl.BlockSpec(memory_space=pltpu.HBM)] * 7,
        out_specs=[anywhere] * 4,
        scratch_shapes=[pltpu.VMEM(x.shape, x.dtype) for x in inputs[:4]]
        + [pltpu.SMEM(x.shape, x.dtype) for x in inputs[4:]]
        + [pltpu.VMEM(x.shape, x.dtype) for x in outputs]
        + [
            slabs, slabs, slabs,
            pltpu.VMEM((ROWS, 384), BF16),
            field, field, field,
            pltpu.VMEM((2, 8 * PAIRS, 128), F32),
            rows, rows, rows,
            pltpu.VMEM((8, 48, 128), F32),
            pltpu.VMEM((8, PAIRS, 384), BF16),
            pltpu.VMEM((3, 128, 384), F32),
            pltpu.VMEM((2 * PLANE * SHARE, 128), F32),
            big, big, big, big,
            pltpu.VMEM((SLOTS, RIMS, STRIP), BF16),
            pltpu.VMEM((SLOTS, STRIP, RIMS), BF16),
            pltpu.VMEM((SLOTS, RIMS, 128), BF16),
            thin_pool, pool, pool, pool, thin_pool, thin_pool,
        ]
        + reduction
        + reduction
        + [
            pltpu.SemaphoreType.DMA((7,)),
            pltpu.SemaphoreType.DMA((4,)),
            pltpu.SemaphoreType.DMA((8, SLOTS)),
            pltpu.SemaphoreType.DMA((6, PLANE)),
            pltpu.SemaphoreType.DMA((6, PLANE)),
        ],
        compiler_params=pltpu.CompilerParams(
            collective_id=0, has_side_effects=True, vmem_limit_bytes=48 * 2**20
        ),
        name="level",
    )(*inputs)
    pooled, grad, first, second = pl.pallas_call(
        finish_kernel,
        out_shape=outputs,
        in_specs=[anywhere] * 4,
        out_specs=[anywhere] * 4,
        scratch_shapes=[pltpu.SemaphoreType.DMA((4,))],
        compiler_params=pltpu.CompilerParams(vmem_limit_bytes=4 * 2**20),
        name="finish",
    )(*results)
    return pooled[None], grad[None], first, second


def solution(mesh):
    return jax.shard_map(
        local,
        mesh=mesh,
        in_specs=(
            P("tiles", None, None),
            P(),
            P(),
            P("tiles", None, None),
            P("tiles", None),
            P("tiles", None),
            P("tiles", None),
        ),
        out_specs=(P("tiles", None, None), P("tiles", None, None), P(), P()),
        check_vma=False,
    )
```

```python
import functools

import jax
import jax.numpy as jnp
from jax import lax
from jax.experimental import pallas as pl
from jax.experimental.pallas import tpu as pltpu
from jax.sharding import PartitionSpec as P

REACH = 3
SLOTS = 2 * REACH + 1
SIDE = 64
CHANS = 64
PAIRS = SIDE // 2
ROWS = PAIRS * SIDE
STRIP = 4 * SIDE
PLANE = 32
LEVELS = 8
SHARE = 9
CHUNK = 8
RIMS = 4 * SIDE + 32
MESH = pl.DeviceIdType.MESH
BF16 = jnp.bfloat16
F32 = jnp.float32
EDGE_DIRS = ((0, 2), (2, 1), (4, 0), (6, 3))
CORNER_DIRS = ((1, 2, False), (3, 0, False), (5, 0, True), (7, 2, True))
OFFSETS = (1, -1, 2, -2, 3, -3)


def dot(a, b):
    return jnp.dot(a, b, preferred_element_type=F32)


def dot_rows(a, b):
    return lax.dot_general(a, b, (((0,), (0,)), ((), ())), preferred_element_type=F32)


def half_turn(x):
    return pltpu.roll(x, 64, axis=1)


def low_half(x):
    return lax.broadcasted_iota(jnp.int32, x.shape, 1) < 64


def swap(x, y):
    low = low_half(x)
    return jnp.where(low, x, half_turn(y)), jnp.where(low, half_turn(x), y)


def sigmoid(z):
    return 1.0 / (1.0 + jnp.exp(-z))


def hops(steps, size):
    return min(steps, size - steps)


PLANE_STEPS = sorted(
    ((x, y, core) for x in range(4) for y in range(4) for core in range(2) if x or y or core),
    key=lambda step: -(hops(step[0], 4) + hops(step[1], 4)),
)
LEVEL_STEPS = sorted(range(1, LEVELS), key=lambda step: -hops(step, LEVELS))


def plane_members(here):
    x, y, core = here // 8 % 4, here // 2 % 4, here % 2
    xs = [8 * ((x + step) % 4) for step in range(4)]
    ys = [2 * ((y + step) % 4) for step in range(4)]
    cores = [core, 1 - core]
    return [xs[a] + ys[b] + cores[c] for a, b, c in PLANE_STEPS]


def level_members(here):
    return [(here // PLANE + step) % LEVELS for step in LEVEL_STEPS]


def blocks_of(w_ref, dilation, turned):
    taps = [w_ref[t].astype(F32) for t in range(9)]
    if turned:
        taps = [jnp.transpose(tap) for tap in taps]
    zero = jnp.zeros((CHANS, CHANS), F32)
    result = {}
    for a in range(3):
        left, mid, right = taps[3 * a : 3 * a + 3]
        if dilation == 2:
            quads = {d: (w, zero, zero, w) for d, w in ((-1, left), (0, mid), (1, right))}
        else:
            quads = {-1: (zero, zero, left, zero), 0: (mid, left, right, mid), 1: (zero, right, zero, zero)}
        for d, (q00, q01, q10, q11) in quads.items():
            if turned:
                q01, q10 = q10, q01
                d = -d
            block = jnp.concatenate(
                [jnp.concatenate([q00, q01], 1), jnp.concatenate([q10, q11], 1)], 0
            )
            result[a, d] = block.astype(BF16)
    return result


def fill_weights(w_ref, dilation, turned, big):
    for (a, d), block in blocks_of(w_ref, dilation, turned).items():
        big[(d + 1) * 128 : (d + 2) * 128, a * 128 : (a + 1) * 128] = block


def combine(product, dilation, turned):
    rows = product.shape[0]
    up, mid, down = product[:, :128], product[:, 128:256], product[:, 256:]
    if turned:
        up, down = down, up
    i = lax.broadcasted_iota(jnp.int32, (rows, 128), 0) % SIDE
    up = jnp.where(i >= dilation, pltpu.roll(up, dilation, axis=0), 0.0)
    down = jnp.where(i < SIDE - dilation, pltpu.roll(down, rows - dilation, axis=0), 0.0)
    return mid + up + down


def neighbouring(x_ref, start, count):
    parts = [x_ref[pl.ds(start + k, count)].reshape(count * SIDE, 128) for k in range(3)]
    return jnp.concatenate(parts, 1)


def chunks(body):
    def step(c, unused):
        body(c)
        return unused

    lax.fori_loop(0, PAIRS // CHUNK, step, 0)


def chunk_rows(c):
    return pl.ds(pl.multiple_of(c * (CHUNK * SIDE), CHUNK * SIDE), CHUNK * SIDE)


def convolve(x_ref, big, z_ref, dilation):
    def body(c):
        product = dot(neighbouring(x_ref, c * CHUNK, CHUNK), big[...])
        z_ref[chunk_rows(c), :] = combine(product, dilation, False)

    chunks(body)


def edge_row(edge_ref, side, depth):
    return edge_ref[side, pl.ds(depth if side == 0 else 7 - depth, PAIRS, stride=8), :]


def border_of(make):
    rows = {}
    for depth in range(2):
        rows[0, depth] = make(pl.ds(depth, PAIRS, stride=SIDE))
        rows[1, depth] = make(pl.ds(SIDE - 1 - depth, PAIRS, stride=SIDE))
    return rows, make(slice(0, SIDE)), make(slice(ROWS - SIDE, ROWS))


def write_strips(border, strip_ref):
    rows, first, last = border
    strip_ref[0:64] = jnp.concatenate(swap(rows[0, 0], rows[0, 1]), 0).astype(BF16)
    strip_ref[64:128] = first.astype(BF16)
    strip_ref[128:192] = jnp.concatenate(swap(rows[1, 0], rows[1, 1]), 0).astype(BF16)
    strip_ref[192:256] = half_turn(last).astype(BF16)


def write_thin_strips(x_ref, edge_ref, strip_ref):
    strip_ref[0:64] = jnp.concatenate(swap(edge_row(edge_ref, 0, 0), edge_row(edge_ref, 1, 0)), 0).astype(BF16)
    first, last = x_ref[1].astype(F32), x_ref[PAIRS].astype(F32)
    strip_ref[64:128] = jnp.where(low_half(first), first, last).astype(BF16)


def fill_select(here, devices, nbr_ref, turn_ref, corner_ref, select, thin):
    def slot_of(j):
        return lax.rem(nbr_ref[0, j] - here + REACH + devices, devices)

    def columns_of(p, edge, quarter, flips):
        source = lax.rem(edge + 4 - quarter, 4)
        flip = jnp.where(quarter == flips[0], 1, jnp.where(quarter == flips[1], 1, 0))
        p = p + flip * (63 - 2 * p)
        split = (p % 2) * 32 + p // 2
        place = split + lax.rem(source, 2) * (p - split)
        return source * 64 + place, lax.rem(source, 2) * 64 + place

    lane = lax.broadcasted_iota(jnp.int32, (SIDE, STRIP), 1)
    row = lax.broadcasted_iota(jnp.int32, (SIDE, STRIP), 0)
    for n, (j, edge) in enumerate(EDGE_DIRS):
        if edge % 2 == 0:
            cols, thin_cols = columns_of(row % 32 * 2 + row // 32, edge, turn_ref[0, j], (2, 3))
        else:
            cols, thin_cols = columns_of(row, edge, turn_ref[0, j], (1, 2))
        hit = jnp.where(lane == cols, 1.0, 0.0)
        thin_hit = jnp.where(lane == thin_cols, 1.0, 0.0)[:, :128]
        slot = slot_of(j)
        for k in range(SLOTS):
            here_it_is = jnp.where(slot == k, 1.0, 0.0)
            select[k, n * 64 : (n + 1) * 64] = (hit * here_it_is).astype(BF16)
            thin[k, n * 64 : (n + 1) * 64] = (thin_hit * here_it_is).astype(BF16)
    lane = lane[:8]
    row = row[:8]
    hits = []
    for j, edge, last in CORNER_DIRS:
        cols, thin_cols = columns_of(63 - row if last else row, edge, turn_ref[0, j], (2, 3))
        keep = jnp.where(row < 2, 1.0, 0.0) * corner_ref[0, j // 2].astype(F32)
        hit = jnp.where(lane == cols, 1.0, 0.0) * keep
        thin_hit = (jnp.where(lane == thin_cols, 1.0, 0.0) * keep)[:, :128]
        hits.append((hit, thin_hit, slot_of(j)))
    for k in range(SLOTS):
        parts = [hit * jnp.where(slot == k, 1.0, 0.0) for hit, unused, slot in hits]
        select[k, 256:288] = jnp.concatenate(parts, 0).astype(BF16)
        parts = [hit * jnp.where(slot == k, 1.0, 0.0) for unused, hit, slot in hits]
        thin[k, 256:288] = jnp.concatenate(parts, 0).astype(BF16)


def exchange_halves(rims, turn_ref):
    parts = []
    places = [(j, edge, 64) for j, edge in EDGE_DIRS] + [(j, edge, 8) for j, edge, unused in CORNER_DIRS]
    start = 0
    for j, edge, count in places:
        block = rims[start : start + count]
        high = (lax.rem(edge + 4 - turn_ref[0, j], 4) // 2).astype(F32)
        parts.append(block * (1.0 - high) + half_turn(block) * high)
        start += count
    return jnp.concatenate(parts, 0)


def place_rims(rims, x_ref, rows_ref):
    north, east, south, west = (rims[64 * n : 64 * n + 64] for n in range(4))
    x_ref[PAIRS + 1] = east.astype(BF16)
    x_ref[0] = half_turn(west).astype(BF16)
    ne, se, sw, nw = (rims[256 + 8 * n : 264 + 8 * n] for n in range(4))
    for base, strip, right, left in ((0, north, ne, nw), (2, south, se, sw)):
        inner = swap(strip[:32], strip[32:])
        ends = swap(right[0:1], right[1:2])
        starts = swap(left[1:2], left[0:1])
        for d in range(2):
            rows_ref[base + d, 8:40, :] = inner[d]
            rows_ref[base + d, 40:41, :] = ends[d]
            rows_ref[base + d, 7:8, :] = starts[d]


def keep_outer_rows(edge_ref, outer):
    for depth in range(3):
        outer[1 + depth, 8:40, :] = edge_row(edge_ref, 0, depth)
        outer[6 - depth, 8:40, :] = edge_row(edge_ref, 1, depth)


def finish_outer_rows(x_ref, rows_ref, outer, beside):
    outer[0] = rows_ref[0]
    outer[7] = rows_ref[2]
    for place, x in ((7, x_ref[0].astype(F32)), (40, x_ref[PAIRS + 1].astype(F32))):
        for n in range(3):
            outer[1 + n, place : place + 1, :] = x[n : n + 1]
            outer[4 + n, place : place + 1, :] = x[SIDE - 3 + n : SIDE - 2 + n]
    for n in range(8):
        beside[n] = jnp.concatenate([outer[n, 7 + d : 39 + d, :] for d in range(3)], 1).astype(BF16)


def strips_beside(rows_ref):
    parts = []
    for k in range(4):
        parts.append(jnp.concatenate([rows_ref[k, 7 + d : 39 + d, :] for d in range(3)], 1))
    return jnp.concatenate(parts, 0).astype(BF16)


def add_rims(x_ref, beside, big, z_ref, dilation):
    west = combine(dot(x_ref[0], big[0:128, :]), dilation, False)
    z_ref[0:64, :] += west
    east = combine(dot(x_ref[PAIRS + 1], big[256:384, :]), dilation, False)
    z_ref[ROWS - 64 : ROWS, :] += east
    north = dot(beside[:64], big[:, 0:128])
    south = dot(beside[64:], big[:, 256:384])
    for d in range(dilation):
        z_ref[pl.ds(dilation - 1 - d, PAIRS, stride=SIDE), :] += north[32 * d : 32 * d + 32]
        z_ref[pl.ds(SIDE - dilation + d, PAIRS, stride=SIDE), :] += south[32 * d : 32 * d + 32]


def transposed(g_ref, big, z_ref, dilation):
    def body(c):
        product = dot(neighbouring(g_ref, c * CHUNK, CHUNK), big[...])
        z_ref[chunk_rows(c), :] = combine(product, dilation, True)

    chunks(body)


def leaving_rims(border, rows_ref, big, dilation):
    rows, first, last = border
    before = combine(dot(first.astype(BF16), big[256:384, :]), dilation, True)
    after = combine(dot(last.astype(BF16), big[0:128, :]), dilation, True)
    strips, corners = [], []
    gap = jnp.zeros((6, 128), F32)
    for side in range(2):
        lines = []
        for d in range(2):
            if d < dilation:
                rows_ref[2 * side + d, 8:40, :] = rows[side, dilation - 1 - d]
                near = [rows_ref[2 * side + d, 6 + k : 46 + k, :] for k in range(3)]
                near = jnp.concatenate(near, 1).astype(BF16)
                lines.append(dot(near, big[:, 256 * side : 256 * side + 128]))
            else:
                lines.append(jnp.zeros((40, 128), F32))
        strips.append(jnp.concatenate(swap(lines[0][1:33], lines[1][1:33]), 0))
        upper, lower = swap(lines[0][33:34], lines[1][33:34])
        right = jnp.concatenate([upper, lower, gap], 0)
        lower, upper = swap(lines[0][0:1], lines[1][0:1])
        left = jnp.concatenate([upper, lower, gap], 0)
        corners.append((right, left))
    order = [strips[0], after, strips[1], half_turn(before)]
    order += [corners[0][0], corners[1][0], corners[1][1], corners[0][1]]
    return jnp.concatenate(order, 0)


def add_returned(strips, z_ref, dilation):
    z_ref[0:64, :] += strips[64:128]
    z_ref[ROWS - 64 : ROWS, :] += half_turn(strips[192:256])
    top = swap(strips[0:32], strips[32:64])
    bottom = swap(strips[128:160], strips[160:192])
    for d in range(dilation):
        z_ref[pl.ds(d, PAIRS, stride=SIDE), :] += top[d]
        z_ref[pl.ds(SIDE - 1 - d, PAIRS, stride=SIDE), :] += bottom[d]


def add_thin_returned(strips, z_ref):
    top, bottom = swap(strips[0:32], strips[32:64])
    z_ref[pl.ds(0, PAIRS, stride=SIDE), :] += top
    z_ref[pl.ds(SIDE - 1, PAIRS, stride=SIDE), :] += bottom
    sides = strips[64:128]
    low = low_half(sides)
    z_ref[0:64, :] += jnp.where(low, sides, 0.0)
    z_ref[ROWS - 64 : ROWS, :] += jnp.where(low, 0.0, sides)


def row_shifts(g, dilation):
    rows = g.shape[0]
    i = lax.broadcasted_iota(jnp.int32, g.shape, 0) % SIDE
    up = jnp.where(i < SIDE - dilation, pltpu.roll(g, rows - dilation, axis=0), 0.0)
    down = jnp.where(i >= dilation, pltpu.roll(g, dilation, axis=0), 0.0)
    return up.astype(BF16), g.astype(BF16), down.astype(BF16)


def store_shifts(c, g, dilation, shifted):
    for n, moved in enumerate(row_shifts(g, dilation)):
        shifted[chunk_rows(c), 128 * n : 128 * n + 128] = moved


def store_slabs(c, g, g_ref):
    g_ref[pl.ds(c * CHUNK + 1, CHUNK)] = g.astype(BF16).reshape(CHUNK, SIDE, 128)


def inner_products(x_ref, shifted, raw):
    for k in range(3):
        raw[k] = dot_rows(x_ref[k : k + PAIRS].reshape(ROWS, 128), shifted[...])


def strip_products(beside, border, raw):
    rows = border[0]
    zero = jnp.zeros((PAIRS, 128), F32)
    grads = [jnp.concatenate([rows[0, 1 - d], zero, zero], 1) for d in range(2)]
    grads += [jnp.concatenate([zero, zero, rows[1, 1 - d]], 1) for d in range(2)]
    grads = jnp.concatenate(grads, 0).astype(BF16)
    for k in range(3):
        raw[k] += dot_rows(beside[:, 128 * k : 128 * k + 128], grads)


def without_outer_rows(g):
    i = lax.broadcasted_iota(jnp.int32, g.shape, 0) % SIDE
    return jnp.where(i < 2, 0.0, jnp.where(i >= SIDE - 2, 0.0, g))


def border_products(x_ref, outer, border, raw):
    rows, first, last = border
    grads = jnp.concatenate([rows[0, 0], rows[0, 1], rows[1, 1], rows[1, 0]], 0).astype(BF16)
    by_row = []
    for a in range(3):
        near = jnp.concatenate([outer[n] for n in (a, a + 1, a + 4, a + 5)], 0)
        by_row.append(dot_rows(near, grads))
    by_row = jnp.concatenate(by_row, 1)
    left = jnp.concatenate(row_shifts(without_outer_rows(first), 1), 1)
    right = jnp.concatenate(row_shifts(without_outer_rows(last), 1), 1)
    sides = jnp.concatenate([left, right], 0)
    for k in range(3):
        near = jnp.concatenate([x_ref[k], x_ref[PAIRS - 1 + k]], 0)
        raw[k] += by_row[128 * k : 128 * k + 128] + dot_rows(near, sides)


def pack_taps(raw, flat, dilation):
    taps = []
    for a in range(3):
        lanes = slice(128 * a, 128 * a + 128)
        upper = [raw[k, 0:64, lanes] for k in range(3)]
        lower = [raw[k, 64:128, lanes] for k in range(3)]
        if dilation == 2:
            taps += [upper[k] + half_turn(lower[k]) for k in range(3)]
        else:
            taps.append(half_turn(upper[1]) + lower[0])
            taps.append(upper[1] + half_turn(lower[1]))
            taps.append(lower[1] + half_turn(upper[2]))
    low = low_half(taps[0])
    for t in range(0, 8, 2):
        flat[32 * t : 32 * t + 64, :] = jnp.where(low, taps[t], half_turn(taps[t + 1]))
    flat[256:288, :] = jnp.where(low[:32], taps[8][:32], half_turn(taps[8][32:]))


def write_taps(total_ref, flat, out_ref):
    for n in range(PLANE):
        flat[SHARE * n : SHARE * n + SHARE, :] = total_ref[n]
    for t in range(8):
        block = flat[t // 2 * 64 : t // 2 * 64 + 64, :]
        if t % 2 == 1:
            block = half_turn(block)
        out_ref[t] = block[:, :CHANS]
    last = flat[256:288, :]
    out_ref[8] = jnp.concatenate([last, half_turn(last)], 0)[:, :CHANS]


class Ring:
    def __init__(self, peers, source, target, send, recv):
        self.peers, self.source, self.target, self.send, self.recv = peers, source, target, send, recv

    def copy(self, offset):
        return pltpu.make_async_remote_copy(
            src_ref=self.source(offset),
            dst_ref=self.target.at[REACH - offset],
            send_sem=self.send.at[REACH + offset],
            recv_sem=self.recv.at[REACH - offset],
            device_id=(self.peers[offset],),
            device_id_type=MESH,
        )

    def start(self, offset):
        self.copy(offset).start()

    def arrived(self, slot):
        there = self.target.at[slot]
        pltpu.make_async_copy(there, there, self.recv.at[slot]).wait()

    def finish(self):
        for offset in OFFSETS:
            self.copy(offset).wait_send()


class Reduction:
    def __init__(self, here, members, levels, src, plane, level, out, sems):
        self.src, self.plane, self.level, self.out, self.sems = src, plane, level, out, sems
        self.me = here % PLANE
        self.floor = here // PLANE
        self.members = members
        self.in_plane = [here - self.me + member for member in members]
        self.levels = levels
        self.in_column = [PLANE * floor + self.me for floor in levels]

    def copies(self, step):
        result = []
        for n, device in enumerate(self.in_column if step == 1 else self.in_plane):
            if step == 0:
                src, dst = self.src.at[self.members[n]], self.plane.at[n]
            elif step == 1:
                src = dst = self.level.at[self.floor]
            else:
                src = dst = self.out.at[self.me]
            result.append(
                pltpu.make_async_remote_copy(
                    src_ref=src, dst_ref=dst,
                    send_sem=self.sems.at[2 * step, n], recv_sem=self.sems.at[2 * step + 1, n],
                    device_id=(device,), device_id_type=MESH,
                )
            )
        return result

    def start(self, step):
        for copy in self.copies(step):
            copy.start()

    def arrived(self, step):
        places = (
            [self.plane.at[n] for n in range(len(self.members))],
            [self.level.at[n] for n in self.levels],
            [self.out.at[n] for n in self.members],
        )
        for n, there in enumerate(places[step]):
            pltpu.make_async_copy(there, there, self.sems.at[2 * step + 1, n]).wait()

    def sent(self, step):
        for copy in self.copies(step):
            copy.wait_send()

    def scatter(self, flat):
        for n in range(PLANE):
            self.src[n] = flat[SHARE * n : SHARE * n + SHARE, :]
        self.start(0)
        self.plane[PLANE - 1] = self.src[self.me]

    def across(self):
        self.arrived(0)
        self.level[self.floor] = jnp.sum(self.plane[...], axis=0)
        self.start(1)

    def gather(self):
        self.arrived(1)
        self.out[self.me] = jnp.sum(self.level[...], axis=0)
        self.start(2)

    def gathered(self):
        for step in range(3):
            self.sent(step)
        self.arrived(2)


def level_kernel(
    devices,
    f_hbm, w1_hbm, w2_hbm, cot_hbm, nbr_hbm, turn_hbm, corner_hbm,
    pooled_ref, gin_ref, dw1_ref, dw2_ref,
    f_ref, w1_ref, w2_ref, cot_ref, nbr_ref, turn_ref, corner_ref,
    x1, x2, g_ref, shifted, z_ref, d_ref, act_ref, edge_ref, rows1, rows2, leave, outer, near_outer, raw, flat,
    big1, big1t, big2, big2t, select, select_turned, thin,
    pool1, pool2, out2, back2, out1, back1,
    src2, plane2, level2, total2,
    src1, plane1, level1, total1,
    load_sems, ring_sems, sems2, sems1,
):
    here = lax.axis_index("tiles")
    loads = (
        (f_hbm, f_ref), (nbr_hbm, nbr_ref), (turn_hbm, turn_ref), (corner_hbm, corner_ref),
        (w1_hbm, w1_ref), (w2_hbm, w2_ref), (cot_hbm, cot_ref),
    )
    loads = [pltpu.make_async_copy(a, b, load_sems.at[n]) for n, (a, b) in enumerate(loads)]
    for load in loads:
        load.start()
    barrier = pltpu.get_barrier_semaphore()

    peers = {offset: lax.rem(here + offset + devices, devices) for offset in OFFSETS}
    members, levels = plane_members(here), level_members(here)
    floor = here // PLANE * PLANE
    greeted = [PLANE * level + here % PLANE for level in levels]
    greeted += [floor + member for member in members]
    greeted += [peers[offset] for offset in OFFSETS]
    for device in greeted:
        pl.semaphore_signal(barrier, inc=1, device_id=(device,), device_id_type=MESH)

    ring1 = Ring(peers, lambda o: pool1.at[REACH], pool1, ring_sems.at[0], ring_sems.at[1])
    ring2 = Ring(peers, lambda o: pool2.at[REACH], pool2, ring_sems.at[2], ring_sems.at[3])
    ring3 = Ring(peers, lambda o: out2.at[REACH + o], back2, ring_sems.at[4], ring_sems.at[5])
    ring4 = Ring(peers, lambda o: out1.at[REACH + o], back1, ring_sems.at[6], ring_sems.at[7])
    sum2 = Reduction(here, members, levels, src2, plane2, level2, total2, sems2)
    sum1 = Reduction(here, members, levels, src1, plane1, level1, total1, sems1)

    def collect(ring, pool, chosen):
        rims = dot(chosen[REACH], pool[REACH])
        for offset in OFFSETS:
            slot = REACH - offset
            ring.arrived(slot)
            rims = rims + dot(chosen[slot], pool[slot])
        return rims

    def send_back(ring, out_ref, rims, product):
        rims = rims.astype(BF16)
        for offset in OFFSETS:
            out_ref[REACH + offset] = product(REACH + offset, rims).astype(BF16)
            ring.start(offset)
        return product(REACH, rims)

    def take_back(ring, back_ref, own):
        for offset in OFFSETS:
            ring.arrived(REACH - offset)
            own = own + back_ref[REACH - offset].astype(F32)
        return own

    empty = jnp.zeros((SIDE, 128), BF16)
    for x in (x1, x2, g_ref):
        x[0] = empty
        x[PAIRS + 1] = empty
    leave[...] = jnp.zeros_like(leave)
    loads[0].wait()
    for jp in range(PAIRS):
        x1[jp + 1] = f_ref[:, 128 * jp : 128 * jp + 128]
    for jp in range(PAIRS):
        edge_ref[0, 8 * jp : 8 * jp + 8, :] = f_ref[0:16, 128 * jp : 128 * jp + 128].astype(F32)[:8]
        edge_ref[1, 8 * jp : 8 * jp + 8, :] = f_ref[48:64, 128 * jp : 128 * jp + 128].astype(F32)[8:]
    write_thin_strips(x1, edge_ref, pool1.at[REACH])
    pl.semaphore_wait(barrier, len(greeted))
    for offset in OFFSETS:
        ring1.start(offset)

    for load in loads[1:]:
        load.wait()
    fill_weights(w1_ref, 1, False, big1)
    convolve(x1, big1, z_ref, 1)
    fill_select(here, devices, nbr_ref, turn_ref, corner_ref, select, thin)
    fill_weights(w2_ref, 2, False, big2)
    fill_weights(w2_ref, 2, True, big2t)
    fill_weights(w1_ref, 1, True, big1t)
    low = lax.broadcasted_iota(jnp.int32, (PAIRS, 128), 1) < 64
    for t in range(PAIRS // 2):
        both = cot_ref[:, 128 * t : 128 * t + 128].astype(F32) * 0.25
        turned = half_turn(both)
        for jp, value in ((2 * t, jnp.where(low, both, turned)), (2 * t + 1, jnp.where(low, turned, both))):
            act_ref[pl.ds(SIDE * jp, PAIRS, stride=2), :] = value
            act_ref[pl.ds(SIDE * jp + 1, PAIRS, stride=2), :] = value
    keep_outer_rows(edge_ref, outer)
    for k in range(SLOTS):
        select_turned[k] = jnp.transpose(select[k].astype(F32)).astype(BF16)
    place_rims(exchange_halves(collect(ring1, pool1, thin), turn_ref), x1, rows1)
    add_rims(x1, strips_beside(rows1), big1, z_ref, 1)

    def outer_y(place):
        z = z_ref[place, :]
        return z * sigmoid(z)

    write_strips(border_of(outer_y), pool2.at[REACH])
    for offset in OFFSETS:
        ring2.start(offset)

    def activate(c):
        z = z_ref[chunk_rows(c), :]
        s = sigmoid(z)
        y = z * s
        d_ref[chunk_rows(c), :] = s * (1.0 + z * (1.0 - s))
        store_slabs(c, y, x2)

    chunks(activate)
    finish_outer_rows(x1, rows1, outer, near_outer)

    convolve(x2, big2, z_ref, 2)
    place_rims(collect(ring2, pool2, select), x2, rows2)
    beside2 = strips_beside(rows2)
    add_rims(x2, beside2, big2, z_ref, 2)

    def second_gradient(place):
        z = z_ref[place, :]
        s = sigmoid(z)
        g = act_ref[place, :] * s * (1.0 + z * (1.0 - s))
        return g.astype(BF16).astype(F32)

    border2 = border_of(second_gradient)
    rims = leaving_rims(border2, leave, big2t, 2)
    own = send_back(ring3, out2, rims, lambda k, x: dot(select_turned[k], x))

    def second(c):
        z = z_ref[chunk_rows(c), :]
        s = sigmoid(z)
        z_ref[chunk_rows(c), :] = z * s * 0.25
        g = (act_ref[chunk_rows(c), :] * s * (1.0 + z * (1.0 - s))).astype(BF16).astype(F32)
        store_slabs(c, g, g_ref)
        store_shifts(c, g, 2, shifted)

    chunks(second)
    inner_products(x2, shifted, raw)
    strip_products(beside2, border2, raw)
    pack_taps(raw, flat, 2)
    for t in range(PAIRS // 2):
        sums = []
        for jp in (2 * t, 2 * t + 1):
            v = z_ref[pl.ds(SIDE * jp, PAIRS, stride=2), :] + z_ref[pl.ds(SIDE * jp + 1, PAIRS, stride=2), :]
            sums.append(v + half_turn(v))
        pooled_ref[:, 128 * t : 128 * t + 128] = jnp.where(low, sums[0], sums[1]).astype(BF16)
    transposed(g_ref, big2t, z_ref, 2)

    def inside(c):
        g = without_outer_rows(z_ref[chunk_rows(c), :] * d_ref[chunk_rows(c), :])
        store_shifts(c, g, 1, shifted)

    chunks(inside)
    shifted[0:SIDE] = jnp.zeros((SIDE, 384), BF16)
    shifted[ROWS - SIDE : ROWS] = jnp.zeros((SIDE, 384), BF16)
    inner_products(x1, shifted, raw)
    sum2.scatter(flat)
    add_returned(take_back(ring3, back2, own), z_ref, 2)

    def first_gradient(place):
        return (z_ref[place, :] * d_ref[place, :]).astype(BF16).astype(F32)

    border1 = border_of(first_gradient)
    border_products(x1, near_outer, border1, raw)
    pack_taps(raw, flat, 1)
    sum1.scatter(flat)
    rims = exchange_halves(leaving_rims(border1, leave, big1t, 1), turn_ref)

    def first(c):
        store_slabs(c, z_ref[chunk_rows(c), :] * d_ref[chunk_rows(c), :], g_ref)

    chunks(first)
    transposed(g_ref, big1t, z_ref, 1)
    sum2.across()
    sum1.across()
    own = send_back(ring4, out1, rims, lambda k, x: dot_rows(thin[k], x))
    sum2.gather()
    sum1.gather()
    add_thin_returned(take_back(ring4, back1, own), z_ref)
    for jp in range(PAIRS):
        gin_ref[:, 128 * jp : 128 * jp + 128] = z_ref[SIDE * jp : SIDE * jp + SIDE, :].astype(BF16)
    sum2.gathered()
    for ring in (ring1, ring2, ring3, ring4):
        ring.finish()
    write_taps(total2, flat, dw2_ref)
    sum1.gathered()
    write_taps(total1, flat, dw1_ref)


def finish_kernel(*refs):
    copies = [pltpu.make_async_copy(refs[n], refs[4 + n], refs[8].at[n]) for n in range(4)]
    for copy in copies:
        copy.start()
    for copy in copies:
        copy.wait()


def local(features, weights_first, weights_second, cotangent, neighbours, turns, corners):
    devices = lax.axis_size("tiles")
    anywhere = pl.BlockSpec(memory_space=pl.ANY)
    inputs = (features[0], weights_first, weights_second, cotangent[0], neighbours, turns, corners)
    inputs = tuple(pltpu.with_memory_space_constraint(x, pltpu.HBM) for x in inputs)
    outputs = (
        jax.ShapeDtypeStruct((PAIRS, PAIRS * CHANS), BF16),
        jax.ShapeDtypeStruct((SIDE, SIDE * CHANS), BF16),
        jax.ShapeDtypeStruct((9, CHANS, CHANS), F32),
        jax.ShapeDtypeStruct((9, CHANS, CHANS), F32),
    )
    slabs = pltpu.VMEM((PAIRS + 2, SIDE, 128), BF16)
    field = pltpu.VMEM((ROWS, 128), F32)
    big = pltpu.VMEM((384, 384), BF16)
    pool = pltpu.VMEM((SLOTS, STRIP, 128), BF16)
    thin_pool = pltpu.VMEM((SLOTS, 128, 128), BF16)
    rows = pltpu.VMEM((4, 48, 128), F32)

    def shares(count):
        return pltpu.VMEM((count, SHARE, 128), F32)

    reduction = [shares(n) for n in (PLANE, PLANE, LEVELS, PLANE)]
    results = pl.pallas_call(
        functools.partial(level_kernel, devices),
        out_shape=tuple(pltpu.VMEM(x.shape, x.dtype) for x in outputs),
        in_specs=[pl.BlockSpec(memory_space=pltpu.HBM)] * 7,
        out_specs=[pl.BlockSpec(memory_space=pltpu.VMEM)] * 4,
        scratch_shapes=[pltpu.VMEM(x.shape, x.dtype) for x in inputs[:4]]
        + [pltpu.SMEM(x.shape, x.dtype) for x in inputs[4:]]
        + [
            slabs, slabs, slabs,
            pltpu.VMEM((ROWS, 384), BF16),
            field, field, field,
            pltpu.VMEM((2, 8 * PAIRS, 128), F32),
            rows, rows, rows,
            pltpu.VMEM((8, 48, 128), F32),
            pltpu.VMEM((8, PAIRS, 384), BF16),
            pltpu.VMEM((3, 128, 384), F32),
            pltpu.VMEM((2 * PLANE * SHARE, 128), F32),
            big, big, big, big,
            pltpu.VMEM((SLOTS, RIMS, STRIP), BF16),
            pltpu.VMEM((SLOTS, STRIP, RIMS), BF16),
            pltpu.VMEM((SLOTS, RIMS, 128), BF16),
            thin_pool, pool, pool, pool, thin_pool, thin_pool,
        ]
        + reduction
        + reduction
        + [
            pltpu.SemaphoreType.DMA((7,)),
            pltpu.SemaphoreType.DMA((8, SLOTS)),
            pltpu.SemaphoreType.DMA((6, PLANE)),
            pltpu.SemaphoreType.DMA((6, PLANE)),
        ],
        compiler_params=pltpu.CompilerParams(
            collective_id=0, has_side_effects=True, vmem_limit_bytes=48 * 2**20
        ),
        name="level",
    )(*inputs)
    pooled, grad, first, second = pl.pallas_call(
        finish_kernel,
        out_shape=outputs,
        in_specs=[anywhere] * 4,
        out_specs=[anywhere] * 4,
        scratch_shapes=[pltpu.SemaphoreType.DMA((4,))],
        compiler_params=pltpu.CompilerParams(vmem_limit_bytes=4 * 2**20),
        name="finish",
    )(*results)
    return pooled[None], grad[None], first, second


def solution(mesh):
    return jax.shard_map(
        local,
        mesh=mesh,
        in_specs=(
            P("tiles", None, None),
            P(),
            P(),
            P("tiles", None, None),
            P("tiles", None),
            P("tiles", None),
            P("tiles", None),
        ),
        out_specs=(P("tiles", None, None), P("tiles", None, None), P(), P()),
        check_vma=False,
    )
```

```python
import functools

import jax
import jax.numpy as jnp
from jax import lax
from jax.experimental import pallas as pl
from jax.experimental.pallas import tpu as pltpu
from jax.sharding import PartitionSpec as P

REACH = 3
SLOTS = 2 * REACH + 1
SIDE = 64
CHANS = 64
PAIRS = SIDE // 2
ROWS = PAIRS * SIDE
STRIP = 4 * SIDE
PLANE = 32
LEVELS = 8
SHARE = 9
CHUNK = 8
RIMS = 4 * SIDE + 32
MESH = pl.DeviceIdType.MESH
BF16 = jnp.bfloat16
F32 = jnp.float32
EDGE_DIRS = ((0, 2), (2, 1), (4, 0), (6, 3))
CORNER_DIRS = ((1, 2, False), (3, 0, False), (5, 0, True), (7, 2, True))
OFFSETS = (1, -1, 2, -2, 3, -3)


def dot(a, b):
    return jnp.dot(a, b, preferred_element_type=F32)


def dot_rows(a, b):
    return lax.dot_general(a, b, (((0,), (0,)), ((), ())), preferred_element_type=F32)


def half_turn(x):
    return pltpu.roll(x, 64, axis=1)


def low_half(x):
    return lax.broadcasted_iota(jnp.int32, x.shape, 1) < 64


def swap(x, y):
    low = low_half(x)
    return jnp.where(low, x, half_turn(y)), jnp.where(low, half_turn(x), y)


def sigmoid(z):
    return 1.0 / (1.0 + jnp.exp(-z))


def hops(steps, size):
    return min(steps, size - steps)


PLANE_STEPS = sorted(
    ((x, y, core) for x in range(4) for y in range(4) for core in range(2) if x or y or core),
    key=lambda step: -(hops(step[0], 4) + hops(step[1], 4)),
)
LEVEL_STEPS = sorted(range(1, LEVELS), key=lambda step: -hops(step, LEVELS))


def plane_members(here):
    x, y, core = here // 8 % 4, here // 2 % 4, here % 2
    xs = [8 * ((x + step) % 4) for step in range(4)]
    ys = [2 * ((y + step) % 4) for step in range(4)]
    cores = [core, 1 - core]
    return [xs[a] + ys[b] + cores[c] for a, b, c in PLANE_STEPS]


def level_members(here):
    return [(here // PLANE + step) % LEVELS for step in LEVEL_STEPS]


def blocks_of(w_ref, dilation, turned):
    taps = [w_ref[t].astype(F32) for t in range(9)]
    if turned:
        taps = [jnp.transpose(tap) for tap in taps]
    zero = jnp.zeros((CHANS, CHANS), F32)
    result = {}
    for a in range(3):
        left, mid, right = taps[3 * a : 3 * a + 3]
        if dilation == 2:
            quads = {d: (w, zero, zero, w) for d, w in ((-1, left), (0, mid), (1, right))}
        else:
            quads = {-1: (zero, zero, left, zero), 0: (mid, left, right, mid), 1: (zero, right, zero, zero)}
        for d, (q00, q01, q10, q11) in quads.items():
            if turned:
                q01, q10 = q10, q01
                d = -d
            block = jnp.concatenate(
                [jnp.concatenate([q00, q01], 1), jnp.concatenate([q10, q11], 1)], 0
            )
            result[a, d] = block.astype(BF16)
    return result


def fill_weights(w_ref, dilation, turned, big):
    for (a, d), block in blocks_of(w_ref, dilation, turned).items():
        big[(d + 1) * 128 : (d + 2) * 128, a * 128 : (a + 1) * 128] = block


def combine(product, dilation, turned):
    rows = product.shape[0]
    up, mid, down = product[:, :128], product[:, 128:256], product[:, 256:]
    if turned:
        up, down = down, up
    i = lax.broadcasted_iota(jnp.int32, (rows, 128), 0) % SIDE
    up = jnp.where(i >= dilation, pltpu.roll(up, dilation, axis=0), 0.0)
    down = jnp.where(i < SIDE - dilation, pltpu.roll(down, rows - dilation, axis=0), 0.0)
    return mid + up + down


def neighbouring(x_ref, start, count):
    parts = [x_ref[pl.ds(start + k, count)].reshape(count * SIDE, 128) for k in range(3)]
    return jnp.concatenate(parts, 1)


def chunks(body):
    def step(c, unused):
        body(c)
        return unused

    lax.fori_loop(0, PAIRS // CHUNK, step, 0)


def chunk_rows(c):
    return pl.ds(pl.multiple_of(c * (CHUNK * SIDE), CHUNK * SIDE), CHUNK * SIDE)


def convolve(x_ref, big, z_ref, dilation):
    def body(c):
        product = dot(neighbouring(x_ref, c * CHUNK, CHUNK), big[...])
        z_ref[chunk_rows(c), :] = combine(product, dilation, False)

    chunks(body)


def edge_row(edge_ref, side, depth):
    return edge_ref[side, pl.ds(depth if side == 0 else 7 - depth, PAIRS, stride=8), :]


def border_of(make):
    rows = {}
    for depth in range(2):
        rows[0, depth] = make(pl.ds(depth, PAIRS, stride=SIDE))
        rows[1, depth] = make(pl.ds(SIDE - 1 - depth, PAIRS, stride=SIDE))
    return rows, make(slice(0, SIDE)), make(slice(ROWS - SIDE, ROWS))


def write_strips(border, strip_ref):
    rows, first, last = border
    strip_ref[0:64] = jnp.concatenate(swap(rows[0, 0], rows[0, 1]), 0).astype(BF16)
    strip_ref[64:128] = first.astype(BF16)
    strip_ref[128:192] = jnp.concatenate(swap(rows[1, 0], rows[1, 1]), 0).astype(BF16)
    strip_ref[192:256] = half_turn(last).astype(BF16)


def write_thin_strips(x_ref, edge_ref, strip_ref):
    strip_ref[0:64] = jnp.concatenate(swap(edge_row(edge_ref, 0, 0), edge_row(edge_ref, 1, 0)), 0).astype(BF16)
    first, last = x_ref[1].astype(F32), x_ref[PAIRS].astype(F32)
    strip_ref[64:128] = jnp.where(low_half(first), first, last).astype(BF16)


def fill_select(here, devices, nbr_ref, turn_ref, corner_ref, select, thin):
    def slot_of(j):
        return lax.rem(nbr_ref[0, j] - here + REACH + devices, devices)

    def columns_of(p, edge, quarter, flips):
        source = lax.rem(edge + 4 - quarter, 4)
        flip = jnp.where(quarter == flips[0], 1, jnp.where(quarter == flips[1], 1, 0))
        p = p + flip * (63 - 2 * p)
        split = (p % 2) * 32 + p // 2
        place = split + lax.rem(source, 2) * (p - split)
        return source * 64 + place, lax.rem(source, 2) * 64 + place

    lane = lax.broadcasted_iota(jnp.int32, (SIDE, STRIP), 1)
    row = lax.broadcasted_iota(jnp.int32, (SIDE, STRIP), 0)
    for n, (j, edge) in enumerate(EDGE_DIRS):
        if edge % 2 == 0:
            cols, thin_cols = columns_of(row % 32 * 2 + row // 32, edge, turn_ref[0, j], (2, 3))
        else:
            cols, thin_cols = columns_of(row, edge, turn_ref[0, j], (1, 2))
        hit = jnp.where(lane == cols, 1.0, 0.0)
        thin_hit = jnp.where(lane == thin_cols, 1.0, 0.0)[:, :128]
        slot = slot_of(j)
        for k in range(SLOTS):
            here_it_is = jnp.where(slot == k, 1.0, 0.0)
            select[k, n * 64 : (n + 1) * 64] = (hit * here_it_is).astype(BF16)
            thin[k, n * 64 : (n + 1) * 64] = (thin_hit * here_it_is).astype(BF16)
    lane = lane[:8]
    row = row[:8]
    hits = []
    for j, edge, last in CORNER_DIRS:
        cols, thin_cols = columns_of(63 - row if last else row, edge, turn_ref[0, j], (2, 3))
        keep = jnp.where(row < 2, 1.0, 0.0) * corner_ref[0, j // 2].astype(F32)
        hit = jnp.where(lane == cols, 1.0, 0.0) * keep
        thin_hit = (jnp.where(lane == thin_cols, 1.0, 0.0) * keep)[:, :128]
        hits.append((hit, thin_hit, slot_of(j)))
    for k in range(SLOTS):
        parts = [hit * jnp.where(slot == k, 1.0, 0.0) for hit, unused, slot in hits]
        select[k, 256:288] = jnp.concatenate(parts, 0).astype(BF16)
        parts = [hit * jnp.where(slot == k, 1.0, 0.0) for unused, hit, slot in hits]
        thin[k, 256:288] = jnp.concatenate(parts, 0).astype(BF16)


def exchange_halves(rims, turn_ref):
    parts = []
    places = [(j, edge, 64) for j, edge in EDGE_DIRS] + [(j, edge, 8) for j, edge, unused in CORNER_DIRS]
    start = 0
    for j, edge, count in places:
        block = rims[start : start + count]
        high = (lax.rem(edge + 4 - turn_ref[0, j], 4) // 2).astype(F32)
        parts.append(block * (1.0 - high) + half_turn(block) * high)
        start += count
    return jnp.concatenate(parts, 0)


def place_rims(rims, x_ref, rows_ref):
    north, east, south, west = (rims[64 * n : 64 * n + 64] for n in range(4))
    x_ref[PAIRS + 1] = east.astype(BF16)
    x_ref[0] = half_turn(west).astype(BF16)
    ne, se, sw, nw = (rims[256 + 8 * n : 264 + 8 * n] for n in range(4))
    for base, strip, right, left in ((0, north, ne, nw), (2, south, se, sw)):
        inner = swap(strip[:32], strip[32:])
        ends = swap(right[0:1], right[1:2])
        starts = swap(left[1:2], left[0:1])
        for d in range(2):
            rows_ref[base + d, 8:40, :] = inner[d]
            rows_ref[base + d, 40:41, :] = ends[d]
            rows_ref[base + d, 7:8, :] = starts[d]


def keep_outer_rows(edge_ref, outer):
    for depth in range(3):
        outer[1 + depth, 8:40, :] = edge_row(edge_ref, 0, depth)
        outer[6 - depth, 8:40, :] = edge_row(edge_ref, 1, depth)


def finish_outer_rows(x_ref, rows_ref, outer, beside):
    outer[0] = rows_ref[0]
    outer[7] = rows_ref[2]
    for place, x in ((7, x_ref[0].astype(F32)), (40, x_ref[PAIRS + 1].astype(F32))):
        for n in range(3):
            outer[1 + n, place : place + 1, :] = x[n : n + 1]
            outer[4 + n, place : place + 1, :] = x[SIDE - 3 + n : SIDE - 2 + n]
    for n in range(8):
        beside[n] = jnp.concatenate([outer[n, 7 + d : 39 + d, :] for d in range(3)], 1).astype(BF16)


def strips_beside(rows_ref):
    parts = []
    for k in range(4):
        parts.append(jnp.concatenate([rows_ref[k, 7 + d : 39 + d, :] for d in range(3)], 1))
    return jnp.concatenate(parts, 0).astype(BF16)


def add_rims(x_ref, beside, big, z_ref, dilation):
    west = combine(dot(x_ref[0], big[0:128, :]), dilation, False)
    z_ref[0:64, :] += west
    east = combine(dot(x_ref[PAIRS + 1], big[256:384, :]), dilation, False)
    z_ref[ROWS - 64 : ROWS, :] += east
    north = dot(beside[:64], big[:, 0:128])
    south = dot(beside[64:], big[:, 256:384])
    for d in range(dilation):
        z_ref[pl.ds(dilation - 1 - d, PAIRS, stride=SIDE), :] += north[32 * d : 32 * d + 32]
        z_ref[pl.ds(SIDE - dilation + d, PAIRS, stride=SIDE), :] += south[32 * d : 32 * d + 32]


def transposed(g_ref, big, z_ref, dilation):
    def body(c):
        product = dot(neighbouring(g_ref, c * CHUNK, CHUNK), big[...])
        z_ref[chunk_rows(c), :] = combine(product, dilation, True)

    chunks(body)


def leaving_rims(border, rows_ref, big, dilation):
    rows, first, last = border
    before = combine(dot(first.astype(BF16), big[256:384, :]), dilation, True)
    after = combine(dot(last.astype(BF16), big[0:128, :]), dilation, True)
    strips, corners = [], []
    gap = jnp.zeros((6, 128), F32)
    for side in range(2):
        lines = []
        for d in range(2):
            if d < dilation:
                rows_ref[2 * side + d, 8:40, :] = rows[side, dilation - 1 - d]
                near = [rows_ref[2 * side + d, 6 + k : 46 + k, :] for k in range(3)]
                near = jnp.concatenate(near, 1).astype(BF16)
                lines.append(dot(near, big[:, 256 * side : 256 * side + 128]))
            else:
                lines.append(jnp.zeros((40, 128), F32))
        strips.append(jnp.concatenate(swap(lines[0][1:33], lines[1][1:33]), 0))
        upper, lower = swap(lines[0][33:34], lines[1][33:34])
        right = jnp.concatenate([upper, lower, gap], 0)
        lower, upper = swap(lines[0][0:1], lines[1][0:1])
        left = jnp.concatenate([upper, lower, gap], 0)
        corners.append((right, left))
    order = [strips[0], after, strips[1], half_turn(before)]
    order += [corners[0][0], corners[1][0], corners[1][1], corners[0][1]]
    return jnp.concatenate(order, 0)


def add_returned(strips, z_ref, dilation):
    z_ref[0:64, :] += strips[64:128]
    z_ref[ROWS - 64 : ROWS, :] += half_turn(strips[192:256])
    top = swap(strips[0:32], strips[32:64])
    bottom = swap(strips[128:160], strips[160:192])
    for d in range(dilation):
        z_ref[pl.ds(d, PAIRS, stride=SIDE), :] += top[d]
        z_ref[pl.ds(SIDE - 1 - d, PAIRS, stride=SIDE), :] += bottom[d]


def add_thin_returned(strips, z_ref):
    top, bottom = swap(strips[0:32], strips[32:64])
    z_ref[pl.ds(0, PAIRS, stride=SIDE), :] += top
    z_ref[pl.ds(SIDE - 1, PAIRS, stride=SIDE), :] += bottom
    sides = strips[64:128]
    low = low_half(sides)
    z_ref[0:64, :] += jnp.where(low, sides, 0.0)
    z_ref[ROWS - 64 : ROWS, :] += jnp.where(low, 0.0, sides)


def row_shifts(g, dilation):
    rows = g.shape[0]
    i = lax.broadcasted_iota(jnp.int32, g.shape, 0) % SIDE
    up = jnp.where(i < SIDE - dilation, pltpu.roll(g, rows - dilation, axis=0), 0.0)
    down = jnp.where(i >= dilation, pltpu.roll(g, dilation, axis=0), 0.0)
    return up.astype(BF16), g.astype(BF16), down.astype(BF16)


def store_shifts(c, g, dilation, shifted):
    for n, moved in enumerate(row_shifts(g, dilation)):
        shifted[chunk_rows(c), 128 * n : 128 * n + 128] = moved


def store_slabs(c, g, g_ref):
    g_ref[pl.ds(c * CHUNK + 1, CHUNK)] = g.astype(BF16).reshape(CHUNK, SIDE, 128)


def inner_products(x_ref, shifted, raw):
    for k in range(3):
        raw[k] = dot_rows(x_ref[k : k + PAIRS].reshape(ROWS, 128), shifted[...])


def strip_products(beside, border, raw):
    rows = border[0]
    zero = jnp.zeros((PAIRS, 128), F32)
    grads = [jnp.concatenate([rows[0, 1 - d], zero, zero], 1) for d in range(2)]
    grads += [jnp.concatenate([zero, zero, rows[1, 1 - d]], 1) for d in range(2)]
    grads = jnp.concatenate(grads, 0).astype(BF16)
    for k in range(3):
        raw[k] += dot_rows(beside[:, 128 * k : 128 * k + 128], grads)


def without_outer_rows(g):
    i = lax.broadcasted_iota(jnp.int32, g.shape, 0) % SIDE
    return jnp.where(i < 2, 0.0, jnp.where(i >= SIDE - 2, 0.0, g))


def border_products(x_ref, outer, border, raw):
    rows, first, last = border
    grads = jnp.concatenate([rows[0, 0], rows[0, 1], rows[1, 1], rows[1, 0]], 0).astype(BF16)
    by_row = []
    for a in range(3):
        near = jnp.concatenate([outer[n] for n in (a, a + 1, a + 4, a + 5)], 0)
        by_row.append(dot_rows(near, grads))
    by_row = jnp.concatenate(by_row, 1)
    left = jnp.concatenate(row_shifts(without_outer_rows(first), 1), 1)
    right = jnp.concatenate(row_shifts(without_outer_rows(last), 1), 1)
    sides = jnp.concatenate([left, right], 0)
    for k in range(3):
        near = jnp.concatenate([x_ref[k], x_ref[PAIRS - 1 + k]], 0)
        raw[k] += by_row[128 * k : 128 * k + 128] + dot_rows(near, sides)


def pack_taps(raw, flat, dilation):
    taps = []
    for a in range(3):
        lanes = slice(128 * a, 128 * a + 128)
        upper = [raw[k, 0:64, lanes] for k in range(3)]
        lower = [raw[k, 64:128, lanes] for k in range(3)]
        if dilation == 2:
            taps += [upper[k] + half_turn(lower[k]) for k in range(3)]
        else:
            taps.append(half_turn(upper[1]) + lower[0])
            taps.append(upper[1] + half_turn(lower[1]))
            taps.append(lower[1] + half_turn(upper[2]))
    low = low_half(taps[0])
    for t in range(0, 8, 2):
        flat[32 * t : 32 * t + 64, :] = jnp.where(low, taps[t], half_turn(taps[t + 1]))
    flat[256:288, :] = jnp.where(low[:32], taps[8][:32], half_turn(taps[8][32:]))


def write_taps(total_ref, flat, out_ref):
    for n in range(PLANE):
        flat[SHARE * n : SHARE * n + SHARE, :] = total_ref[n]
    for t in range(8):
        block = flat[t // 2 * 64 : t // 2 * 64 + 64, :]
        if t % 2 == 1:
            block = half_turn(block)
        out_ref[t] = block[:, :CHANS]
    last = flat[256:288, :]
    out_ref[8] = jnp.concatenate([last, half_turn(last)], 0)[:, :CHANS]


class Ring:
    def __init__(self, peers, source, target, send, recv):
        self.peers, self.source, self.target, self.send, self.recv = peers, source, target, send, recv

    def copy(self, offset):
        return pltpu.make_async_remote_copy(
            src_ref=self.source(offset),
            dst_ref=self.target.at[REACH - offset],
            send_sem=self.send.at[REACH + offset],
            recv_sem=self.recv.at[REACH - offset],
            device_id=(self.peers[offset],),
            device_id_type=MESH,
        )

    def start(self, offset):
        self.copy(offset).start()

    def arrived(self, slot):
        there = self.target.at[slot]
        pltpu.make_async_copy(there, there, self.recv.at[slot]).wait()

    def finish(self):
        for offset in OFFSETS:
            self.copy(offset).wait_send()


class Reduction:
    def __init__(self, here, members, levels, src, plane, level, out, sems):
        self.src, self.plane, self.level, self.out, self.sems = src, plane, level, out, sems
        self.me = here % PLANE
        self.floor = here // PLANE
        self.members = members
        self.in_plane = [here - self.me + member for member in members]
        self.levels = levels
        self.in_column = [PLANE * floor + self.me for floor in levels]

    def copies(self, step):
        result = []
        for n, device in enumerate(self.in_column if step == 1 else self.in_plane):
            if step == 0:
                src, dst = self.src.at[self.members[n]], self.plane.at[n]
            elif step == 1:
                src = dst = self.level.at[self.floor]
            else:
                src = dst = self.out.at[self.me]
            result.append(
                pltpu.make_async_remote_copy(
                    src_ref=src, dst_ref=dst,
                    send_sem=self.sems.at[2 * step, n], recv_sem=self.sems.at[2 * step + 1, n],
                    device_id=(device,), device_id_type=MESH,
                )
            )
        return result

    def start(self, step):
        for copy in self.copies(step):
            copy.start()

    def arrived(self, step):
        places = (
            [self.plane.at[n] for n in range(len(self.members))],
            [self.level.at[n] for n in self.levels],
            [self.out.at[n] for n in self.members],
        )
        for n, there in reversed(list(enumerate(places[step]))):
            pltpu.make_async_copy(there, there, self.sems.at[2 * step + 1, n]).wait()

    def sent(self, step):
        for copy in self.copies(step):
            copy.wait_send()

    def scatter(self, flat):
        for n in range(PLANE):
            self.src[n] = flat[SHARE * n : SHARE * n + SHARE, :]
        self.start(0)
        self.plane[PLANE - 1] = self.src[self.me]

    def across(self):
        self.arrived(0)
        self.level[self.floor] = jnp.sum(self.plane[...], axis=0)
        self.start(1)

    def gather(self):
        self.arrived(1)
        self.out[self.me] = jnp.sum(self.level[...], axis=0)
        self.start(2)

    def gathered(self):
        for step in range(3):
            self.sent(step)
        self.arrived(2)


def level_kernel(
    devices,
    f_hbm, w1_hbm, w2_hbm, cot_hbm, nbr_hbm, turn_hbm, corner_hbm,
    pooled_ref, gin_ref, dw1_ref, dw2_ref,
    f_ref, w1_ref, w2_ref, cot_ref, nbr_ref, turn_ref, corner_ref,
    x1, x2, g_ref, shifted, z_ref, d_ref, act_ref, edge_ref, rows1, rows2, leave, outer, near_outer, raw, flat,
    big1, big1t, big2, big2t, select, select_turned, thin,
    pool1, pool2, out2, back2, out1, back1,
    src2, plane2, level2, total2,
    src1, plane1, level1, total1,
    load_sems, ring_sems, sems2, sems1,
):
    here = lax.axis_index("tiles")
    loads = (
        (f_hbm, f_ref), (nbr_hbm, nbr_ref), (turn_hbm, turn_ref), (corner_hbm, corner_ref),
        (w1_hbm, w1_ref), (w2_hbm, w2_ref), (cot_hbm, cot_ref),
    )
    loads = [pltpu.make_async_copy(a, b, load_sems.at[n]) for n, (a, b) in enumerate(loads)]
    for load in loads:
        load.start()
    barrier = pltpu.get_barrier_semaphore()

    peers = {offset: lax.rem(here + offset + devices, devices) for offset in OFFSETS}
    members, levels = plane_members(here), level_members(here)
    floor = here // PLANE * PLANE
    greeted = [peers[offset] for offset in OFFSETS]
    greeted += [PLANE * level + here % PLANE for level in levels]
    greeted += [floor + member for member in members]
    for device in greeted:
        pl.semaphore_signal(barrier, inc=1, device_id=(device,), device_id_type=MESH)

    ring1 = Ring(peers, lambda o: pool1.at[REACH], pool1, ring_sems.at[0], ring_sems.at[1])
    ring2 = Ring(peers, lambda o: pool2.at[REACH], pool2, ring_sems.at[2], ring_sems.at[3])
    ring3 = Ring(peers, lambda o: out2.at[REACH + o], back2, ring_sems.at[4], ring_sems.at[5])
    ring4 = Ring(peers, lambda o: out1.at[REACH + o], back1, ring_sems.at[6], ring_sems.at[7])
    sum2 = Reduction(here, members, levels, src2, plane2, level2, total2, sems2)
    sum1 = Reduction(here, members, levels, src1, plane1, level1, total1, sems1)

    def collect(ring, pool, chosen):
        rims = dot(chosen[REACH], pool[REACH])
        for offset in OFFSETS:
            slot = REACH - offset
            ring.arrived(slot)
            rims = rims + dot(chosen[slot], pool[slot])
        return rims

    def send_back(ring, out_ref, rims, product):
        rims = rims.astype(BF16)
        for offset in OFFSETS:
            out_ref[REACH + offset] = product(REACH + offset, rims).astype(BF16)
            ring.start(offset)
        return product(REACH, rims)

    def take_back(ring, back_ref, own):
        for offset in OFFSETS:
            ring.arrived(REACH - offset)
            own = own + back_ref[REACH - offset].astype(F32)
        return own

    empty = jnp.zeros((SIDE, 128), BF16)
    for x in (x1, x2, g_ref):
        x[0] = empty
        x[PAIRS + 1] = empty
    leave[...] = jnp.zeros_like(leave)
    loads[0].wait()
    for jp in range(PAIRS):
        x1[jp + 1] = f_ref[:, 128 * jp : 128 * jp + 128]
    for jp in range(PAIRS):
        edge_ref[0, 8 * jp : 8 * jp + 8, :] = f_ref[0:16, 128 * jp : 128 * jp + 128].astype(F32)[:8]
        edge_ref[1, 8 * jp : 8 * jp + 8, :] = f_ref[48:64, 128 * jp : 128 * jp + 128].astype(F32)[8:]
    write_thin_strips(x1, edge_ref, pool1.at[REACH])
    pl.semaphore_wait(barrier, len(greeted))
    for offset in OFFSETS:
        ring1.start(offset)

    for load in loads[1:]:
        load.wait()
    fill_weights(w1_ref, 1, False, big1)
    convolve(x1, big1, z_ref, 1)
    fill_select(here, devices, nbr_ref, turn_ref, corner_ref, select, thin)
    fill_weights(w2_ref, 2, False, big2)
    fill_weights(w2_ref, 2, True, big2t)
    fill_weights(w1_ref, 1, True, big1t)
    low = lax.broadcasted_iota(jnp.int32, (PAIRS, 128), 1) < 64
    for t in range(PAIRS // 2):
        both = cot_ref[:, 128 * t : 128 * t + 128].astype(F32) * 0.25
        turned = half_turn(both)
        for jp, value in ((2 * t, jnp.where(low, both, turned)), (2 * t + 1, jnp.where(low, turned, both))):
            act_ref[pl.ds(SIDE * jp, PAIRS, stride=2), :] = value
            act_ref[pl.ds(SIDE * jp + 1, PAIRS, stride=2), :] = value
    keep_outer_rows(edge_ref, outer)
    for k in range(SLOTS):
        select_turned[k] = jnp.transpose(select[k].astype(F32)).astype(BF16)
    place_rims(exchange_halves(collect(ring1, pool1, thin), turn_ref), x1, rows1)
    add_rims(x1, strips_beside(rows1), big1, z_ref, 1)

    def outer_y(place):
        z = z_ref[place, :]
        return z * sigmoid(z)

    write_strips(border_of(outer_y), pool2.at[REACH])
    for offset in OFFSETS:
        ring2.start(offset)

    def activate(c):
        z = z_ref[chunk_rows(c), :]
        s = sigmoid(z)
        y = z * s
        d_ref[chunk_rows(c), :] = s * (1.0 + z * (1.0 - s))
        store_slabs(c, y, x2)

    chunks(activate)
    finish_outer_rows(x1, rows1, outer, near_outer)

    convolve(x2, big2, z_ref, 2)
    place_rims(collect(ring2, pool2, select), x2, rows2)
    beside2 = strips_beside(rows2)
    add_rims(x2, beside2, big2, z_ref, 2)

    def second_gradient(place):
        z = z_ref[place, :]
        s = sigmoid(z)
        g = act_ref[place, :] * s * (1.0 + z * (1.0 - s))
        return g.astype(BF16).astype(F32)

    border2 = border_of(second_gradient)
    rims = leaving_rims(border2, leave, big2t, 2)
    own = send_back(ring3, out2, rims, lambda k, x: dot(select_turned[k], x))

    def second(c):
        z = z_ref[chunk_rows(c), :]
        s = sigmoid(z)
        z_ref[chunk_rows(c), :] = z * s * 0.25
        g = (act_ref[chunk_rows(c), :] * s * (1.0 + z * (1.0 - s))).astype(BF16).astype(F32)
        store_slabs(c, g, g_ref)
        store_shifts(c, g, 2, shifted)

    chunks(second)
    inner_products(x2, shifted, raw)
    strip_products(beside2, border2, raw)
    pack_taps(raw, flat, 2)
    for t in range(PAIRS // 2):
        sums = []
        for jp in (2 * t, 2 * t + 1):
            v = z_ref[pl.ds(SIDE * jp, PAIRS, stride=2), :] + z_ref[pl.ds(SIDE * jp + 1, PAIRS, stride=2), :]
            sums.append(v + half_turn(v))
        pooled_ref[:, 128 * t : 128 * t + 128] = jnp.where(low, sums[0], sums[1]).astype(BF16)
    transposed(g_ref, big2t, z_ref, 2)

    def inside(c):
        g = without_outer_rows(z_ref[chunk_rows(c), :] * d_ref[chunk_rows(c), :])
        store_shifts(c, g, 1, shifted)

    chunks(inside)
    shifted[0:SIDE] = jnp.zeros((SIDE, 384), BF16)
    shifted[ROWS - SIDE : ROWS] = jnp.zeros((SIDE, 384), BF16)
    inner_products(x1, shifted, raw)
    sum2.scatter(flat)
    add_returned(take_back(ring3, back2, own), z_ref, 2)

    def first_gradient(place):
        return (z_ref[place, :] * d_ref[place, :]).astype(BF16).astype(F32)

    border1 = border_of(first_gradient)
    border_products(x1, near_outer, border1, raw)
    pack_taps(raw, flat, 1)
    sum1.scatter(flat)
    rims = exchange_halves(leaving_rims(border1, leave, big1t, 1), turn_ref)

    def first(c):
        store_slabs(c, z_ref[chunk_rows(c), :] * d_ref[chunk_rows(c), :], g_ref)

    chunks(first)
    transposed(g_ref, big1t, z_ref, 1)
    sum2.across()
    sum1.across()
    own = send_back(ring4, out1, rims, lambda k, x: dot_rows(thin[k], x))
    sum2.gather()
    sum1.gather()
    add_thin_returned(take_back(ring4, back1, own), z_ref)
    for jp in range(PAIRS):
        gin_ref[:, 128 * jp : 128 * jp + 128] = z_ref[SIDE * jp : SIDE * jp + SIDE, :].astype(BF16)
    sum2.gathered()
    for ring in (ring1, ring2, ring3, ring4):
        ring.finish()
    write_taps(total2, flat, dw2_ref)
    sum1.gathered()
    write_taps(total1, flat, dw1_ref)


def finish_kernel(*refs):
    copies = [pltpu.make_async_copy(refs[n], refs[4 + n], refs[8].at[n]) for n in range(4)]
    for copy in copies:
        copy.start()
    for copy in copies:
        copy.wait()


def local(features, weights_first, weights_second, cotangent, neighbours, turns, corners):
    devices = lax.axis_size("tiles")
    anywhere = pl.BlockSpec(memory_space=pl.ANY)
    inputs = (features[0], weights_first, weights_second, cotangent[0], neighbours, turns, corners)
    inputs = tuple(pltpu.with_memory_space_constraint(x, pltpu.HBM) for x in inputs)
    outputs = (
        jax.ShapeDtypeStruct((PAIRS, PAIRS * CHANS), BF16),
        jax.ShapeDtypeStruct((SIDE, SIDE * CHANS), BF16),
        jax.ShapeDtypeStruct((9, CHANS, CHANS), F32),
        jax.ShapeDtypeStruct((9, CHANS, CHANS), F32),
    )
    slabs = pltpu.VMEM((PAIRS + 2, SIDE, 128), BF16)
    field = pltpu.VMEM((ROWS, 128), F32)
    big = pltpu.VMEM((384, 384), BF16)
    pool = pltpu.VMEM((SLOTS, STRIP, 128), BF16)
    thin_pool = pltpu.VMEM((SLOTS, 128, 128), BF16)
    rows = pltpu.VMEM((4, 48, 128), F32)

    def shares(count):
        return pltpu.VMEM((count, SHARE, 128), F32)

    reduction = [shares(n) for n in (PLANE, PLANE, LEVELS, PLANE)]
    results = pl.pallas_call(
        functools.partial(level_kernel, devices),
        out_shape=tuple(pltpu.VMEM(x.shape, x.dtype) for x in outputs),
        in_specs=[pl.BlockSpec(memory_space=pltpu.HBM)] * 7,
        out_specs=[pl.BlockSpec(memory_space=pltpu.VMEM)] * 4,
        scratch_shapes=[pltpu.VMEM(x.shape, x.dtype) for x in inputs[:4]]
        + [pltpu.SMEM(x.shape, x.dtype) for x in inputs[4:]]
        + [
            slabs, slabs, slabs,
            pltpu.VMEM((ROWS, 384), BF16),
            field, field, field,
            pltpu.VMEM((2, 8 * PAIRS, 128), F32),
            rows, rows, rows,
            pltpu.VMEM((8, 48, 128), F32),
            pltpu.VMEM((8, PAIRS, 384), BF16),
            pltpu.VMEM((3, 128, 384), F32),
            pltpu.VMEM((2 * PLANE * SHARE, 128), F32),
            big, big, big, big,
            pltpu.VMEM((SLOTS, RIMS, STRIP), BF16),
            pltpu.VMEM((SLOTS, STRIP, RIMS), BF16),
            pltpu.VMEM((SLOTS, RIMS, 128), BF16),
            thin_pool, pool, pool, pool, thin_pool, thin_pool,
        ]
        + reduction
        + reduction
        + [
            pltpu.SemaphoreType.DMA((7,)),
            pltpu.SemaphoreType.DMA((8, SLOTS)),
            pltpu.SemaphoreType.DMA((6, PLANE)),
            pltpu.SemaphoreType.DMA((6, PLANE)),
        ],
        compiler_params=pltpu.CompilerParams(
            collective_id=0, has_side_effects=True, vmem_limit_bytes=48 * 2**20
        ),
        name="level",
    )(*inputs)
    pooled, grad, first, second = pl.pallas_call(
        finish_kernel,
        out_shape=outputs,
        in_specs=[anywhere] * 4,
        out_specs=[anywhere] * 4,
        scratch_shapes=[pltpu.SemaphoreType.DMA((4,))],
        compiler_params=pltpu.CompilerParams(vmem_limit_bytes=4 * 2**20),
        name="finish",
    )(*results)
    return pooled[None], grad[None], first, second


def solution(mesh):
    return jax.shard_map(
        local,
        mesh=mesh,
        in_specs=(
            P("tiles", None, None),
            P(),
            P(),
            P("tiles", None, None),
            P("tiles", None),
            P("tiles", None),
            P("tiles", None),
        ),
        out_specs=(P("tiles", None, None), P("tiles", None, None), P(), P()),
        check_vma=False,
    )
```

```python
import functools

import jax
import jax.numpy as jnp
from jax import lax
from jax.experimental import pallas as pl
from jax.experimental.pallas import tpu as pltpu
from jax.sharding import PartitionSpec as P

REACH = 3
SLOTS = 2 * REACH + 1
SIDE = 64
CHANS = 64
PAIRS = SIDE // 2
ROWS = PAIRS * SIDE
STRIP = 4 * SIDE
PLANE = 32
LEVELS = 8
SHARE = 9
CHUNK = 8
RIMS = 4 * SIDE + 32
MESH = pl.DeviceIdType.MESH
BF16 = jnp.bfloat16
F32 = jnp.float32
EDGE_DIRS = ((0, 2), (2, 1), (4, 0), (6, 3))
CORNER_DIRS = ((1, 2, False), (3, 0, False), (5, 0, True), (7, 2, True))
OFFSETS = (1, -1, 2, -2, 3, -3)


def dot(a, b):
    return jnp.dot(a, b, preferred_element_type=F32)


def dot_rows(a, b):
    return lax.dot_general(a, b, (((0,), (0,)), ((), ())), preferred_element_type=F32)


def half_turn(x):
    return pltpu.roll(x, 64, axis=1)


def low_half(x):
    return lax.broadcasted_iota(jnp.int32, x.shape, 1) < 64


def swap(x, y):
    low = low_half(x)
    return jnp.where(low, x, half_turn(y)), jnp.where(low, half_turn(x), y)


def sigmoid(z):
    return 1.0 / (1.0 + jnp.exp(-z))


def hops(steps, size):
    return min(steps, size - steps)


PLANE_STEPS = sorted(
    ((x, y, core) for x in range(4) for y in range(4) for core in range(2) if x or y or core),
    key=lambda step: -(hops(step[0], 4) + hops(step[1], 4)),
)
LEVEL_STEPS = sorted(range(1, LEVELS), key=lambda step: -hops(step, LEVELS))


def plane_members(here):
    x, y, core = here // 8 % 4, here // 2 % 4, here % 2
    xs = [8 * ((x + step) % 4) for step in range(4)]
    ys = [2 * ((y + step) % 4) for step in range(4)]
    cores = [core, 1 - core]
    return [xs[a] + ys[b] + cores[c] for a, b, c in PLANE_STEPS]


def level_members(here):
    return [(here // PLANE + step) % LEVELS for step in LEVEL_STEPS]


def blocks_of(w_ref, dilation, turned):
    taps = [w_ref[t].astype(F32) for t in range(9)]
    if turned:
        taps = [jnp.transpose(tap) for tap in taps]
    zero = jnp.zeros((CHANS, CHANS), F32)
    result = {}
    for a in range(3):
        left, mid, right = taps[3 * a : 3 * a + 3]
        if dilation == 2:
            quads = {d: (w, zero, zero, w) for d, w in ((-1, left), (0, mid), (1, right))}
        else:
            quads = {-1: (zero, zero, left, zero), 0: (mid, left, right, mid), 1: (zero, right, zero, zero)}
        for d, (q00, q01, q10, q11) in quads.items():
            if turned:
                q01, q10 = q10, q01
                d = -d
            block = jnp.concatenate(
                [jnp.concatenate([q00, q01], 1), jnp.concatenate([q10, q11], 1)], 0
            )
            result[a, d] = block.astype(BF16)
    return result


def fill_weights(w_ref, dilation, turned, big):
    for (a, d), block in blocks_of(w_ref, dilation, turned).items():
        big[(d + 1) * 128 : (d + 2) * 128, a * 128 : (a + 1) * 128] = block


def combine(product, dilation, turned):
    rows = product.shape[0]
    up, mid, down = product[:, :128], product[:, 128:256], product[:, 256:]
    if turned:
        up, down = down, up
    i = lax.broadcasted_iota(jnp.int32, (rows, 128), 0) % SIDE
    up = jnp.where(i >= dilation, pltpu.roll(up, dilation, axis=0), 0.0)
    down = jnp.where(i < SIDE - dilation, pltpu.roll(down, rows - dilation, axis=0), 0.0)
    return mid + up + down


def neighbouring(x_ref, start, count):
    parts = [x_ref[pl.ds(start + k, count)].reshape(count * SIDE, 128) for k in range(3)]
    return jnp.concatenate(parts, 1)


def chunks(body):
    def step(c, unused):
        body(c)
        return unused

    lax.fori_loop(0, PAIRS // CHUNK, step, 0)


def chunk_rows(c):
    return pl.ds(pl.multiple_of(c * (CHUNK * SIDE), CHUNK * SIDE), CHUNK * SIDE)


def convolve(x_ref, big, z_ref, dilation):
    def body(c):
        product = dot(neighbouring(x_ref, c * CHUNK, CHUNK), big[...])
        z_ref[chunk_rows(c), :] = combine(product, dilation, False)

    chunks(body)


def edge_row(edge_ref, side, depth):
    return edge_ref[side, pl.ds(depth if side == 0 else 7 - depth, PAIRS, stride=8), :]


def border_of(make):
    rows = {}
    for depth in range(2):
        rows[0, depth] = make(pl.ds(depth, PAIRS, stride=SIDE))
        rows[1, depth] = make(pl.ds(SIDE - 1 - depth, PAIRS, stride=SIDE))
    return rows, make(slice(0, SIDE)), make(slice(ROWS - SIDE, ROWS))


def write_strips(border, strip_ref):
    rows, first, last = border
    strip_ref[0:64] = jnp.concatenate(swap(rows[0, 0], rows[0, 1]), 0).astype(BF16)
    strip_ref[64:128] = first.astype(BF16)
    strip_ref[128:192] = jnp.concatenate(swap(rows[1, 0], rows[1, 1]), 0).astype(BF16)
    strip_ref[192:256] = half_turn(last).astype(BF16)


def write_thin_strips(x_ref, edge_ref, strip_ref):
    strip_ref[0:64] = jnp.concatenate(swap(edge_row(edge_ref, 0, 0), edge_row(edge_ref, 1, 0)), 0).astype(BF16)
    first, last = x_ref[1].astype(F32), x_ref[PAIRS].astype(F32)
    strip_ref[64:128] = jnp.where(low_half(first), first, last).astype(BF16)


def fill_select(here, devices, nbr_ref, turn_ref, corner_ref, select, thin):
    def slot_of(j):
        return lax.rem(nbr_ref[0, j] - here + REACH + devices, devices)

    def columns_of(p, edge, quarter, flips):
        source = lax.rem(edge + 4 - quarter, 4)
        flip = jnp.where(quarter == flips[0], 1, jnp.where(quarter == flips[1], 1, 0))
        p = p + flip * (63 - 2 * p)
        split = (p % 2) * 32 + p // 2
        place = split + lax.rem(source, 2) * (p - split)
        return source * 64 + place, lax.rem(source, 2) * 64 + place

    lane = lax.broadcasted_iota(jnp.int32, (SIDE, STRIP), 1)
    row = lax.broadcasted_iota(jnp.int32, (SIDE, STRIP), 0)
    for n, (j, edge) in enumerate(EDGE_DIRS):
        if edge % 2 == 0:
            cols, thin_cols = columns_of(row % 32 * 2 + row // 32, edge, turn_ref[0, j], (2, 3))
        else:
            cols, thin_cols = columns_of(row, edge, turn_ref[0, j], (1, 2))
        hit = jnp.where(lane == cols, 1.0, 0.0)
        thin_hit = jnp.where(lane == thin_cols, 1.0, 0.0)[:, :128]
        slot = slot_of(j)
        for k in range(SLOTS):
            here_it_is = jnp.where(slot == k, 1.0, 0.0)
            select[k, n * 64 : (n + 1) * 64] = (hit * here_it_is).astype(BF16)
            thin[k, n * 64 : (n + 1) * 64] = (thin_hit * here_it_is).astype(BF16)
    lane = lane[:8]
    row = row[:8]
    hits = []
    for j, edge, last in CORNER_DIRS:
        cols, thin_cols = columns_of(63 - row if last else row, edge, turn_ref[0, j], (2, 3))
        keep = jnp.where(row < 2, 1.0, 0.0) * corner_ref[0, j // 2].astype(F32)
        hit = jnp.where(lane == cols, 1.0, 0.0) * keep
        thin_hit = (jnp.where(lane == thin_cols, 1.0, 0.0) * keep)[:, :128]
        hits.append((hit, thin_hit, slot_of(j)))
    for k in range(SLOTS):
        parts = [hit * jnp.where(slot == k, 1.0, 0.0) for hit, unused, slot in hits]
        select[k, 256:288] = jnp.concatenate(parts, 0).astype(BF16)
        parts = [hit * jnp.where(slot == k, 1.0, 0.0) for unused, hit, slot in hits]
        thin[k, 256:288] = jnp.concatenate(parts, 0).astype(BF16)


def exchange_halves(rims, turn_ref):
    parts = []
    places = [(j, edge, 64) for j, edge in EDGE_DIRS] + [(j, edge, 8) for j, edge, unused in CORNER_DIRS]
    start = 0
    for j, edge, count in places:
        block = rims[start : start + count]
        high = (lax.rem(edge + 4 - turn_ref[0, j], 4) // 2).astype(F32)
        parts.append(block * (1.0 - high) + half_turn(block) * high)
        start += count
    return jnp.concatenate(parts, 0)


def place_rims(rims, x_ref, rows_ref):
    north, east, south, west = (rims[64 * n : 64 * n + 64] for n in range(4))
    x_ref[PAIRS + 1] = east.astype(BF16)
    x_ref[0] = half_turn(west).astype(BF16)
    ne, se, sw, nw = (rims[256 + 8 * n : 264 + 8 * n] for n in range(4))
    for base, strip, right, left in ((0, north, ne, nw), (2, south, se, sw)):
        inner = swap(strip[:32], strip[32:])
        ends = swap(right[0:1], right[1:2])
        starts = swap(left[1:2], left[0:1])
        for d in range(2):
            rows_ref[base + d, 8:40, :] = inner[d]
            rows_ref[base + d, 40:41, :] = ends[d]
            rows_ref[base + d, 7:8, :] = starts[d]


def keep_outer_rows(edge_ref, outer):
    for depth in range(3):
        outer[1 + depth, 8:40, :] = edge_row(edge_ref, 0, depth)
        outer[6 - depth, 8:40, :] = edge_row(edge_ref, 1, depth)


def finish_outer_rows(x_ref, rows_ref, outer, beside):
    outer[0] = rows_ref[0]
    outer[7] = rows_ref[2]
    for place, x in ((7, x_ref[0].astype(F32)), (40, x_ref[PAIRS + 1].astype(F32))):
        for n in range(3):
            outer[1 + n, place : place + 1, :] = x[n : n + 1]
            outer[4 + n, place : place + 1, :] = x[SIDE - 3 + n : SIDE - 2 + n]
    for n in range(8):
        beside[n] = jnp.concatenate([outer[n, 7 + d : 39 + d, :] for d in range(3)], 1).astype(BF16)


def strips_beside(rows_ref):
    parts = []
    for k in range(4):
        parts.append(jnp.concatenate([rows_ref[k, 7 + d : 39 + d, :] for d in range(3)], 1))
    return jnp.concatenate(parts, 0).astype(BF16)


def add_rims(x_ref, beside, big, z_ref, dilation):
    west = combine(dot(x_ref[0], big[0:128, :]), dilation, False)
    z_ref[0:64, :] += west
    east = combine(dot(x_ref[PAIRS + 1], big[256:384, :]), dilation, False)
    z_ref[ROWS - 64 : ROWS, :] += east
    north = dot(beside[:64], big[:, 0:128])
    south = dot(beside[64:], big[:, 256:384])
    for d in range(dilation):
        z_ref[pl.ds(dilation - 1 - d, PAIRS, stride=SIDE), :] += north[32 * d : 32 * d + 32]
        z_ref[pl.ds(SIDE - dilation + d, PAIRS, stride=SIDE), :] += south[32 * d : 32 * d + 32]


def transposed(g_ref, big, z_ref, dilation):
    def body(c):
        product = dot(neighbouring(g_ref, c * CHUNK, CHUNK), big[...])
        z_ref[chunk_rows(c), :] = combine(product, dilation, True)

    chunks(body)


def leaving_rims(border, rows_ref, big, dilation):
    rows, first, last = border
    before = combine(dot(first.astype(BF16), big[256:384, :]), dilation, True)
    after = combine(dot(last.astype(BF16), big[0:128, :]), dilation, True)
    strips, corners = [], []
    gap = jnp.zeros((6, 128), F32)
    for side in range(2):
        lines = []
        for d in range(2):
            if d < dilation:
                rows_ref[2 * side + d, 8:40, :] = rows[side, dilation - 1 - d]
                near = [rows_ref[2 * side + d, 6 + k : 46 + k, :] for k in range(3)]
                near = jnp.concatenate(near, 1).astype(BF16)
                lines.append(dot(near, big[:, 256 * side : 256 * side + 128]))
            else:
                lines.append(jnp.zeros((40, 128), F32))
        strips.append(jnp.concatenate(swap(lines[0][1:33], lines[1][1:33]), 0))
        upper, lower = swap(lines[0][33:34], lines[1][33:34])
        right = jnp.concatenate([upper, lower, gap], 0)
        lower, upper = swap(lines[0][0:1], lines[1][0:1])
        left = jnp.concatenate([upper, lower, gap], 0)
        corners.append((right, left))
    order = [strips[0], after, strips[1], half_turn(before)]
    order += [corners[0][0], corners[1][0], corners[1][1], corners[0][1]]
    return jnp.concatenate(order, 0)


def add_returned(strips, z_ref, dilation):
    z_ref[0:64, :] += strips[64:128]
    z_ref[ROWS - 64 : ROWS, :] += half_turn(strips[192:256])
    top = swap(strips[0:32], strips[32:64])
    bottom = swap(strips[128:160], strips[160:192])
    for d in range(dilation):
        z_ref[pl.ds(d, PAIRS, stride=SIDE), :] += top[d]
        z_ref[pl.ds(SIDE - 1 - d, PAIRS, stride=SIDE), :] += bottom[d]


def add_thin_returned(strips, z_ref):
    top, bottom = swap(strips[0:32], strips[32:64])
    z_ref[pl.ds(0, PAIRS, stride=SIDE), :] += top
    z_ref[pl.ds(SIDE - 1, PAIRS, stride=SIDE), :] += bottom
    sides = strips[64:128]
    low = low_half(sides)
    z_ref[0:64, :] += jnp.where(low, sides, 0.0)
    z_ref[ROWS - 64 : ROWS, :] += jnp.where(low, 0.0, sides)


def row_shifts(g, dilation):
    rows = g.shape[0]
    i = lax.broadcasted_iota(jnp.int32, g.shape, 0) % SIDE
    up = jnp.where(i < SIDE - dilation, pltpu.roll(g, rows - dilation, axis=0), 0.0)
    down = jnp.where(i >= dilation, pltpu.roll(g, dilation, axis=0), 0.0)
    return up.astype(BF16), g.astype(BF16), down.astype(BF16)


def store_shifts(c, g, dilation, shifted):
    for n, moved in enumerate(row_shifts(g, dilation)):
        shifted[chunk_rows(c), 128 * n : 128 * n + 128] = moved


def store_slabs(c, g, g_ref):
    g_ref[pl.ds(c * CHUNK + 1, CHUNK)] = g.astype(BF16).reshape(CHUNK, SIDE, 128)


def inner_products(x_ref, shifted, raw):
    for k in range(3):
        raw[k] = dot_rows(x_ref[k : k + PAIRS].reshape(ROWS, 128), shifted[...])


def strip_products(beside, border, raw):
    rows = border[0]
    zero = jnp.zeros((PAIRS, 128), F32)
    grads = [jnp.concatenate([rows[0, 1 - d], zero, zero], 1) for d in range(2)]
    grads += [jnp.concatenate([zero, zero, rows[1, 1 - d]], 1) for d in range(2)]
    grads = jnp.concatenate(grads, 0).astype(BF16)
    for k in range(3):
        raw[k] += dot_rows(beside[:, 128 * k : 128 * k + 128], grads)


def without_outer_rows(g):
    i = lax.broadcasted_iota(jnp.int32, g.shape, 0) % SIDE
    return jnp.where(i < 2, 0.0, jnp.where(i >= SIDE - 2, 0.0, g))


def border_products(x_ref, outer, border, raw):
    rows, first, last = border
    grads = jnp.concatenate([rows[0, 0], rows[0, 1], rows[1, 1], rows[1, 0]], 0).astype(BF16)
    by_row = []
    for a in range(3):
        near = jnp.concatenate([outer[n] for n in (a, a + 1, a + 4, a + 5)], 0)
        by_row.append(dot_rows(near, grads))
    by_row = jnp.concatenate(by_row, 1)
    left = jnp.concatenate(row_shifts(without_outer_rows(first), 1), 1)
    right = jnp.concatenate(row_shifts(without_outer_rows(last), 1), 1)
    sides = jnp.concatenate([left, right], 0)
    for k in range(3):
        near = jnp.concatenate([x_ref[k], x_ref[PAIRS - 1 + k]], 0)
        raw[k] += by_row[128 * k : 128 * k + 128] + dot_rows(near, sides)


def pack_taps(raw, flat, dilation):
    taps = []
    for a in range(3):
        lanes = slice(128 * a, 128 * a + 128)
        upper = [raw[k, 0:64, lanes] for k in range(3)]
        lower = [raw[k, 64:128, lanes] for k in range(3)]
        if dilation == 2:
            taps += [upper[k] + half_turn(lower[k]) for k in range(3)]
        else:
            taps.append(half_turn(upper[1]) + lower[0])
            taps.append(upper[1] + half_turn(lower[1]))
            taps.append(lower[1] + half_turn(upper[2]))
    low = low_half(taps[0])
    for t in range(0, 8, 2):
        flat[32 * t : 32 * t + 64, :] = jnp.where(low, taps[t], half_turn(taps[t + 1]))
    flat[256:288, :] = jnp.where(low[:32], taps[8][:32], half_turn(taps[8][32:]))


def write_taps(total_ref, flat, out_ref):
    for n in range(PLANE):
        flat[SHARE * n : SHARE * n + SHARE, :] = total_ref[n]
    for t in range(8):
        block = flat[t // 2 * 64 : t // 2 * 64 + 64, :]
        if t % 2 == 1:
            block = half_turn(block)
        out_ref[t] = block[:, :CHANS]
    last = flat[256:288, :]
    out_ref[8] = jnp.concatenate([last, half_turn(last)], 0)[:, :CHANS]


class Ring:
    def __init__(self, peers, source, target, send, recv):
        self.peers, self.source, self.target, self.send, self.recv = peers, source, target, send, recv

    def copy(self, offset):
        return pltpu.make_async_remote_copy(
            src_ref=self.source(offset),
            dst_ref=self.target.at[REACH - offset],
            send_sem=self.send.at[REACH + offset],
            recv_sem=self.recv.at[REACH - offset],
            device_id=(self.peers[offset],),
            device_id_type=MESH,
        )

    def start(self, offset):
        self.copy(offset).start()

    def arrived(self, slot):
        there = self.target.at[slot]
        pltpu.make_async_copy(there, there, self.recv.at[slot]).wait()

    def finish(self):
        for offset in OFFSETS:
            self.copy(offset).wait_send()


class Reduction:
    def __init__(self, here, members, levels, src, plane, level, out, sems):
        self.src, self.plane, self.level, self.out, self.sems = src, plane, level, out, sems
        self.me = here % PLANE
        self.floor = here // PLANE
        self.members = members
        self.in_plane = [here - self.me + member for member in members]
        self.levels = levels
        self.in_column = [PLANE * floor + self.me for floor in levels]

    def copies(self, step):
        result = []
        for n, device in enumerate(self.in_column if step == 1 else self.in_plane):
            if step == 0:
                src, dst = self.src.at[self.members[n]], self.plane.at[n]
            elif step == 1:
                src = dst = self.level.at[self.floor]
            else:
                src = dst = self.out.at[self.me]
            result.append(
                pltpu.make_async_remote_copy(
                    src_ref=src, dst_ref=dst,
                    send_sem=self.sems.at[2 * step, n], recv_sem=self.sems.at[2 * step + 1, n],
                    device_id=(device,), device_id_type=MESH,
                )
            )
        return result

    def start(self, step):
        for copy in self.copies(step):
            copy.start()

    def arrived(self, step):
        places = (
            [self.plane.at[n] for n in range(len(self.members))],
            [self.level.at[n] for n in self.levels],
            [self.out.at[n] for n in self.members],
        )
        for n, there in reversed(list(enumerate(places[step]))):
            pltpu.make_async_copy(there, there, self.sems.at[2 * step + 1, n]).wait()

    def sent(self, step):
        for copy in self.copies(step):
            copy.wait_send()

    def scatter(self, flat):
        for n in range(PLANE):
            self.src[n] = flat[SHARE * n : SHARE * n + SHARE, :]
        self.start(0)
        self.plane[PLANE - 1] = self.src[self.me]

    def across(self):
        self.arrived(0)
        self.level[self.floor] = jnp.sum(self.plane[...], axis=0)
        self.start(1)

    def gather(self):
        self.arrived(1)
        self.out[self.me] = jnp.sum(self.level[...], axis=0)
        self.start(2)

    def gathered(self):
        for step in range(3):
            self.sent(step)
        self.arrived(2)


def level_kernel(
    devices,
    f_hbm, w1_hbm, w2_hbm, cot_hbm, nbr_hbm, turn_hbm, corner_hbm,
    pooled_ref, gin_ref, dw1_ref, dw2_ref,
    f_ref, w1_ref, w2_ref, cot_ref, nbr_ref, turn_ref, corner_ref,
    x1, x2, g_ref, shifted, z_ref, d_ref, act_ref, edge_ref, rows1, rows2, leave, outer, near_outer, raw, flat,
    big1, big1t, big2, big2t, select, select_turned, thin,
    pool1, pool2, out2, back2, out1, back1,
    src2, plane2, level2, total2,
    src1, plane1, level1, total1,
    load_sems, ring_sems, sems2, sems1,
):
    here = lax.axis_index("tiles")
    loads = (
        (f_hbm, f_ref), (nbr_hbm, nbr_ref), (turn_hbm, turn_ref), (corner_hbm, corner_ref),
        (w1_hbm, w1_ref), (w2_hbm, w2_ref), (cot_hbm, cot_ref),
    )
    loads = [pltpu.make_async_copy(a, b, load_sems.at[n]) for n, (a, b) in enumerate(loads)]
    for load in loads:
        load.start()
    barrier = pltpu.get_barrier_semaphore()

    peers = {offset: lax.rem(here + offset + devices, devices) for offset in OFFSETS}
    members, levels = plane_members(here), level_members(here)
    floor = here // PLANE * PLANE
    greeted = [peers[offset] for offset in OFFSETS]
    greeted += [PLANE * level + here % PLANE for level in levels]
    greeted += [floor + member for member in members]
    for device in greeted:
        pl.semaphore_signal(barrier, inc=1, device_id=(device,), device_id_type=MESH)

    ring1 = Ring(peers, lambda o: pool1.at[REACH], pool1, ring_sems.at[0], ring_sems.at[1])
    ring2 = Ring(peers, lambda o: pool2.at[REACH], pool2, ring_sems.at[2], ring_sems.at[3])
    ring3 = Ring(peers, lambda o: out2.at[REACH + o], back2, ring_sems.at[4], ring_sems.at[5])
    ring4 = Ring(peers, lambda o: out1.at[REACH + o], back1, ring_sems.at[6], ring_sems.at[7])
    sum2 = Reduction(here, members, levels, src2, plane2, level2, total2, sems2)
    sum1 = Reduction(here, members, levels, src1, plane1, level1, total1, sems1)

    def collect(ring, pool, chosen):
        rims = dot(chosen[REACH], pool[REACH])
        for offset in OFFSETS:
            slot = REACH - offset
            ring.arrived(slot)
            rims = rims + dot(chosen[slot], pool[slot])
        return rims

    def send_back(ring, out_ref, rims, product):
        rims = rims.astype(BF16)
        for offset in OFFSETS:
            out_ref[REACH + offset] = product(REACH + offset, rims).astype(BF16)
            ring.start(offset)
        return product(REACH, rims)

    def take_back(ring, back_ref, own):
        for offset in OFFSETS:
            ring.arrived(REACH - offset)
            own = own + back_ref[REACH - offset].astype(F32)
        return own

    empty = jnp.zeros((SIDE, 128), BF16)
    for x in (x1, x2, g_ref):
        x[0] = empty
        x[PAIRS + 1] = empty
    leave[...] = jnp.zeros_like(leave)
    loads[0].wait()
    for jp in (0, PAIRS - 1):
        x1[jp + 1] = f_ref[:, 128 * jp : 128 * jp + 128]
    for jp in range(PAIRS):
        edge_ref[0, 8 * jp : 8 * jp + 8, :] = f_ref[0:16, 128 * jp : 128 * jp + 128].astype(F32)[:8]
        edge_ref[1, 8 * jp : 8 * jp + 8, :] = f_ref[48:64, 128 * jp : 128 * jp + 128].astype(F32)[8:]
    write_thin_strips(x1, edge_ref, pool1.at[REACH])
    pl.semaphore_wait(barrier, len(greeted))
    for offset in OFFSETS:
        ring1.start(offset)
    for jp in range(1, PAIRS - 1):
        x1[jp + 1] = f_ref[:, 128 * jp : 128 * jp + 128]

    for load in loads[1:]:
        load.wait()
    fill_weights(w1_ref, 1, False, big1)
    convolve(x1, big1, z_ref, 1)
    fill_select(here, devices, nbr_ref, turn_ref, corner_ref, select, thin)
    fill_weights(w2_ref, 2, False, big2)
    fill_weights(w2_ref, 2, True, big2t)
    fill_weights(w1_ref, 1, True, big1t)
    low = lax.broadcasted_iota(jnp.int32, (PAIRS, 128), 1) < 64
    for t in range(PAIRS // 2):
        both = cot_ref[:, 128 * t : 128 * t + 128].astype(F32) * 0.25
        turned = half_turn(both)
        for jp, value in ((2 * t, jnp.where(low, both, turned)), (2 * t + 1, jnp.where(low, turned, both))):
            act_ref[pl.ds(SIDE * jp, PAIRS, stride=2), :] = value
            act_ref[pl.ds(SIDE * jp + 1, PAIRS, stride=2), :] = value
    keep_outer_rows(edge_ref, outer)
    for k in range(SLOTS):
        select_turned[k] = jnp.transpose(select[k].astype(F32)).astype(BF16)
    place_rims(exchange_halves(collect(ring1, pool1, thin), turn_ref), x1, rows1)
    add_rims(x1, strips_beside(rows1), big1, z_ref, 1)

    def outer_y(place):
        z = z_ref[place, :]
        return z * sigmoid(z)

    write_strips(border_of(outer_y), pool2.at[REACH])
    for offset in OFFSETS:
        ring2.start(offset)

    def activate(c):
        z = z_ref[chunk_rows(c), :]
        s = sigmoid(z)
        y = z * s
        d_ref[chunk_rows(c), :] = s * (1.0 + z * (1.0 - s))
        store_slabs(c, y, x2)

    chunks(activate)
    finish_outer_rows(x1, rows1, outer, near_outer)

    convolve(x2, big2, z_ref, 2)
    place_rims(collect(ring2, pool2, select), x2, rows2)
    beside2 = strips_beside(rows2)
    add_rims(x2, beside2, big2, z_ref, 2)

    def second_gradient(place):
        z = z_ref[place, :]
        s = sigmoid(z)
        g = act_ref[place, :] * s * (1.0 + z * (1.0 - s))
        return g.astype(BF16).astype(F32)

    border2 = border_of(second_gradient)
    rims = leaving_rims(border2, leave, big2t, 2)
    own = send_back(ring3, out2, rims, lambda k, x: dot(select_turned[k], x))

    def second(c):
        z = z_ref[chunk_rows(c), :]
        s = sigmoid(z)
        z_ref[chunk_rows(c), :] = z * s * 0.25
        g = (act_ref[chunk_rows(c), :] * s * (1.0 + z * (1.0 - s))).astype(BF16).astype(F32)
        store_slabs(c, g, g_ref)
        store_shifts(c, g, 2, shifted)

    chunks(second)
    inner_products(x2, shifted, raw)
    strip_products(beside2, border2, raw)
    pack_taps(raw, flat, 2)
    for t in range(PAIRS // 2):
        sums = []
        for jp in (2 * t, 2 * t + 1):
            v = z_ref[pl.ds(SIDE * jp, PAIRS, stride=2), :] + z_ref[pl.ds(SIDE * jp + 1, PAIRS, stride=2), :]
            sums.append(v + half_turn(v))
        pooled_ref[:, 128 * t : 128 * t + 128] = jnp.where(low, sums[0], sums[1]).astype(BF16)
    transposed(g_ref, big2t, z_ref, 2)

    def inside(c):
        g = without_outer_rows(z_ref[chunk_rows(c), :] * d_ref[chunk_rows(c), :])
        store_shifts(c, g, 1, shifted)

    chunks(inside)
    shifted[0:SIDE] = jnp.zeros((SIDE, 384), BF16)
    shifted[ROWS - SIDE : ROWS] = jnp.zeros((SIDE, 384), BF16)
    inner_products(x1, shifted, raw)
    sum2.scatter(flat)
    add_returned(take_back(ring3, back2, own), z_ref, 2)

    def first_gradient(place):
        return (z_ref[place, :] * d_ref[place, :]).astype(BF16).astype(F32)

    border1 = border_of(first_gradient)
    border_products(x1, near_outer, border1, raw)
    pack_taps(raw, flat, 1)
    sum1.scatter(flat)
    rims = exchange_halves(leaving_rims(border1, leave, big1t, 1), turn_ref)

    def first(c):
        store_slabs(c, z_ref[chunk_rows(c), :] * d_ref[chunk_rows(c), :], g_ref)

    chunks(first)
    transposed(g_ref, big1t, z_ref, 1)
    sum2.across()
    sum1.across()
    own = send_back(ring4, out1, rims, lambda k, x: dot_rows(thin[k], x))
    sum2.gather()
    sum1.gather()
    add_thin_returned(take_back(ring4, back1, own), z_ref)
    for jp in range(PAIRS):
        gin_ref[:, 128 * jp : 128 * jp + 128] = z_ref[SIDE * jp : SIDE * jp + SIDE, :].astype(BF16)
    sum2.gathered()
    for ring in (ring1, ring2, ring3, ring4):
        ring.finish()
    write_taps(total2, flat, dw2_ref)
    sum1.gathered()
    write_taps(total1, flat, dw1_ref)


def finish_kernel(*refs):
    copies = [pltpu.make_async_copy(refs[n], refs[4 + n], refs[8].at[n]) for n in range(4)]
    for copy in copies:
        copy.start()
    for copy in copies:
        copy.wait()


def local(features, weights_first, weights_second, cotangent, neighbours, turns, corners):
    devices = lax.axis_size("tiles")
    anywhere = pl.BlockSpec(memory_space=pl.ANY)
    inputs = (features[0], weights_first, weights_second, cotangent[0], neighbours, turns, corners)
    inputs = tuple(pltpu.with_memory_space_constraint(x, pltpu.HBM) for x in inputs)
    outputs = (
        jax.ShapeDtypeStruct((PAIRS, PAIRS * CHANS), BF16),
        jax.ShapeDtypeStruct((SIDE, SIDE * CHANS), BF16),
        jax.ShapeDtypeStruct((9, CHANS, CHANS), F32),
        jax.ShapeDtypeStruct((9, CHANS, CHANS), F32),
    )
    slabs = pltpu.VMEM((PAIRS + 2, SIDE, 128), BF16)
    field = pltpu.VMEM((ROWS, 128), F32)
    big = pltpu.VMEM((384, 384), BF16)
    pool = pltpu.VMEM((SLOTS, STRIP, 128), BF16)
    thin_pool = pltpu.VMEM((SLOTS, 128, 128), BF16)
    rows = pltpu.VMEM((4, 48, 128), F32)

    def shares(count):
        return pltpu.VMEM((count, SHARE, 128), F32)

    reduction = [shares(n) for n in (PLANE, PLANE, LEVELS, PLANE)]
    results = pl.pallas_call(
        functools.partial(level_kernel, devices),
        out_shape=tuple(pltpu.VMEM(x.shape, x.dtype) for x in outputs),
        in_specs=[pl.BlockSpec(memory_space=pltpu.HBM)] * 7,
        out_specs=[pl.BlockSpec(memory_space=pltpu.VMEM)] * 4,
        scratch_shapes=[pltpu.VMEM(x.shape, x.dtype) for x in inputs[:4]]
        + [pltpu.SMEM(x.shape, x.dtype) for x in inputs[4:]]
        + [
            slabs, slabs, slabs,
            pltpu.VMEM((ROWS, 384), BF16),
            field, field, field,
            pltpu.VMEM((2, 8 * PAIRS, 128), F32),
            rows, rows, rows,
            pltpu.VMEM((8, 48, 128), F32),
            pltpu.VMEM((8, PAIRS, 384), BF16),
            pltpu.VMEM((3, 128, 384), F32),
            pltpu.VMEM((2 * PLANE * SHARE, 128), F32),
            big, big, big, big,
            pltpu.VMEM((SLOTS, RIMS, STRIP), BF16),
            pltpu.VMEM((SLOTS, STRIP, RIMS), BF16),
            pltpu.VMEM((SLOTS, RIMS, 128), BF16),
            thin_pool, pool, pool, pool, thin_pool, thin_pool,
        ]
        + reduction
        + reduction
        + [
            pltpu.SemaphoreType.DMA((7,)),
            pltpu.SemaphoreType.DMA((8, SLOTS)),
            pltpu.SemaphoreType.DMA((6, PLANE)),
            pltpu.SemaphoreType.DMA((6, PLANE)),
        ],
        compiler_params=pltpu.CompilerParams(
            collective_id=0, has_side_effects=True, vmem_limit_bytes=48 * 2**20
        ),
        name="level",
    )(*inputs)
    pooled, grad, first, second = pl.pallas_call(
        finish_kernel,
        out_shape=outputs,
        in_specs=[anywhere] * 4,
        out_specs=[anywhere] * 4,
        scratch_shapes=[pltpu.SemaphoreType.DMA((4,))],
        compiler_params=pltpu.CompilerParams(vmem_limit_bytes=4 * 2**20),
        name="finish",
    )(*results)
    return pooled[None], grad[None], first, second


def solution(mesh):
    return jax.shard_map(
        local,
        mesh=mesh,
        in_specs=(
            P("tiles", None, None),
            P(),
            P(),
            P("tiles", None, None),
            P("tiles", None),
            P("tiles", None),
            P("tiles", None),
        ),
        out_specs=(P("tiles", None, None), P("tiles", None, None), P(), P()),
        check_vma=False,
    )
```
